32 devices in a mesh: chan: 8 (over y, x, core), win: 4 (over z).
Axes of the slice: x: 2, y: 2, z: 4, core: 2. Of those that a mesh axis runs over, the one named last changes fastest.
Arguments:
- traces: bfloat16 [64, 512, 512], P('win', 'chan'), may hold values from -80 to 80
- valid: int32 [64, 512], P('win', 'chan'), may hold values 0 or 1
- reach: int32 [512], P('chan'), may hold values from 1 to 256
Outputs:
- stack: float32 [256, 512, 256], P('win', 'chan')
The draws below stay inside these ranges and needn't reach their ends.
All inputs are finite; a program needn't handle non-finite values. No bound on the sum of `valid` on one device may be relied on, other than what follows from the above.
Results may differ from the reference program's by a relative error of at most 0.0045.
Values may be sent and summed in bfloat16 or wider, within the bound.
No kernel may reach another device: no remote copies, remote signals or barrier semaphores. Data moves between devices by JAX's collectives and lax.ppermute only.
A program may use at most 128 MiB of HBM per device.

```python
import math
import jax
import jax.numpy as jnp
from jax import lax

S = 512
F = 128
FIRST = 16
BAND = 256
CHANNELS = 512
WINDOWS = 64


def draw_traces(key, part):
    key_noise = jax.random.fold_in(key, 11)
    key_scale = jax.random.fold_in(key, 12)
    noise = jnp.clip(jax.random.normal(key_noise, (WINDOWS, CHANNELS, S), jnp.float32), -6.0, 6.0)
    scales = jnp.exp(jax.random.uniform(key_scale, (WINDOWS, CHANNELS, 1), jnp.float32, 0.0, jnp.log(10.0)))
    return (noise * scales).astype(jnp.bfloat16)


def set_ends(result, rng, low, top_value):
    longest = result.shape.index(max(result.shape))
    spots = []
    for shift in (0, 1):
        where = [jax.random.randint(jax.random.fold_in(rng, axis), (), 0, length) for axis, length in enumerate(result.shape)]
        where[longest] = (where[longest] + shift) % result.shape[longest]
        spots.append(tuple(where))
    return result.at[spots[0]].set(low).at[spots[1]].set(top_value)


def setup_inputs(seed: int = 0) -> dict:
    splits = jax.random.split(jax.random.key(seed), 4)
    return {
        "traces": draw_traces(jax.random.fold_in(splits[3], 71), 0),
        "valid": set_ends((jax.random.randint(splits[1], (WINDOWS, CHANNELS), 0, 8) < 7).astype(jnp.int32), jax.random.fold_in(splits[1], 1), 0, 1),
        "reach": set_ends(jax.random.randint(splits[2], (CHANNELS,), 1, BAND + 1), jax.random.fold_in(splits[2], 1), 1, BAND).astype(jnp.int32),
    }


def make_table():
    t_int = jnp.arange(S, dtype=jnp.int32)
    j_int = jnp.arange(F, dtype=jnp.int32) + FIRST
    phase = t_int[:, None] * j_int[None, :] % S
    angle = 2.0 * math.pi / S * phase.astype(jnp.float32)
    hann = 0.5 - 0.5 * jnp.cos(2.0 * math.pi / S * t_int.astype(jnp.float32))
    return jnp.concatenate([hann[:, None] * jnp.cos(angle), -hann[:, None] * jnp.sin(angle)], axis=1).astype(jnp.bfloat16)

def whiten(spectra, valid):
    real_part = spectra[..., :F]
    imag_part = spectra[..., F:]
    amplitude = jnp.sqrt(real_part * real_part + imag_part * imag_part)
    level = jnp.sqrt(lax.optimization_barrier(jnp.mean(amplitude * amplitude, axis=-1, keepdims=True)) + 1e-06)
    factor = valid.astype(jnp.float32)[..., None] / (amplitude + 0.1 * level)
    return jnp.concatenate([real_part * factor, imag_part * factor], axis=-1).astype(jnp.bfloat16)

def reference(traces, valid, reach):
    table = make_table()
    spectra = jnp.einsum('wct,tj->wcj', traces, table, preferred_element_type=jnp.float32)
    whitened = whiten(spectra, valid).astype(jnp.float32)
    scale = 1.0 / math.sqrt(WINDOWS)
    a_re = whitened[..., :F]
    a_im = whitened[..., F:]

    def one_offset(offset):
        rolled = jnp.roll(whitened, -offset, axis=1)
        b_re = rolled[..., :F]
        b_im = rolled[..., F:]
        real_sum = lax.optimization_barrier(jnp.sum(a_re * b_re + a_im * b_im, axis=0))
        imag_sum = lax.optimization_barrier(jnp.sum(a_im * b_re - a_re * b_im, axis=0))
        inside = (offset < reach).astype(jnp.float32)
        return jnp.concatenate([real_sum, imag_sum], axis=-1) * inside[:, None] * scale
    return lax.map(one_offset, jnp.arange(BAND, dtype=jnp.int32))
```

```python
import functools
import math

import jax
import jax.numpy as jnp
import numpy as np
from jax import lax
from jax.experimental import pallas as pl
from jax.experimental.pallas import tpu as pltpu
from jax.sharding import PartitionSpec as P

F = 128
FIRST = 16
BAND = 256
AXES = ("chan", "win")
VMEM_LIMIT = 48 * 1024 * 1024
FREQUENCY_STEPS = 4
CHANNEL_BLOCK = 8


def make_table(samples):
    t_int = np.arange(samples, dtype=np.int64)
    j_int = np.arange(F, dtype=np.int64) + FIRST
    angle = 2.0 * np.pi / samples * (j_int[:, None] * t_int[None, :] % samples)
    hann = 0.5 - 0.5 * np.cos(2.0 * np.pi / samples * t_int)
    rows = np.concatenate([hann * np.cos(angle), -hann * np.sin(angle)], axis=0)
    return jnp.asarray(rows.astype(np.float32)).astype(jnp.bfloat16)


def whiten_kernel(table_ref, traces_ref, valid_ref, out_ref, rows):
    windows, width, samples = traces_ref.shape
    for g in range(windows // 2):
        block = traces_ref[2 * g : 2 * g + 2].reshape(2 * width, samples)
        spectra = lax.dot_general(
            table_ref[...], block, (((1,), (1,)), ((), ())), preferred_element_type=jnp.float32
        )
        re, im = spectra[:F], spectra[F:]
        power = re * re + im * im
        level = jnp.sqrt(jnp.mean(power, axis=0, keepdims=True) + 1e-06)
        usable = jnp.concatenate(
            [valid_ref[2 * g : 2 * g + 1, :], valid_ref[2 * g + 1 : 2 * g + 2, :]], axis=1
        ).astype(jnp.float32)
        factor = usable / (jnp.sqrt(power) + 0.1 * level)
        re, im = re * factor, im * factor
        for k in range(2):
            half = slice(k * width, (k + 1) * width)
            rows[pl.ds(2 * g + k, F, stride=windows), :] = jnp.concatenate(
                [re[:, half], im[:, half]], axis=1
            )
    out_ref[...] = rows[...].reshape(out_ref.shape).astype(jnp.bfloat16)


def whitened_chunk(traces, valid):
    windows, width, samples = traces.shape
    return pl.pallas_call(
        whiten_kernel,
        out_shape=jax.ShapeDtypeStruct((F, windows, 2 * width), jnp.bfloat16),
        in_specs=[pl.BlockSpec(memory_space=pltpu.VMEM)] * 3,
        out_specs=pl.BlockSpec(memory_space=pltpu.VMEM),
        scratch_shapes=[pltpu.VMEM((F * windows, 2 * width), jnp.float32)],
        compiler_params=pltpu.CompilerParams(vmem_limit_bytes=VMEM_LIMIT),
        cost_estimate=pl.CostEstimate(
            flops=4 * F * windows * width * samples, bytes_accessed=2 * traces.size, transcendentals=0
        ),
        name="whiten",
    )(make_table(samples), traces, valid)


def stack_kernel(slots, f_steps, scale, place_ref, reach_ref, *refs):
    own_refs, first_refs, second_refs = refs[:slots], refs[slots : 2 * slots], refs[2 * slots : 3 * slots]
    out_ref, products = refs[3 * slots], refs[3 * slots + 1]
    step = pl.program_id(0)
    f_block, _, lanes = own_refs[0].shape
    width = lanes // 2
    offsets, i_block, _ = out_ref.shape

    @pl.when(step < f_steps)
    def _():
        def one_bin(f, carry):
            a = jnp.concatenate([r[f] for r in own_refs], axis=0)
            at = a.T
            left = jnp.concatenate([at[:width], at[width:]], axis=1)
            tops, bottoms = [], []
            for group in (first_refs, second_refs):
                b = jnp.concatenate([r[f] for r in group], axis=0)
                tops.append(b)
                bottoms.append(jnp.concatenate([b[:, width:], -b[:, :width]], axis=1))
            right = jnp.concatenate(
                [jnp.concatenate(tops, axis=1), jnp.concatenate(bottoms, axis=1)], axis=0
            )
            row = (step * f_block + f) * width
            both = jnp.dot(left, right, preferred_element_type=jnp.float32)
            for half in range(2):
                products[half, pl.ds(pl.multiple_of(row, width), width), :] = both[
                    :, half * lanes : (half + 1) * lanes
                ]
            return carry

        lax.fori_loop(0, f_block, one_bin, 0, unroll=4)

    @pl.when(step >= f_steps)
    def _():
        lane = lax.broadcasted_iota(jnp.int32, (offsets, 2 * lanes), 1)
        k = lax.broadcasted_iota(jnp.int32, (offsets, 2 * lanes), 0)
        partner = lane % width + jnp.where(lane >= lanes, width, 0)
        is_real = lane % lanes < width
        far = 4 * lanes
        shift_re = jnp.where(is_real, partner - k, far)
        shift_im = jnp.where(is_real, far, partner - k)
        first_k = place_ref[0]
        base = (step - f_steps) * i_block
        row_k = lax.broadcasted_iota(jnp.int32, (offsets, F), 0) + first_k
        for il in range(i_block):
            i = base + il
            at = i + place_ref[1]
            pick = jnp.concatenate(
                [
                    jnp.where(shift_re == at, 1.0, 0.0),
                    jnp.where(shift_im == at, -1.0, 0.0),
                ],
                axis=0,
            ).astype(jnp.bfloat16)
            x = jnp.concatenate(
                [products[half, pl.ds(i, F, stride=width), :] for half in range(2)], axis=1
            ).astype(jnp.bfloat16)
            y = lax.dot_general(
                pick, x, (((1,), (1,)), ((), ())), preferred_element_type=jnp.float32
            )
            inside = jnp.where(row_k < reach_ref[i], scale, 0.0)
            out_ref[:, il, 0:F] = y[:offsets] * inside
            out_ref[:, il, F : 2 * F] = y[offsets:] * inside


def stacked(own, first, second, place, reach, offsets, windows):
    slots = len(own)
    bins, chunk_windows, lanes = own[0].shape
    width = lanes // 2
    f_steps, i_steps = FREQUENCY_STEPS, width // CHANNEL_BLOCK
    chunk_spec = pl.BlockSpec(
        (bins // f_steps, chunk_windows, lanes), lambda s, *_: (jnp.minimum(s, f_steps - 1), 0, 0)
    )
    return pl.pallas_call(
        functools.partial(stack_kernel, slots, f_steps, 1.0 / math.sqrt(windows)),
        out_shape=jax.ShapeDtypeStruct((offsets, width, 2 * F), jnp.float32),
        grid_spec=pltpu.PrefetchScalarGridSpec(
            num_scalar_prefetch=2,
            grid=(f_steps + i_steps,),
            in_specs=[chunk_spec] * (3 * slots),
            out_specs=pl.BlockSpec(
                (offsets, CHANNEL_BLOCK, 2 * F), lambda s, *_: (0, jnp.maximum(s - f_steps, 0), 0)
            ),
            scratch_shapes=[pltpu.VMEM((2, bins * width, lanes), jnp.float32)],
        ),
        compiler_params=pltpu.CompilerParams(vmem_limit_bytes=VMEM_LIMIT),
        cost_estimate=pl.CostEstimate(
            flops=16 * bins * width * width * windows,
            bytes_accessed=8 * offsets * width * F + 6 * slots * own[0].size,
            transcendentals=0,
        ),
        name="stack",
    )(place, reach, *own, *first, *second)


def send(array, pairs):
    return lax.ppermute(array, AXES, pairs)


def pairs_of(n_win, n_chan, target):
    pairs = []
    for z in range(n_win):
        for c in range(n_chan):
            to = target(z, c)
            if to is not None:
                pairs.append((c * n_win + z, to * n_win + z))
    return pairs


def partners_direct(piece, hops, n_win, n_chan):
    first = send(piece, pairs_of(n_win, n_chan, lambda z, c: (c - hops[z]) % n_chan))
    second = send(piece, pairs_of(n_win, n_chan, lambda z, c: (c - hops[z] - 1) % n_chan))
    return first, second


def partners_square(piece, n_win, n_chan):
    z, c = lax.axis_index("win"), lax.axis_index("chan")
    core, x = c % 2, c // 2 % 2
    along_y = pairs_of(n_win, n_chan, lambda z, c: c ^ 4 if z == 3 or c % 2 == 0 else None)

    def x_target(z, c):
        core, x = c % 2, c // 2 % 2
        if z == 0:
            return c ^ 2 if x == 1 and core == 0 else None
        if z == 3:
            return c ^ 2 if x == 1 and core == 1 else None
        return c ^ 2 if x == 1 or core == 1 else None

    def onward_target(z, c):
        core, x = c % 2, c // 2 % 2
        if z == 0:
            return c ^ 2 if x == 0 and core == 0 else None
        if z == 3:
            return c ^ 2 if x == 0 and core == 1 else None
        if core == 0:
            return c ^ 2 if x == 0 else None
        return c ^ 4 if x == 1 else None

    from_y = send(piece, along_y)
    from_x = send(piece, pairs_of(n_win, n_chan, x_target))
    relay = jnp.where((core == 0) | (z == 3), from_y, from_x)
    onward = send(relay, pairs_of(n_win, n_chan, onward_target))
    next_chip = jnp.where(x == 0, from_x, onward)
    for_core = jnp.where(
        core == 0, jnp.where(z < 2, next_chip, from_y), jnp.where(z < 2, piece, next_chip)
    )
    swapped = send(for_core, pairs_of(n_win, n_chan, lambda z, c: c ^ 1))
    first = jnp.where(z == 0, piece, jnp.where(z == 2, next_chip, swapped))
    second = jnp.where(z == 1, next_chip, jnp.where(z == 3, from_y, swapped))
    return first, second


def on_device(traces, valid, reach):
    width = traces.shape[1]
    n_win, n_chan = lax.axis_size("win"), lax.axis_size("chan")
    windows = traces.shape[0] * n_win
    offsets = BAND // n_win
    hops = [z * offsets // width for z in range(n_win)]
    first_offset = lax.axis_index("win") * offsets
    place = jnp.stack([first_offset, first_offset % width]).astype(jnp.int32)
    piece = whitened_chunk(traces, valid)
    own, first, second = [], [], []
    for slot in range(n_win):
        if slot:
            piece = lax.ppermute(piece, "win", [(z, (z + 1) % n_win) for z in range(n_win)])
        if n_chan == 8 and hops == list(range(4)):
            b1, b2 = partners_square(piece, n_win, n_chan)
        else:
            b1, b2 = partners_direct(piece, hops, n_win, n_chan)
        own.append(piece)
        first.append(b1)
        second.append(b2)
    return stacked(own, first, second, place, reach, offsets, windows)


def solution(mesh):
    in_specs = (P("win", "chan", None), P("win", "chan"), P("chan"))
    out_specs = P("win", "chan", None)
    return jax.shard_map(
        on_device, mesh=mesh, in_specs=in_specs, out_specs=out_specs, check_vma=False
    )
```

```python
import functools
import math

import jax
import jax.numpy as jnp
import numpy as np
from jax import lax
from jax.experimental import pallas as pl
from jax.experimental.pallas import tpu as pltpu
from jax.sharding import PartitionSpec as P

F = 128
FIRST = 16
BAND = 256
AXES = ("chan", "win")
VMEM_LIMIT = 48 * 1024 * 1024
FREQUENCY_STEPS = 4
CHANNEL_BLOCK = 8
WHITEN_WINDOWS = 4


def make_table(samples):
    t_int = np.arange(samples, dtype=np.int64)
    j_int = np.arange(F, dtype=np.int64) + FIRST
    angle = 2.0 * np.pi / samples * (j_int[:, None] * t_int[None, :] % samples)
    hann = 0.5 - 0.5 * np.cos(2.0 * np.pi / samples * t_int)
    rows = np.concatenate([hann * np.cos(angle), -hann * np.sin(angle)], axis=0)
    return jnp.asarray(rows.astype(np.float32)).astype(jnp.bfloat16)


def whiten_kernel(table_ref, traces_ref, valid_ref, out_ref, rows):
    step, steps = pl.program_id(0), pl.num_programs(0)
    block_windows, width, samples = traces_ref.shape
    windows = out_ref.shape[1]
    for g in range(block_windows // 2):
        block = traces_ref[2 * g : 2 * g + 2].reshape(2 * width, samples)
        spectra = lax.dot_general(
            table_ref[...], block, (((1,), (1,)), ((), ())), preferred_element_type=jnp.float32
        )
        re, im = spectra[:F], spectra[F:]
        power = re * re + im * im
        level = jnp.sqrt(jnp.mean(power, axis=0, keepdims=True) + 1e-06)
        w = step * block_windows + 2 * g
        usable = jnp.concatenate(
            [valid_ref[pl.ds(w, 1), :], valid_ref[pl.ds(w + 1, 1), :]], axis=1
        ).astype(jnp.float32)
        factor = usable / (jnp.sqrt(power) + 0.1 * level)
        re, im = re * factor, im * factor
        for k in range(2):
            half = slice(k * width, (k + 1) * width)
            rows[pl.ds(w + k, F, stride=windows), :] = jnp.concatenate(
                [re[:, half], im[:, half]], axis=1
            )

    @pl.when(step == steps - 1)
    def _():
        out_ref[...] = rows[...].reshape(out_ref.shape).astype(jnp.bfloat16)


def whitened_chunk(traces, valid):
    windows, width, samples = traces.shape
    block = math.gcd(windows, WHITEN_WINDOWS)
    return pl.pallas_call(
        whiten_kernel,
        out_shape=jax.ShapeDtypeStruct((F, windows, 2 * width), jnp.bfloat16),
        grid=(windows // block,),
        in_specs=[
            pl.BlockSpec((2 * F, samples), lambda s: (0, 0)),
            pl.BlockSpec((block, width, samples), lambda s: (s, 0, 0)),
            pl.BlockSpec((windows, width), lambda s: (0, 0)),
        ],
        out_specs=pl.BlockSpec((F, windows, 2 * width), lambda s: (0, 0, 0)),
        scratch_shapes=[pltpu.VMEM((F * windows, 2 * width), jnp.float32)],
        compiler_params=pltpu.CompilerParams(vmem_limit_bytes=VMEM_LIMIT),
        cost_estimate=pl.CostEstimate(
            flops=4 * F * windows * width * samples, bytes_accessed=2 * traces.size, transcendentals=0
        ),
        name="whiten",
    )(make_table(samples), traces, valid)


def stack_kernel(counts, f_steps, scale, has_partial, place_ref, reach_ref, *refs):
    slots = len(counts)
    refs = list(refs)
    groups = [[refs.pop(0) for _ in range(count)] for count in counts]
    partial_ref = refs.pop(0) if has_partial else None
    out_ref, products, chosen, diagonals = refs
    step = pl.program_id(0)
    f_block, chunk_windows, lanes = groups[0][0].shape
    width = lanes // 2
    pitch = products.shape[1] // (f_block * f_steps)
    offsets, i_block, _ = out_ref.shape

    @pl.when(step < f_steps)
    def _():
        for slot, group in enumerate(groups):
            rows = slice(slot * chunk_windows, (slot + 1) * chunk_windows)
            for which in range(2):
                code = place_ref[2 + 2 * slot + which]
                for index, ref in enumerate(group):

                    @pl.when(code == index)
                    def _(ref=ref, which=which, rows=rows):
                        chosen[which, :, rows, :] = ref[...]

        def one_bin(f, carry):
            at = jnp.concatenate([group[0][f] for group in groups], axis=0).T
            left = jnp.concatenate([at[:width], at[width:]], axis=1)
            tops = [chosen[which, f] for which in range(2)]
            bottoms = [jnp.concatenate([b[:, width:], -b[:, :width]], axis=1) for b in tops]
            right = jnp.concatenate(
                [jnp.concatenate(tops, axis=1), jnp.concatenate(bottoms, axis=1)], axis=0
            )
            row = (step * f_block + f) * pitch
            both = jnp.dot(left, right, preferred_element_type=jnp.float32)
            for half in range(2):
                products[half, pl.ds(pl.multiple_of(row, 8), width), :] = both[
                    :, half * lanes : (half + 1) * lanes
                ]
            return carry

        lax.fori_loop(0, f_block, one_bin, 0, unroll=4)

    @pl.when(step >= f_steps)
    def _():
        lane = lax.broadcasted_iota(jnp.int32, (offsets, 2 * lanes), 1)
        k = lax.broadcasted_iota(jnp.int32, (offsets, 2 * lanes), 0)
        partner = lane % width + jnp.where(lane >= lanes, width, 0)
        is_real = lane % lanes < width
        far = 4 * lanes
        shift_re = jnp.where(is_real, partner - k, far)
        shift_im = jnp.where(is_real, far, partner - k)
        base = (step - f_steps) * i_block
        row_k = lax.broadcasted_iota(jnp.int32, (offsets, F), 0) + place_ref[0]
        for il in range(i_block):
            i = base + il
            at = i + place_ref[1]
            pick = jnp.concatenate(
                [
                    jnp.where(shift_re == at, 1.0, 0.0),
                    jnp.where(shift_im == at, -1.0, 0.0),
                ],
                axis=0,
            ).astype(jnp.bfloat16)
            x = jnp.concatenate(
                [products[half, pl.ds(i, F, stride=pitch), :] for half in range(2)], axis=1
            ).astype(jnp.bfloat16)
            y = lax.dot_general(
                pick, x, (((1,), (1,)), ((), ())), preferred_element_type=jnp.float32
            )
            inside = jnp.where(row_k < reach_ref[i], scale, 0.0)
            for part in range(2):
                diagonals[part, pl.ds(il, offsets, stride=i_block), :] = (
                    y[part * offsets : (part + 1) * offsets] * inside
                )
        for part in range(2):
            columns = slice(part * F, (part + 1) * F)
            value = diagonals[part].reshape(offsets, i_block, F)
            if has_partial:
                value = value + partial_ref[:, :, columns]
            out_ref[:, :, columns] = value


def stacked(slot_buffers, slot_codes, place, reach, offsets, windows, partial):
    slots = len(slot_buffers)
    bins, chunk_windows, lanes = slot_buffers[0][0].shape
    width = lanes // 2
    f_steps, i_steps = FREQUENCY_STEPS, width // CHANNEL_BLOCK
    codes = [code for pair in slot_codes for code in pair]
    place = jnp.stack([jnp.asarray(v, jnp.int32) for v in place + codes])

    def chunk_spec(slot, index):
        def block(s, place_ref, reach_ref):
            f = jnp.minimum(s, f_steps - 1)
            if index == 0:
                return f, 0, 0
            used = (place_ref[2 + 2 * slot] == index) | (place_ref[3 + 2 * slot] == index)
            return jnp.where(used, f, 0), 0, 0

        return pl.BlockSpec((bins // f_steps, chunk_windows, lanes), block)

    out_spec = pl.BlockSpec(
        (offsets, CHANNEL_BLOCK, 2 * F), lambda s, *_: (0, jnp.maximum(s - f_steps, 0), 0)
    )
    in_specs = [chunk_spec(s, n) for s in range(slots) for n in range(len(slot_buffers[s]))]
    operands = [buffer for buffers in slot_buffers for buffer in buffers]
    if partial is not None:
        in_specs.append(out_spec)
        operands.append(partial)
    counts = tuple(len(buffers) for buffers in slot_buffers)
    return pl.pallas_call(
        functools.partial(
            stack_kernel, counts, f_steps, 1.0 / math.sqrt(windows), partial is not None
        ),
        out_shape=jax.ShapeDtypeStruct((offsets, width, 2 * F), jnp.float32),
        grid_spec=pltpu.PrefetchScalarGridSpec(
            num_scalar_prefetch=2,
            grid=(f_steps + i_steps,),
            in_specs=in_specs,
            out_specs=out_spec,
            scratch_shapes=[
                pltpu.VMEM((2, bins * (width + 8), lanes), jnp.float32),
                pltpu.VMEM((2, bins // f_steps, slots * chunk_windows, lanes), jnp.bfloat16),
                pltpu.VMEM((2, offsets * CHANNEL_BLOCK, F), jnp.float32),
            ],
        ),
        compiler_params=pltpu.CompilerParams(vmem_limit_bytes=VMEM_LIMIT),
        cost_estimate=pl.CostEstimate(
            flops=16 * bins * width * width * windows,
            bytes_accessed=30_000_000,
            transcendentals=0,
        ),
        name="stack",
    )(place, reach, *operands)


def send(array, pairs):
    return lax.ppermute(array, AXES, pairs)


def pairs_of(n_win, n_chan, target):
    pairs = []
    for z in range(n_win):
        for c in range(n_chan):
            to = target(z, c)
            if to is not None:
                pairs.append((c * n_win + z, to * n_win + z))
    return pairs


def partners_direct(piece, hops, n_win, n_chan):
    first = send(piece, pairs_of(n_win, n_chan, lambda z, c: (c - hops[z]) % n_chan))
    second = send(piece, pairs_of(n_win, n_chan, lambda z, c: (c - hops[z] - 1) % n_chan))
    return (piece, first, second), (1, 2)


def crosses(z, core):
    return core == 0 if z == 0 else core == 1 if z == 3 else True


def partners_square(piece, n_win, n_chan, last):
    z, c = lax.axis_index("win"), lax.axis_index("chan")
    core, x = c % 2, c // 2 % 2

    def pairs(target):
        return pairs_of(n_win, n_chan, lambda z, c: target(z, c, c % 2, c // 2 % 2))

    def swap(next_chip, from_y):
        outgoing = jnp.where(
            core == 0, jnp.where(z < 2, next_chip, from_y), jnp.where(z < 2, piece, next_chip)
        )
        return send(outgoing, pairs(lambda z, c, core, x: c ^ 1))

    def codes(next_code, y_code, swap_code):
        first = jnp.where(z == 0, 0, jnp.where(z == 2, next_code, swap_code))
        second = jnp.where(z == 1, next_code, jnp.where(z == 3, y_code, swap_code))
        return first, second

    if not last:

        def y_target(z, c, core, x):
            needed = z == 3 or (z == 2 and core == 0) or (x == 0 and crosses(z, core))
            return c ^ 4 if needed else None

        from_y = send(piece, pairs(y_target))
        next_chip = send(
            jnp.where(x == 1, piece, from_y),
            pairs(lambda z, c, core, x: c ^ 2 if crosses(z, core) else None),
        )
        swapped = swap(next_chip, from_y)
        return (piece, next_chip, from_y, swapped), codes(1, 2, 3)

    def early_target(z, c, core, x):
        return c ^ 4 if (core == 1 if z == 3 else x == 0 and core == 0) else None

    def x_target(z, c, core, x):
        needed = crosses(z, core) if x == 1 else z in (1, 2) and core == 1
        return c ^ 2 if needed else None

    def onward_target(z, c, core, x):
        if x == 0:
            return c ^ 2 if crosses(z, core) and (z == 3 or core == 0) else None
        return c ^ 4 if z in (1, 2) and core == 1 else None

    def late_target(z, c, core, x):
        return c ^ 4 if core == 0 and (z == 3 or (z == 2 and x == 1)) else None

    early = send(piece, pairs(early_target))
    from_x = send(piece, pairs(x_target))
    relay = jnp.where((core == 0) | (z == 3), early, from_x)
    onward = send(relay, pairs(onward_target))
    piece_then, _ = lax.optimization_barrier((piece, early))
    late = send(piece_then, pairs(late_target))
    is_early = ((z == 3) & (core == 1)) | ((z == 2) & (x == 0))
    swapped = swap(jnp.where(x == 0, from_x, onward), jnp.where(is_early, early, late))
    return (
        (piece, from_x, onward, early, late, swapped),
        codes(jnp.where(x == 0, 1, 2), jnp.where(is_early, 3, 4), 5),
    )


def on_device(traces, valid, reach):
    width = traces.shape[1]
    n_win, n_chan = lax.axis_size("win"), lax.axis_size("chan")
    windows = traces.shape[0] * n_win
    offsets = BAND // n_win
    hops = [z * offsets // width for z in range(n_win)]
    first_offset = lax.axis_index("win") * offsets
    place = [first_offset, first_offset % width]
    piece = whitened_chunk(traces, valid)
    buffers, codes = [], []
    partial = None
    for slot in range(n_win):
        if slot:
            piece = lax.ppermute(piece, "win", [(z, (z + 1) % n_win) for z in range(n_win)])
        if n_chan == 8 and hops == list(range(4)):
            found, code = partners_square(piece, n_win, n_chan, slot == n_win - 1)
        else:
            found, code = partners_direct(piece, hops, n_win, n_chan)
        buffers.append(found)
        codes.append(code)
        if slot in (n_win // 2 - 1, n_win - 1):
            partial = stacked(buffers, codes, place, reach, offsets, windows, partial)
            buffers, codes = [], []
    return partial


def solution(mesh):
    in_specs = (P("win", "chan", None), P("win", "chan"), P("chan"))
    out_specs = P("win", "chan", None)
    return jax.shard_map(
        on_device, mesh=mesh, in_specs=in_specs, out_specs=out_specs, check_vma=False
    )
```

```python
import functools
import math

import jax
import jax.numpy as jnp
import numpy as np
from jax import lax
from jax.experimental import pallas as pl
from jax.experimental.pallas import tpu as pltpu
from jax.sharding import PartitionSpec as P

F = 128
FIRST = 16
BAND = 256
AXES = ("chan", "win")
CHANNEL_BLOCK = 8
WHITEN_BLOCKS = 4
PITCH_PAD = 8
MIB = 1024 * 1024
VMEM = pl.BlockSpec(memory_space=pltpu.VMEM)
SMEM = pl.BlockSpec(memory_space=pltpu.SMEM)
SMALL = pl.CostEstimate(flops=1, bytes_accessed=1, transcendentals=0)
ANY = pl.BlockSpec(memory_space=pl.ANY)


def make_table(samples):
    t_int = np.arange(samples, dtype=np.int64)
    j_int = np.arange(F, dtype=np.int64) + FIRST
    angle = 2.0 * np.pi / samples * (j_int[:, None] * t_int[None, :] % samples)
    hann = 0.5 - 0.5 * np.cos(2.0 * np.pi / samples * t_int)
    rows = np.concatenate([hann * np.cos(angle), -hann * np.sin(angle)], axis=0)
    return jnp.asarray(rows.astype(np.float32)).astype(jnp.bfloat16)


def whiten_kernel(table_hbm, traces_hbm, valid_hbm, out_ref, table, traces, valid, rows, sems):
    windows, width, samples = traces.shape
    block = windows // WHITEN_BLOCKS if windows % (2 * WHITEN_BLOCKS) == 0 else windows
    copies = [
        pltpu.make_async_copy(table_hbm, table, sems.at[0]),
        pltpu.make_async_copy(valid_hbm, valid, sems.at[1]),
    ]
    for n in range(windows // block):
        part = pl.ds(n * block, block)
        copies.append(
            pltpu.make_async_copy(traces_hbm.at[part], traces.at[part], sems.at[2 + n])
        )
    for copy in copies:
        copy.start()
    copies[0].wait()
    copies[1].wait()
    for w in range(0, windows, 2):
        if w % block == 0:
            copies[2 + w // block].wait()
        spectra = lax.dot_general(
            table[...],
            traces[w : w + 2].reshape(2 * width, samples),
            (((1,), (1,)), ((), ())),
            preferred_element_type=jnp.float32,
        )
        re, im = spectra[:F], spectra[F:]
        power = re * re + im * im
        level = jnp.sqrt(jnp.mean(power, axis=0, keepdims=True) + 1e-06)
        usable = jnp.concatenate([valid[w : w + 1, :], valid[w + 1 : w + 2, :]], axis=1)
        factor = usable.astype(jnp.float32) / (jnp.sqrt(power) + 0.1 * level)
        re, im = re * factor, im * factor
        for k in range(2):
            half = slice(k * width, (k + 1) * width)
            rows[pl.ds(w + k, F, stride=windows), :] = jnp.concatenate(
                [re[:, half], im[:, half]], axis=1
            )
    out_ref[...] = rows[...].reshape(out_ref.shape).astype(jnp.bfloat16)


def whitened_chunk(traces, valid):
    windows, width, samples = traces.shape
    return pl.pallas_call(
        whiten_kernel,
        out_shape=jax.ShapeDtypeStruct((F, windows, 2 * width), jnp.bfloat16),
        in_specs=[ANY] * 3,
        out_specs=VMEM,
        scratch_shapes=[
            pltpu.VMEM((2 * F, samples), jnp.bfloat16),
            pltpu.VMEM(traces.shape, traces.dtype),
            pltpu.VMEM(valid.shape, valid.dtype),
            pltpu.VMEM((F * windows, 2 * width), jnp.float32),
            pltpu.SemaphoreType.DMA((2 + WHITEN_BLOCKS,)),
        ],
        compiler_params=pltpu.CompilerParams(vmem_limit_bytes=62 * MIB),
        cost_estimate=pl.CostEstimate(
            flops=4 * F * traces.size, bytes_accessed=2 * traces.size, transcendentals=0
        ),
        name="whiten",
    )(make_table(samples), traces, valid)


def copy_chosen(code, refs, put):
    for index, ref in enumerate(refs):

        @pl.when(code == index)
        def _(ref=ref):
            put(ref)


def choose_kernel(groups, per_group, codes_ref, *refs):
    out_ref = refs[-1]
    shared = refs[groups * per_group : -1]
    for which in range(out_ref.shape[0]):
        for g in range(groups):

            def put(ref, which=which, g=g):
                out_ref[which, g] = ref[...]

            candidates = list(refs[g * per_group : (g + 1) * per_group])
            candidates += [ref.at[g] for ref in shared]
            copy_chosen(codes_ref[which], candidates, put)


def choose(codes, groups, *shared):
    operands = [buffer for group in groups for buffer in group] + list(shared)
    return pl.pallas_call(
        functools.partial(choose_kernel, len(groups), len(groups[0])),
        out_shape=jax.ShapeDtypeStruct(
            (len(codes), len(groups), *groups[0][0].shape), jnp.bfloat16
        ),
        in_specs=[SMEM] + [VMEM] * len(operands),
        out_specs=VMEM,
        compiler_params=pltpu.CompilerParams(vmem_limit_bytes=4 * MIB),
        cost_estimate=SMALL,
        name="choose",
    )(jnp.stack([jnp.asarray(code, jnp.int32) for code in codes]), *operands)


def own_kernel(*refs):
    out_ref = refs[-1]
    width = out_ref.shape[1]

    def one_bin(f, carry):
        turned = jnp.concatenate([ref[f] for ref in refs[:-1]], axis=0).T
        out_ref[f] = jnp.concatenate([turned[:width], turned[width:]], axis=1)
        return carry

    lax.fori_loop(0, out_ref.shape[0], one_bin, 0, unroll=8)


def own_rows(pieces):
    bins, windows, lanes = pieces[0].shape
    return pl.pallas_call(
        own_kernel,
        out_shape=jax.ShapeDtypeStruct(
            (bins, lanes // 2, 2 * windows * len(pieces)), jnp.bfloat16
        ),
        in_specs=[VMEM] * len(pieces),
        out_specs=VMEM,
        compiler_params=pltpu.CompilerParams(vmem_limit_bytes=4 * MIB),
        cost_estimate=SMALL,
        name="own_rows",
    )(*pieces)


def stack_kernel(scale, place_ref, reach_ref, own_ref, early_ref, *refs):
    last_refs, (out_hbm, products, last, out, sems) = refs[:-5], refs[-5:]
    bins, width, _ = own_ref.shape
    lanes = 2 * width
    offsets = out_hbm.shape[0]
    pitch = products.shape[1] // bins
    for which in range(2):

        def put(ref, which=which):
            last[which] = ref[...]

        copy_chosen(place_ref[2 + which], last_refs, put)

    def one_bin(f, carry):
        tops = [
            jnp.concatenate(
                [early_ref[which, slot, f] for slot in range(early_ref.shape[1])]
                + [last[which, f]],
                axis=0,
            )
            for which in range(2)
        ]
        bottoms = [jnp.concatenate([b[:, width:], -b[:, :width]], axis=1) for b in tops]
        right = jnp.concatenate(
            [jnp.concatenate(tops, axis=1), jnp.concatenate(bottoms, axis=1)], axis=0
        )
        both = jnp.dot(own_ref[f], right, preferred_element_type=jnp.float32)
        row = pl.multiple_of(f * pitch, 8)
        for half in range(2):
            products[half, pl.ds(row, width), :] = both[:, half * lanes : (half + 1) * lanes]
        return carry

    lax.fori_loop(0, bins, one_bin, 0, unroll=8)

    lane = lax.broadcasted_iota(jnp.int32, (offsets, 2 * lanes), 1)
    k = lax.broadcasted_iota(jnp.int32, (offsets, 2 * lanes), 0)
    partner = lane % width + jnp.where(lane >= lanes, width, 0)
    is_real = lane % lanes < width
    far = 4 * lanes
    shift_re = jnp.where(is_real, partner - k, far)
    shift_im = jnp.where(is_real, far, partner - k)
    row_k = lax.broadcasted_iota(jnp.int32, (offsets, F), 0) + place_ref[0]

    def copies(block):
        columns = pl.ds(pl.multiple_of(block * CHANNEL_BLOCK, CHANNEL_BLOCK), CHANNEL_BLOCK)
        return [
            pltpu.make_async_copy(
                out.at[part].reshape(offsets, pitch, F).at[:, columns, :],
                out_hbm.at[:, columns, pl.ds(part * F, F)],
                sems.at[block, part],
            )
            for part in range(2)
        ]

    def one_block(block, carry):
        for il in range(CHANNEL_BLOCK):
            i = block * CHANNEL_BLOCK + il
            at = i + place_ref[1]
            pick = jnp.concatenate(
                [
                    jnp.where(shift_re == at, 1.0, 0.0),
                    jnp.where(shift_im == at, -1.0, 0.0),
                ],
                axis=0,
            ).astype(jnp.bfloat16)
            x = jnp.concatenate(
                [products[half, pl.ds(i, F, stride=pitch), :] for half in range(2)], axis=1
            ).astype(jnp.bfloat16)
            y = lax.dot_general(
                pick, x, (((1,), (1,)), ((), ())), preferred_element_type=jnp.float32
            )
            inside = jnp.where(row_k < reach_ref[i], scale, 0.0)
            for part in range(2):
                out[part, pl.ds(i, offsets, stride=pitch), :] = (
                    y[part * offsets : (part + 1) * offsets] * inside
                )
        for copy in copies(block):
            copy.start()
        return carry

    blocks = width // CHANNEL_BLOCK
    lax.fori_loop(0, blocks, one_block, 0)

    def finish(block, carry):
        for copy in copies(block):
            copy.wait()
        return carry

    lax.fori_loop(0, blocks, finish, 0)


def stacked(own, early, last, place, reach, offsets, windows):
    bins, width, _ = own.shape
    chunk_windows, lanes = last[0].shape[1:]
    pitch = width + PITCH_PAD
    return pl.pallas_call(
        functools.partial(stack_kernel, 1.0 / math.sqrt(windows)),
        out_shape=jax.ShapeDtypeStruct((offsets, width, 2 * F), jnp.float32),
        in_specs=[SMEM, SMEM] + [VMEM] * (2 + len(last)),
        out_specs=ANY,
        scratch_shapes=[
            pltpu.VMEM((2, bins * pitch, lanes), jnp.float32),
            pltpu.VMEM((2, bins, chunk_windows, lanes), jnp.bfloat16),
            pltpu.VMEM((2, offsets * pitch, F), jnp.float32),
            pltpu.SemaphoreType.DMA((width // CHANNEL_BLOCK, 2)),
        ],
        compiler_params=pltpu.CompilerParams(vmem_limit_bytes=24 * MIB),
        cost_estimate=pl.CostEstimate(
            flops=16 * bins * width * width * windows,
            bytes_accessed=30_000_000,
            transcendentals=0,
        ),
        name="stack",
    )(jnp.stack([jnp.asarray(v, jnp.int32) for v in place]), reach, own, early, *last)


def send(array, pairs):
    return lax.ppermute(array, AXES, pairs)


def pairs_of(n_win, n_chan, target):
    pairs = []
    for z in range(n_win):
        for c in range(n_chan):
            to = target(z, c)
            if to is not None:
                pairs.append((c * n_win + z, to * n_win + z))
    return pairs


def after(array, *others):
    return lax.optimization_barrier((array, *others))[0]


def direct_partners(pieces, hops, n_win, n_chan):
    groups = []
    for piece in pieces:
        first = send(piece, pairs_of(n_win, n_chan, lambda z, c: (c - hops[z]) % n_chan))
        second = send(piece, pairs_of(n_win, n_chan, lambda z, c: (c - hops[z] - 1) % n_chan))
        groups.append((first, second))
    return choose((0, 1), groups[:-1]), groups[-1], (0, 1)


def square_partners(pieces, own, n_win, n_chan):
    def pairs(target):
        return pairs_of(n_win, n_chan, lambda z, c: target(z, c, c % 2, c // 2 % 2))

    def first_target(z, c, core, x):
        if z == 3:
            return c ^ 4
        if z == 0:
            return c ^ 2 if core == 0 else None
        if core == 1:
            return c ^ 2
        return c ^ 4 if z == 2 or x == 0 else None

    def second_target(z, c, core, x):
        if z == 3:
            return c ^ 2 if core == 1 else None
        if z == 0:
            return c ^ 4 if core == 0 and x == 1 else None
        if core == 0:
            return c ^ 2
        return c ^ 4 if x == 1 else None

    z, c = lax.axis_index("win"), lax.axis_index("chan")
    core, x = c % 2, c // 2 % 2
    onward = jnp.where((z == 0) | (x == 0) | ((z < 3) & (core == 1)), 1, 0)
    odd_next = jnp.where(x == 0, 1, 2)
    even_next = jnp.where(z == 0, odd_next, 2)
    next_code = jnp.where(core == 0, even_next, jnp.where(z == 3, 2, odd_next))
    outgoing = jnp.where(
        core == 0, jnp.where(z < 2, next_code, 1), jnp.where(z < 2, 0, next_code)
    )
    first_code = jnp.where(z == 0, 0, jnp.where(z == 2, next_code, 3))
    second_code = jnp.where(z == 1, next_code, jnp.where(z == 3, 1, 3))

    held = []
    for slot, piece in enumerate(pieces):
        start = after(piece, held[slot - 2][2]) if slot >= 2 else piece
        moved = send(start, pairs(first_target))
        if slot:
            moved = after(moved, own if slot == len(pieces) - 1 else pieces[slot + 1])
        relay = choose((onward,), [(piece, moved)])[0, 0]
        if slot == len(pieces) - 1:
            held[-1] = (*held[-1][:2], after(held[-1][2], relay))
        held.append((piece, moved, send(relay, pairs(second_target))))

    def swap(groups):
        return send(choose((outgoing,), groups)[0], pairs(lambda z, c, core, x: c ^ 1))

    piece, moved, relayed = held[-1]
    early = choose((first_code, second_code), held[:-1], swap(held[:-1]))
    relayed = after(relayed, early)
    swapped = swap([(piece, moved, relayed)])[0]
    return early, (piece, moved, relayed, swapped), (first_code, second_code)


def on_device(traces, valid, reach):
    width = traces.shape[1]
    n_win, n_chan = lax.axis_size("win"), lax.axis_size("chan")
    offsets = BAND // n_win
    hops = [z * offsets // width for z in range(n_win)]
    first_offset = lax.axis_index("win") * offsets
    pieces = [whitened_chunk(traces, valid)]
    while len(pieces) < n_win:
        ring = [(z, (z + 1) % n_win) for z in range(n_win)]
        pieces.append(lax.ppermute(pieces[-1], "win", ring))
    own = own_rows(pieces)
    if n_chan == 8 and hops == list(range(4)):
        early, last, codes = square_partners(pieces, own, n_win, n_chan)
    else:
        early, last, codes = direct_partners(pieces, hops, n_win, n_chan)
    place = (first_offset, first_offset % width, *codes)
    return stacked(own, early, last, place, reach, offsets, traces.shape[0] * n_win)


def solution(mesh):
    in_specs = (P("win", "chan", None), P("win", "chan"), P("chan"))
    out_specs = P("win", "chan", None)
    return jax.shard_map(
        on_device, mesh=mesh, in_specs=in_specs, out_specs=out_specs, check_vma=False
    )
```

```python
import functools
import math

import jax
import jax.numpy as jnp
import numpy as np
from jax import lax
from jax.experimental import pallas as pl
from jax.experimental.pallas import tpu as pltpu
from jax.sharding import PartitionSpec as P

F = 128
FIRST = 16
BAND = 256
AXES = ("chan", "win")
CHANNEL_BLOCK = 8
WHITEN_BLOCKS = 4
PITCH_PAD = 8
MIB = 1024 * 1024
COPY_BLOCKS = 4
WIDE_BYTES = 24 * MIB
VMEM = pl.BlockSpec(memory_space=pltpu.VMEM)
FEW_MIB = pltpu.CompilerParams(vmem_limit_bytes=4 * MIB)
WHOLE_VMEM = pltpu.CompilerParams(vmem_limit_bytes=62 * MIB)
SMEM = pl.BlockSpec(memory_space=pltpu.SMEM)
SMALL = pl.CostEstimate(flops=1, bytes_accessed=1, transcendentals=0)
ANY = pl.BlockSpec(memory_space=pl.ANY)


def make_table(samples):
    t_int = np.arange(samples, dtype=np.int64)
    j_int = np.arange(F, dtype=np.int64) + FIRST
    angle = 2.0 * np.pi / samples * (j_int[:, None] * t_int[None, :] % samples)
    hann = 0.5 - 0.5 * np.cos(2.0 * np.pi / samples * t_int)
    rows = np.concatenate([hann * np.cos(angle), -hann * np.sin(angle)], axis=0)
    return jnp.asarray(rows.astype(np.float32)).astype(jnp.bfloat16)


def whiten_kernel(table_hbm, traces_hbm, valid_hbm, out_ref, table, traces, valid, rows, sems):
    windows, width, samples = traces.shape
    block = windows // WHITEN_BLOCKS if windows % (2 * WHITEN_BLOCKS) == 0 else windows
    copies = [
        pltpu.make_async_copy(table_hbm, table, sems.at[0]),
        pltpu.make_async_copy(valid_hbm, valid, sems.at[1]),
    ]
    for n in range(windows // block):
        part = pl.ds(n * block, block)
        copies.append(
            pltpu.make_async_copy(traces_hbm.at[part], traces.at[part], sems.at[2 + n])
        )
    for copy in copies:
        copy.start()
    copies[0].wait()
    copies[1].wait()
    for w in range(0, windows, 2):
        if w % block == 0:
            copies[2 + w // block].wait()
        spectra = lax.dot_general(
            table[...],
            traces[w : w + 2].reshape(2 * width, samples),
            (((1,), (1,)), ((), ())),
            preferred_element_type=jnp.float32,
        )
        re, im = spectra[:F], spectra[F:]
        power = re * re + im * im
        level = jnp.sqrt(jnp.mean(power, axis=0, keepdims=True) + 1e-06)
        usable = jnp.concatenate([valid[w : w + 1, :], valid[w + 1 : w + 2, :]], axis=1)
        factor = usable.astype(jnp.float32) / (jnp.sqrt(power) + 0.1 * level)
        re, im = re * factor, im * factor
        for k in range(2):
            half = slice(k * width, (k + 1) * width)
            rows[pl.ds(w + k, F, stride=windows), :] = jnp.concatenate(
                [re[:, half], im[:, half]], axis=1
            )
    out_ref[...] = rows[...].reshape(out_ref.shape).astype(jnp.bfloat16)


def whitened_chunk(traces, valid):
    windows, width, samples = traces.shape
    return pl.pallas_call(
        whiten_kernel,
        out_shape=jax.ShapeDtypeStruct((F, windows, 2 * width), jnp.bfloat16),
        in_specs=[ANY] * 3,
        out_specs=VMEM,
        scratch_shapes=[
            pltpu.VMEM((2 * F, samples), jnp.bfloat16),
            pltpu.VMEM(traces.shape, traces.dtype),
            pltpu.VMEM(valid.shape, valid.dtype),
            pltpu.VMEM((F * windows, 2 * width), jnp.float32),
            pltpu.SemaphoreType.DMA((2 + WHITEN_BLOCKS,)),
        ],
        compiler_params=WHOLE_VMEM,
        cost_estimate=pl.CostEstimate(
            flops=4 * F * traces.size, bytes_accessed=2 * traces.size, transcendentals=0
        ),
        name="whiten",
    )(make_table(samples), traces, valid)


def copy_chosen(code, refs, put):
    for index, ref in enumerate(refs):

        @pl.when(code == index)
        def _(ref=ref):
            put(ref)


def choose_kernel(groups, code_ref, *refs):
    out_ref = refs[-1]
    per_group = (len(refs) - 1) // groups
    for g in range(groups):

        def put(ref, g=g):
            out_ref[g] = ref[...]

        copy_chosen(code_ref[0], refs[g * per_group : (g + 1) * per_group], put)


def choose(code, groups):
    operands = [buffer for group in groups for buffer in group]
    return pl.pallas_call(
        functools.partial(choose_kernel, len(groups)),
        out_shape=jax.ShapeDtypeStruct((len(groups), *groups[0][0].shape), jnp.bfloat16),
        in_specs=[SMEM] + [VMEM] * len(operands),
        out_specs=VMEM,
        compiler_params=FEW_MIB,
        cost_estimate=SMALL,
        name="choose",
    )(jnp.asarray(code, jnp.int32).reshape(1), *operands)


def bank_kernel(slot, codes_ref, *refs):
    store_ref, sems = refs[-2:]
    candidates = refs[:-2]

    def copy(candidate, to):
        return pltpu.make_async_copy(candidates[candidate], store_ref.at[to, slot], sems.at[to])

    copy(0, 0).start()
    for which in range(2):
        for candidate in range(len(candidates)):

            @pl.when(codes_ref[which] == candidate)
            def _(candidate=candidate, which=which):
                copy(candidate, 1 + which).start()

    for to in range(3):
        copy(0, to).wait()


def widened(places, shape):
    return (max(places, WIDE_BYTES // (2 * math.prod(shape))), *shape)


def bank(store, slot, slots, codes, candidates):
    shape = widened(3, (slots, *candidates[0].shape))
    operands = list(candidates)
    aliases = {}
    kernel = functools.partial(bank_kernel, slot)
    if store is not None:
        operands.append(store)
        aliases = {len(operands): 0}

        def kernel(codes_ref, *refs):
            bank_kernel(slot, codes_ref, *refs[: len(candidates)], *refs[-2:])

    return pl.pallas_call(
        kernel,
        out_shape=jax.ShapeDtypeStruct(shape, jnp.bfloat16),
        in_specs=[SMEM] + [VMEM] * len(candidates) + [ANY] * len(aliases),
        out_specs=ANY,
        scratch_shapes=[pltpu.SemaphoreType.DMA((3,))],
        input_output_aliases=aliases,
        compiler_params=FEW_MIB,
        cost_estimate=SMALL,
        name="bank",
    )(jnp.stack([jnp.asarray(code, jnp.int32) for code in codes]), *operands)


def own_kernel(early, store_ref, *refs):
    late_refs, (out_hbm, pieces, out, sems) = refs[:-4], refs[-4:]
    bins, width, _ = out.shape

    def load(slot):
        return pltpu.make_async_copy(store_ref.at[0, slot], pieces.at[slot], sems.at[slot])

    for slot in range(early):
        load(slot).start()
    for slot in range(early):
        load(slot).wait()

    def one_bin(f, carry):
        rows = [pieces[slot, f] for slot in range(early)] + [ref[f] for ref in late_refs]
        turned = jnp.concatenate(rows, axis=0).T
        out[f] = jnp.concatenate([turned[:width], turned[width:]], axis=1)
        return carry

    lax.fori_loop(0, bins, one_bin, 0, unroll=8)
    store = pltpu.make_async_copy(out, out_hbm.at[0], sems.at[0])
    store.start()
    store.wait()


def own_rows(store, late):
    bins, windows, lanes = late[0].shape
    early = store.shape[1]
    rows = (bins, lanes // 2, 2 * windows * (early + len(late)))
    return pl.pallas_call(
        functools.partial(own_kernel, early),
        out_shape=jax.ShapeDtypeStruct(widened(1, rows), jnp.bfloat16),
        in_specs=[ANY] + [VMEM] * len(late),
        out_specs=ANY,
        scratch_shapes=[
            pltpu.VMEM((early, bins, windows, lanes), jnp.bfloat16),
            pltpu.VMEM(rows, jnp.bfloat16),
            pltpu.SemaphoreType.DMA((early,)),
        ],
        compiler_params=pltpu.CompilerParams(vmem_limit_bytes=12 * MIB),
        cost_estimate=SMALL,
        name="own_rows",
    )(store, *late)


def stack_kernel(scale, groups, place_ref, reach_ref, own_hbm, store_ref, *refs):
    buffers, (out_hbm, own, partners, products, out, in_sems, sems) = refs[:-7], refs[-7:]
    bins, width, _ = own.shape
    lanes = 2 * width
    offsets = out_hbm.shape[0]
    pitch = products.shape[1] // bins
    slots = partners.shape[1]
    early = slots - len(groups)
    block_bins = bins // COPY_BLOCKS

    def loads(n):
        block = pl.ds(n * block_bins, block_bins)
        yield pltpu.make_async_copy(own_hbm.at[0, block], own.at[block], in_sems.at[n, 0])
        for which in range(2):
            yield pltpu.make_async_copy(
                store_ref.at[1 + which, :, block],
                partners.at[which, 0:early, block],
                in_sems.at[n, 1 + which],
            )

    for n in range(COPY_BLOCKS):
        for copy in loads(n):
            copy.start()
    for late, group in enumerate(groups):
        for which in range(2):
            candidates = [
                buffers[number] if index is None else buffers[number].at[index]
                for number, index in group
            ]

            def put(ref, late=late, which=which):
                partners[which, early + late] = ref[...]

            copy_chosen(place_ref[2 + 2 * late + which], candidates, put)

    def one_bin(f, carry):
        tops = [
            jnp.concatenate([partners[which, slot, f] for slot in range(slots)], axis=0)
            for which in range(2)
        ]
        bottoms = [jnp.concatenate([b[:, width:], -b[:, :width]], axis=1) for b in tops]
        right = jnp.concatenate(
            [jnp.concatenate(tops, axis=1), jnp.concatenate(bottoms, axis=1)], axis=0
        )
        both = jnp.dot(own[f], right, preferred_element_type=jnp.float32)
        row = pl.multiple_of(f * pitch, 8)
        for half in range(2):
            products[half, pl.ds(row, width), :] = both[:, half * lanes : (half + 1) * lanes]
        return carry

    for n in range(COPY_BLOCKS):
        for copy in loads(n):
            copy.wait()
        lax.fori_loop(n * block_bins, (n + 1) * block_bins, one_bin, 0, unroll=8)

    lane = lax.broadcasted_iota(jnp.int32, (offsets, 2 * lanes), 1)
    k = lax.broadcasted_iota(jnp.int32, (offsets, 2 * lanes), 0)
    partner = lane % width + jnp.where(lane >= lanes, width, 0)
    is_real = lane % lanes < width
    far = 4 * lanes
    shift_re = jnp.where(is_real, partner - k, far)
    shift_im = jnp.where(is_real, far, partner - k)
    row_k = lax.broadcasted_iota(jnp.int32, (offsets, F), 0) + place_ref[0]

    def copies(block):
        columns = pl.ds(pl.multiple_of(block * CHANNEL_BLOCK, CHANNEL_BLOCK), CHANNEL_BLOCK)
        return [
            pltpu.make_async_copy(
                out.at[part].reshape(offsets, pitch, F).at[:, columns, :],
                out_hbm.at[:, columns, pl.ds(part * F, F)],
                sems.at[block, part],
            )
            for part in range(2)
        ]

    def one_block(block, carry):
        for il in range(CHANNEL_BLOCK):
            i = block * CHANNEL_BLOCK + il
            at = i + place_ref[1]
            pick = jnp.concatenate(
                [
                    jnp.where(shift_re == at, 1.0, 0.0),
                    jnp.where(shift_im == at, -1.0, 0.0),
                ],
                axis=0,
            ).astype(jnp.bfloat16)
            x = jnp.concatenate(
                [products[half, pl.ds(i, F, stride=pitch), :] for half in range(2)], axis=1
            ).astype(jnp.bfloat16)
            y = lax.dot_general(
                pick, x, (((1,), (1,)), ((), ())), preferred_element_type=jnp.float32
            )
            inside = jnp.where(row_k < reach_ref[i], scale, 0.0)
            for part in range(2):
                out[part, pl.ds(i, offsets, stride=pitch), :] = (
                    y[part * offsets : (part + 1) * offsets] * inside
                )
        for copy in copies(block):
            copy.start()
        return carry

    blocks = width // CHANNEL_BLOCK
    lax.fori_loop(0, blocks, one_block, 0)

    def finish(block, carry):
        for copy in copies(block):
            copy.wait()
        return carry

    lax.fori_loop(0, blocks, finish, 0)


def stacked(own, store, buffers, groups, place, reach, offsets, windows):
    _, bins, width, depth = own.shape
    chunk_windows, lanes = buffers[0].shape[-2:]
    pitch = width + PITCH_PAD
    slots = store.shape[1] + len(groups)
    return pl.pallas_call(
        functools.partial(stack_kernel, 1.0 / math.sqrt(windows), groups),
        out_shape=jax.ShapeDtypeStruct((offsets, width, 2 * F), jnp.float32),
        in_specs=[SMEM, SMEM, ANY, ANY] + [VMEM] * len(buffers),
        out_specs=ANY,
        scratch_shapes=[
            pltpu.VMEM((bins, width, depth), own.dtype),
            pltpu.VMEM((2, slots, bins, chunk_windows, lanes), jnp.bfloat16),
            pltpu.VMEM((2, bins * pitch, lanes), jnp.float32),
            pltpu.VMEM((2, offsets * pitch, F), jnp.float32),
            pltpu.SemaphoreType.DMA((COPY_BLOCKS, 3)),
            pltpu.SemaphoreType.DMA((width // CHANNEL_BLOCK, 2)),
        ],
        compiler_params=pltpu.CompilerParams(vmem_limit_bytes=32 * MIB),
        cost_estimate=SMALL,
        name="stack",
    )(jnp.stack([jnp.asarray(v, jnp.int32) for v in place]), reach, own, store, *buffers)


def send(array, pairs):
    return lax.ppermute(array, AXES, pairs)


def pairs_of(n_win, n_chan, target):
    pairs = []
    for z in range(n_win):
        for c in range(n_chan):
            to = target(z, c)
            if to is not None:
                pairs.append((c * n_win + z, to * n_win + z))
    return pairs


def after(array, *others):
    return lax.optimization_barrier((array, *others))[0]


def direct_partners(pieces, hops, n_win, n_chan):
    held = []
    for piece in pieces:
        first = send(piece, pairs_of(n_win, n_chan, lambda z, c: (c - hops[z]) % n_chan))
        second = send(piece, pairs_of(n_win, n_chan, lambda z, c: (c - hops[z] - 1) % n_chan))
        held.append((piece, first, second))
    store = None
    early = len(pieces) - 2
    for slot in range(early):
        store = bank(store, slot, early, (1, 2), held[slot])
    buffers = [buffer for group in held[early:] for buffer in group]
    groups = [[(3 * n, None), (3 * n + 1, None), (3 * n + 2, None)] for n in range(2)]
    return own_rows(store, pieces[early:]), store, buffers, groups, (1, 2, 1, 2)


def square_partners(pieces, n_win, n_chan):
    def pairs(target):
        return pairs_of(n_win, n_chan, lambda z, c: target(z, c, c % 2, c // 2 % 2))

    def first_target(z, c, core, x):
        if z == 3:
            return c ^ 4
        if z == 0:
            return c ^ 2 if core == 0 else None
        if core == 1:
            return c ^ 2
        return c ^ 4 if z == 2 or x == 0 else None

    def second_target(z, c, core, x):
        if z == 3:
            return c ^ 2 if core == 1 else None
        if z == 0:
            return c ^ 4 if core == 0 and x == 1 else None
        if core == 0:
            return c ^ 2
        return c ^ 4 if x == 1 else None

    z, c = lax.axis_index("win"), lax.axis_index("chan")
    core, x = c % 2, c // 2 % 2
    onward = jnp.where((z == 0) | (x == 0) | ((z < 3) & (core == 1)), 1, 0)
    odd_next = jnp.where(x == 0, 1, 2)
    even_next = jnp.where(z == 0, odd_next, 2)
    next_code = jnp.where(core == 0, even_next, jnp.where(z == 3, 2, odd_next))
    late_one = jnp.where((z == 3) & (core == 0), 4, 1)
    outgoing = jnp.where(
        core == 0, jnp.where(z < 2, next_code, 1), jnp.where(z < 2, 0, next_code)
    )
    first_code = jnp.where(z == 0, 0, jnp.where(z == 2, next_code, 3))
    second_code = jnp.where(z == 1, next_code, jnp.where(z == 3, 1, 3))
    second_last = jnp.where(z == 1, next_code, jnp.where(z == 3, late_one, 3))

    def swap(code, groups):
        return send(choose(code, groups), pairs(lambda z, c, core, x: c ^ 1))

    count = len(pieces)
    early = count - 2
    held = []
    store = None
    for slot, piece in enumerate(pieces):
        last = slot == count - 1
        if slot >= 2:
            piece = after(piece, held[slot - 2][2])
        moved = send(
            piece,
            pairs(
                lambda z, c, core, x: (
                    None if last and z == 3 and core == 0 else first_target(z, c, core, x)
                )
            ),
        )
        if slot >= 2:
            group = held[slot - 2]
            swapped = swap(outgoing, [group])[0]
            store = bank(store, slot - 2, early, (first_code, second_code), (*group, swapped))
        if last:
            own = own_rows(store, pieces[early:])
        arrived = after(moved, own if last else pieces[slot + 1]) if slot else moved
        relay = choose(onward, [(piece, arrived)])[0]
        held.append((piece, moved, send(relay, pairs(second_target))))
    late = send(
        after(pieces[-1], relay),
        pairs(lambda z, c, core, x: c ^ 4 if z == 3 and core == 0 else None),
    )
    outgoing_late = jnp.where((outgoing == 1) & (late_one == 4), 3, outgoing)
    swapped = swap(outgoing_late, [(*held[-2], held[-2][1]), (*held[-1], late)])
    buffers = [*held[-2], *held[-1], swapped, late]
    groups = [
        [(0, None), (1, None), (2, None), (6, 0)],
        [(3, None), (4, None), (5, None), (6, 1), (7, None)],
    ]
    return own, store, buffers, groups, (first_code, second_code, first_code, second_last)


def on_device(traces, valid, reach):
    width = traces.shape[1]
    n_win, n_chan = lax.axis_size("win"), lax.axis_size("chan")
    offsets = BAND // n_win
    hops = [z * offsets // width for z in range(n_win)]
    first_offset = lax.axis_index("win") * offsets
    pieces = [whitened_chunk(traces, valid)]
    while len(pieces) < n_win:
        ring = [(z, (z + 1) % n_win) for z in range(n_win)]
        pieces.append(lax.ppermute(pieces[-1], "win", ring))
    if n_chan == 8 and hops == list(range(4)):
        own, store, buffers, groups, codes = square_partners(pieces, n_win, n_chan)
    else:
        own, store, buffers, groups, codes = direct_partners(pieces, hops, n_win, n_chan)
    place = (first_offset, first_offset % width, *codes)
    return stacked(
        own, store, buffers, groups, place, reach, offsets, traces.shape[0] * n_win
    )


def solution(mesh):
    in_specs = (P("win", "chan", None), P("win", "chan"), P("chan"))
    out_specs = P("win", "chan", None)
    return jax.shard_map(
        on_device, mesh=mesh, in_specs=in_specs, out_specs=out_specs, check_vma=False
    )
```

```python
import functools
import math

import jax
import jax.numpy as jnp
import numpy as np
from jax import lax
from jax.experimental import pallas as pl
from jax.experimental.pallas import tpu as pltpu
from jax.sharding import PartitionSpec as P

F = 128
FIRST = 16
BAND = 256
AXES = ("chan", "win")
CHANNEL_BLOCK = 8
WHITEN_BLOCKS = 4
PITCH_PAD = 8
MIB = 1024 * 1024
VMEM = pl.BlockSpec(memory_space=pltpu.VMEM)
FEW_MIB = pltpu.CompilerParams(vmem_limit_bytes=4 * MIB)
WHOLE_VMEM = pltpu.CompilerParams(vmem_limit_bytes=62 * MIB)
SMEM = pl.BlockSpec(memory_space=pltpu.SMEM)
SMALL = pl.CostEstimate(flops=1, bytes_accessed=1, transcendentals=0)
ANY = pl.BlockSpec(memory_space=pl.ANY)


def make_table(samples):
    t_int = np.arange(samples, dtype=np.int64)
    j_int = np.arange(F, dtype=np.int64) + FIRST
    angle = 2.0 * np.pi / samples * (j_int[:, None] * t_int[None, :] % samples)
    hann = 0.5 - 0.5 * np.cos(2.0 * np.pi / samples * t_int)
    rows = np.concatenate([hann * np.cos(angle), -hann * np.sin(angle)], axis=0)
    return jnp.asarray(rows.astype(np.float32)).astype(jnp.bfloat16)


def whiten_kernel(table_hbm, traces_hbm, valid_hbm, out_ref, table, traces, valid, rows, sems):
    windows, width, samples = traces.shape
    block = windows // WHITEN_BLOCKS if windows % (2 * WHITEN_BLOCKS) == 0 else windows
    copies = [
        pltpu.make_async_copy(table_hbm, table, sems.at[0]),
        pltpu.make_async_copy(valid_hbm, valid, sems.at[1]),
    ]
    for n in range(windows // block):
        part = pl.ds(n * block, block)
        copies.append(
            pltpu.make_async_copy(traces_hbm.at[part], traces.at[part], sems.at[2 + n])
        )
    for copy in copies:
        copy.start()
    copies[0].wait()
    copies[1].wait()
    for w in range(0, windows, 2):
        if w % block == 0:
            copies[2 + w // block].wait()
        spectra = lax.dot_general(
            table[...],
            traces[w : w + 2].reshape(2 * width, samples),
            (((1,), (1,)), ((), ())),
            preferred_element_type=jnp.float32,
        )
        re, im = spectra[:F], spectra[F:]
        power = re * re + im * im
        level = jnp.sqrt(jnp.mean(power, axis=0, keepdims=True) + 1e-06)
        usable = jnp.concatenate([valid[w : w + 1, :], valid[w + 1 : w + 2, :]], axis=1)
        factor = usable.astype(jnp.float32) / (jnp.sqrt(power) + 0.1 * level)
        re, im = re * factor, im * factor
        for k in range(2):
            half = slice(k * width, (k + 1) * width)
            rows[pl.ds(w + k, F, stride=windows), :] = jnp.concatenate(
                [re[:, half], im[:, half]], axis=1
            )
    out_ref[...] = rows[...].reshape(out_ref.shape).astype(jnp.bfloat16)


def whitened_chunk(traces, valid):
    windows, width, samples = traces.shape
    return pl.pallas_call(
        whiten_kernel,
        out_shape=jax.ShapeDtypeStruct((F, windows, 2 * width), jnp.bfloat16),
        in_specs=[ANY] * 3,
        out_specs=VMEM,
        scratch_shapes=[
            pltpu.VMEM((2 * F, samples), jnp.bfloat16),
            pltpu.VMEM(traces.shape, traces.dtype),
            pltpu.VMEM(valid.shape, valid.dtype),
            pltpu.VMEM((F * windows, 2 * width), jnp.float32),
            pltpu.SemaphoreType.DMA((2 + WHITEN_BLOCKS,)),
        ],
        compiler_params=WHOLE_VMEM,
        cost_estimate=pl.CostEstimate(
            flops=4 * F * traces.size, bytes_accessed=2 * traces.size, transcendentals=0
        ),
        name="whiten",
    )(make_table(samples), traces, valid)


def copy_chosen(code, refs, put):
    for index, ref in enumerate(refs):

        @pl.when(code == index)
        def _(ref=ref):
            put(ref)


def choose_kernel(code_of, groups, *refs):
    out_ref = refs[-1]
    per_group = (len(refs) - 1) // groups
    code = code_of()
    for g in range(groups):

        def put(ref, g=g):
            out_ref[g] = ref[...]

        copy_chosen(code, refs[g * per_group : (g + 1) * per_group], put)


def choose(code_of, groups):
    operands = [buffer for group in groups for buffer in group]
    return pl.pallas_call(
        functools.partial(choose_kernel, code_of, len(groups)),
        out_shape=jax.ShapeDtypeStruct((len(groups), *groups[0][0].shape), jnp.bfloat16),
        in_specs=[VMEM] * len(operands),
        out_specs=VMEM,
        compiler_params=FEW_MIB,
        cost_estimate=SMALL,
        name="choose",
    )(*operands)


def own_kernel(*refs):
    out_ref = refs[-1]
    width = out_ref.shape[1]

    def one_bin(f, carry):
        turned = jnp.concatenate([ref[f] for ref in refs[:-1]], axis=0).T
        out_ref[f] = jnp.concatenate([turned[:width], turned[width:]], axis=1)
        return carry

    lax.fori_loop(0, out_ref.shape[0], one_bin, 0, unroll=8)


def own_rows(pieces):
    bins, windows, lanes = pieces[0].shape
    return pl.pallas_call(
        own_kernel,
        out_shape=jax.ShapeDtypeStruct(
            (bins, lanes // 2, 2 * windows * len(pieces)), jnp.bfloat16
        ),
        in_specs=[VMEM] * len(pieces),
        out_specs=VMEM,
        compiler_params=FEW_MIB,
        cost_estimate=SMALL,
        name="own_rows",
    )(*pieces)


def stack_kernel(scale, groups, codes_of, reach_ref, own, *refs):
    buffers, (out_hbm, partners, products, out, sems) = refs[:-5], refs[-5:]
    bins, width, _ = own.shape
    lanes = 2 * width
    offsets = out_hbm.shape[0]
    pitch = products.shape[1] // bins
    slots = len(groups)
    first_offset = lax.axis_index("win") * offsets
    codes = codes_of()
    for slot, group in enumerate(groups):
        for which in range(2):
            candidates = [
                buffers[number] if index is None else buffers[number].at[index]
                for number, index in group
            ]

            def put(ref, slot=slot, which=which):
                partners[which, slot] = ref[...]

            copy_chosen(codes[which if slot < slots - 1 else 2 + which], candidates, put)

    def one_bin(f, carry):
        tops = [
            jnp.concatenate([partners[which, slot, f] for slot in range(slots)], axis=0)
            for which in range(2)
        ]
        bottoms = [jnp.concatenate([b[:, width:], -b[:, :width]], axis=1) for b in tops]
        right = jnp.concatenate(
            [jnp.concatenate(tops, axis=1), jnp.concatenate(bottoms, axis=1)], axis=0
        )
        both = jnp.dot(own[f], right, preferred_element_type=jnp.float32)
        row = pl.multiple_of(f * pitch, 8)
        for half in range(2):
            products[half, pl.ds(row, width), :] = both[:, half * lanes : (half + 1) * lanes]
        return carry

    lax.fori_loop(0, bins, one_bin, 0, unroll=8)

    lane = lax.broadcasted_iota(jnp.int32, (offsets, 2 * lanes), 1)
    k = lax.broadcasted_iota(jnp.int32, (offsets, 2 * lanes), 0)
    partner = lane % width + jnp.where(lane >= lanes, width, 0)
    is_real = lane % lanes < width
    far = 4 * lanes
    shift_re = jnp.where(is_real, partner - k, far)
    shift_im = jnp.where(is_real, far, partner - k)
    row_k = lax.broadcasted_iota(jnp.int32, (offsets, F), 0) + first_offset

    def copies(block):
        columns = pl.ds(pl.multiple_of(block * CHANNEL_BLOCK, CHANNEL_BLOCK), CHANNEL_BLOCK)
        return [
            pltpu.make_async_copy(
                out.at[part].reshape(offsets, pitch, F).at[:, columns, :],
                out_hbm.at[:, columns, pl.ds(part * F, F)],
                sems.at[block, part],
            )
            for part in range(2)
        ]

    def one_block(block, carry):
        for il in range(CHANNEL_BLOCK):
            i = block * CHANNEL_BLOCK + il
            at = i + first_offset % width
            pick = jnp.concatenate(
                [
                    jnp.where(shift_re == at, 1.0, 0.0),
                    jnp.where(shift_im == at, -1.0, 0.0),
                ],
                axis=0,
            ).astype(jnp.bfloat16)
            x = jnp.concatenate(
                [products[half, pl.ds(i, F, stride=pitch), :] for half in range(2)], axis=1
            ).astype(jnp.bfloat16)
            y = lax.dot_general(
                pick, x, (((1,), (1,)), ((), ())), preferred_element_type=jnp.float32
            )
            inside = jnp.where(row_k < reach_ref[i], scale, 0.0)
            for part in range(2):
                out[part, pl.ds(i, offsets, stride=pitch), :] = (
                    y[part * offsets : (part + 1) * offsets] * inside
                )
        for copy in copies(block):
            copy.start()
        return carry

    blocks = width // CHANNEL_BLOCK
    lax.fori_loop(0, blocks, one_block, 0)

    def finish(block, carry):
        for copy in copies(block):
            copy.wait()
        return carry

    lax.fori_loop(0, blocks, finish, 0)


def stacked(own, buffers, groups, codes_of, reach, offsets, windows):
    bins, width, _ = own.shape
    chunk_windows, lanes = buffers[0].shape[-2:]
    pitch = width + PITCH_PAD
    return pl.pallas_call(
        functools.partial(stack_kernel, 1.0 / math.sqrt(windows), groups, codes_of),
        out_shape=jax.ShapeDtypeStruct((offsets, width, 2 * F), jnp.float32),
        in_specs=[SMEM] + [VMEM] * (1 + len(buffers)),
        out_specs=ANY,
        scratch_shapes=[
            pltpu.VMEM((2, len(groups), bins, chunk_windows, lanes), jnp.bfloat16),
            pltpu.VMEM((2, bins * pitch, lanes), jnp.float32),
            pltpu.VMEM((2, offsets * pitch, F), jnp.float32),
            pltpu.SemaphoreType.DMA((width // CHANNEL_BLOCK, 2)),
        ],
        compiler_params=pltpu.CompilerParams(vmem_limit_bytes=28 * MIB),
        cost_estimate=SMALL,
        name="stack",
    )(reach, own, *buffers)


def send(array, pairs):
    return lax.ppermute(array, AXES, pairs)


def pairs_of(n_win, n_chan, target):
    pairs = []
    for z in range(n_win):
        for c in range(n_chan):
            to = target(z, c)
            if to is not None:
                pairs.append((c * n_win + z, to * n_win + z))
    return pairs


def after(array, *others):
    return lax.optimization_barrier((array, *others))[0]


def direct_partners(pieces, hops, n_win, n_chan):
    buffers = []
    for piece in pieces:
        buffers.append(send(piece, pairs_of(n_win, n_chan, lambda z, c: (c - hops[z]) % n_chan)))
        buffers.append(
            send(piece, pairs_of(n_win, n_chan, lambda z, c: (c - hops[z] - 1) % n_chan))
        )
    groups = [[(2 * n, None), (2 * n + 1, None)] for n in range(len(pieces))]
    return own_rows(pieces), buffers, groups, lambda: (0, 1, 0, 1)


def square_codes():
    z, c = lax.axis_index("win"), lax.axis_index("chan")
    core, x = c & 1, (c >> 1) & 1
    onward = jnp.where((z == 0) | (x == 0) | ((z < 3) & (core == 1)), 1, 0)
    odd_next = jnp.where(x == 0, 1, 2)
    even_next = jnp.where(z == 0, odd_next, 2)
    next_code = jnp.where(core == 0, even_next, jnp.where(z == 3, 2, odd_next))
    outgoing = jnp.where(core == 0, jnp.where(z < 2, next_code, 1), jnp.where(z < 2, 0, next_code))
    first = jnp.where(z == 0, 0, jnp.where(z == 2, next_code, 3))
    second = jnp.where(z == 1, next_code, jnp.where(z == 3, 1, 3))
    is_late = (z == 3) & (core == 0)
    outgoing_late = jnp.where(is_late, 3, outgoing)
    second_last = jnp.where(is_late, 4, second)
    return onward, outgoing, outgoing_late, (first, second, first, second_last)


def square_partners(pieces, n_win, n_chan):
    def pairs(target):
        return pairs_of(n_win, n_chan, lambda z, c: target(z, c, c % 2, c // 2 % 2))

    def first_target(z, c, core, x):
        if z == 3:
            return c ^ 4
        if z == 0:
            return c ^ 2 if core == 0 else None
        if core == 1:
            return c ^ 2
        return c ^ 4 if z == 2 or x == 0 else None

    def second_target(z, c, core, x):
        if z == 3:
            return c ^ 2 if core == 1 else None
        if z == 0:
            return c ^ 4 if core == 0 and x == 1 else None
        if core == 0:
            return c ^ 2
        return c ^ 4 if x == 1 else None

    def swap(code_of, groups):
        return send(choose(code_of, groups), pairs(lambda z, c, core, x: c ^ 1))

    count = len(pieces)
    half = count // 2
    held = []
    for slot, piece in enumerate(pieces):
        last = slot == count - 1
        if slot:
            piece = after(piece, held[slot - 1][1], *([held[slot - 2][2]] if slot >= 2 else []))
        moved = send(
            piece,
            pairs(
                lambda z, c, core, x: (
                    None if last and z == 3 and core == 0 else first_target(z, c, core, x)
                )
            ),
        )
        arrived = moved
        if last:
            held[0] = (*held[0][:2], after(held[0][2], piece))
            swapped_early = swap(lambda: square_codes()[1], held[:half])
            own = own_rows([*pieces[:-1], after(piece, swapped_early)])
            arrived = after(moved, own)
        elif True:
            arrived = after(moved, pieces[slot + 1])
        relay = choose(lambda: square_codes()[0], [(piece, arrived)])[0]
        held.append((piece, moved, send(relay, pairs(second_target))))
    late = send(
        after(pieces[-1], relay),
        pairs(lambda z, c, core, x: c ^ 4 if z == 3 and core == 0 else None),
    )
    late_groups = [(*group, group[1]) for group in held[half:-1]] + [(*held[-1], late)]
    swapped_late = swap(lambda: square_codes()[2], late_groups)
    buffers = [buffer for group in held for buffer in group] + [swapped_early, swapped_late, late]
    groups = []
    for n in range(count):
        swapped = (3 * count, n) if n < half else (3 * count + 1, n - half)
        groups.append([(3 * n, None), (3 * n + 1, None), (3 * n + 2, None), swapped])
    groups[-1].append((3 * count + 2, None))
    return own, buffers, groups, lambda: square_codes()[3]


def on_device(traces, valid, reach):
    width = traces.shape[1]
    n_win, n_chan = lax.axis_size("win"), lax.axis_size("chan")
    offsets = BAND // n_win
    hops = [z * offsets // width for z in range(n_win)]
    pieces = [whitened_chunk(traces, valid)]
    while len(pieces) < n_win:
        ring = [(z, (z + 1) % n_win) for z in range(n_win)]
        pieces.append(lax.ppermute(pieces[-1], "win", ring))
    if n_chan == 8 and hops == list(range(4)):
        own, buffers, groups, codes_of = square_partners(pieces, n_win, n_chan)
    else:
        own, buffers, groups, codes_of = direct_partners(pieces, hops, n_win, n_chan)
    return stacked(own, buffers, groups, codes_of, reach, offsets, traces.shape[0] * n_win)


def solution(mesh):
    in_specs = (P("win", "chan", None), P("win", "chan"), P("chan"))
    out_specs = P("win", "chan", None)
    return jax.shard_map(
        on_device, mesh=mesh, in_specs=in_specs, out_specs=out_specs, check_vma=False
    )
```

```python
import functools
import math

import jax
import jax.numpy as jnp
import numpy as np
from jax import lax
from jax.experimental import pallas as pl
from jax.experimental.pallas import tpu as pltpu
from jax.sharding import PartitionSpec as P

F = 128
FIRST = 16
BAND = 256
AXES = ("chan", "win")
CHANNEL_BLOCK = 8
WHITEN_BLOCKS = 4
PITCH_PAD = 8
MIB = 1024 * 1024
VMEM = pl.BlockSpec(memory_space=pltpu.VMEM)
FEW_MIB = pltpu.CompilerParams(vmem_limit_bytes=4 * MIB)
WHOLE_VMEM = pltpu.CompilerParams(vmem_limit_bytes=62 * MIB)
SMEM = pl.BlockSpec(memory_space=pltpu.SMEM)
SMALL = pl.CostEstimate(flops=1, bytes_accessed=1, transcendentals=0)
ANY = pl.BlockSpec(memory_space=pl.ANY)


def make_table(samples):
    t_int = np.arange(samples, dtype=np.int64)
    j_int = np.arange(F, dtype=np.int64) + FIRST
    angle = 2.0 * np.pi / samples * (j_int[:, None] * t_int[None, :] % samples)
    hann = 0.5 - 0.5 * np.cos(2.0 * np.pi / samples * t_int)
    rows = np.concatenate([hann * np.cos(angle), -hann * np.sin(angle)], axis=0)
    return jnp.asarray(rows.astype(np.float32)).astype(jnp.bfloat16)


def whiten_kernel(table_hbm, traces_hbm, valid_hbm, out_ref, table, traces, valid, rows, sems):
    windows, width, samples = traces.shape
    block = windows // WHITEN_BLOCKS if windows % (2 * WHITEN_BLOCKS) == 0 else windows
    copies = [
        pltpu.make_async_copy(table_hbm, table, sems.at[0]),
        pltpu.make_async_copy(valid_hbm, valid, sems.at[1]),
    ]
    for n in range(windows // block):
        part = pl.ds(n * block, block)
        copies.append(
            pltpu.make_async_copy(traces_hbm.at[part], traces.at[part], sems.at[2 + n])
        )
    for copy in copies:
        copy.start()
    copies[0].wait()
    copies[1].wait()
    for w in range(0, windows, 2):
        if w % block == 0:
            copies[2 + w // block].wait()
        spectra = lax.dot_general(
            table[...],
            traces[w : w + 2].reshape(2 * width, samples),
            (((1,), (1,)), ((), ())),
            preferred_element_type=jnp.float32,
        )
        re, im = spectra[:F], spectra[F:]
        power = re * re + im * im
        level = jnp.sqrt(jnp.mean(power, axis=0, keepdims=True) + 1e-06)
        usable = jnp.concatenate([valid[w : w + 1, :], valid[w + 1 : w + 2, :]], axis=1)
        factor = usable.astype(jnp.float32) / (jnp.sqrt(power) + 0.1 * level)
        re, im = re * factor, im * factor
        for k in range(2):
            half = slice(k * width, (k + 1) * width)
            rows[pl.ds(w + k, F, stride=windows), :] = jnp.concatenate(
                [re[:, half], im[:, half]], axis=1
            )
    out_ref[...] = rows[...].reshape(out_ref.shape).astype(jnp.bfloat16)


def whitened_chunk(traces, valid):
    windows, width, samples = traces.shape
    return pl.pallas_call(
        whiten_kernel,
        out_shape=jax.ShapeDtypeStruct((F, windows, 2 * width), jnp.bfloat16),
        in_specs=[ANY] * 3,
        out_specs=VMEM,
        scratch_shapes=[
            pltpu.VMEM((2 * F, samples), jnp.bfloat16),
            pltpu.VMEM(traces.shape, traces.dtype),
            pltpu.VMEM(valid.shape, valid.dtype),
            pltpu.VMEM((F * windows, 2 * width), jnp.float32),
            pltpu.SemaphoreType.DMA((2 + WHITEN_BLOCKS,)),
        ],
        compiler_params=WHOLE_VMEM,
        cost_estimate=pl.CostEstimate(
            flops=4 * F * traces.size, bytes_accessed=2 * traces.size, transcendentals=0
        ),
        name="whiten",
    )(make_table(samples), traces, valid)


def copy_chosen(code, refs, put):
    for index, ref in enumerate(refs):

        @pl.when(code == index)
        def _(ref=ref):
            put(ref)


def choose_kernel(code_of, groups, *refs):
    out_ref = refs[-1]
    per_group = (len(refs) - 1) // groups
    code = code_of()
    for g in range(groups):

        def put(ref, g=g):
            out_ref[g] = ref[...]

        copy_chosen(code, refs[g * per_group : (g + 1) * per_group], put)


def choose(code_of, groups):
    operands = [buffer for group in groups for buffer in group]
    return pl.pallas_call(
        functools.partial(choose_kernel, code_of, len(groups)),
        out_shape=jax.ShapeDtypeStruct((len(groups), *groups[0][0].shape), jnp.bfloat16),
        in_specs=[VMEM] * len(operands),
        out_specs=VMEM,
        compiler_params=FEW_MIB,
        cost_estimate=SMALL,
        name="choose",
    )(*operands)


def own_kernel(*refs):
    out_ref = refs[-1]
    width = out_ref.shape[1]

    def one_bin(f, carry):
        turned = jnp.concatenate([ref[f] for ref in refs[:-1]], axis=0).T
        out_ref[f] = jnp.concatenate([turned[:width], turned[width:]], axis=1)
        return carry

    lax.fori_loop(0, out_ref.shape[0], one_bin, 0, unroll=8)


def own_rows(pieces):
    bins, windows, lanes = pieces[0].shape
    return pl.pallas_call(
        own_kernel,
        out_shape=jax.ShapeDtypeStruct(
            (bins, lanes // 2, 2 * windows * len(pieces)), jnp.bfloat16
        ),
        in_specs=[VMEM] * len(pieces),
        out_specs=VMEM,
        compiler_params=FEW_MIB,
        cost_estimate=SMALL,
        name="own_rows",
    )(*pieces)


def stack_kernel(scale, groups, codes_of, reach_ref, own, *refs):
    buffers, (out_hbm, partners, products, out, sems) = refs[:-5], refs[-5:]
    bins, width, _ = own.shape
    lanes = 2 * width
    offsets = out_hbm.shape[0]
    pitch = products.shape[1] // bins
    slots = len(groups)
    first_offset = lax.axis_index("win") * offsets
    codes = codes_of()
    for slot, group in enumerate(groups):
        for which in range(2):
            candidates = [
                buffers[number] if index is None else buffers[number].at[index]
                for number, index in group
            ]

            def put(ref, slot=slot, which=which):
                partners[which, slot] = ref[...]

            copy_chosen(codes[which if slot < slots - 1 else 2 + which], candidates, put)

    def one_bin(f, carry):
        tops = [
            jnp.concatenate([partners[which, slot, f] for slot in range(slots)], axis=0)
            for which in range(2)
        ]
        bottoms = [jnp.concatenate([b[:, width:], -b[:, :width]], axis=1) for b in tops]
        right = jnp.concatenate(
            [jnp.concatenate(tops, axis=1), jnp.concatenate(bottoms, axis=1)], axis=0
        )
        both = jnp.dot(own[f], right, preferred_element_type=jnp.float32)
        row = pl.multiple_of(f * pitch, 8)
        for half in range(2):
            products[half, pl.ds(row, width), :] = both[:, half * lanes : (half + 1) * lanes]
        return carry

    lax.fori_loop(0, bins, one_bin, 0, unroll=8)

    lane = lax.broadcasted_iota(jnp.int32, (offsets, 2 * lanes), 1)
    k = lax.broadcasted_iota(jnp.int32, (offsets, 2 * lanes), 0)
    partner = lane % width + jnp.where(lane >= lanes, width, 0)
    is_real = lane % lanes < width
    far = 4 * lanes
    shift_re = jnp.where(is_real, partner - k, far)
    shift_im = jnp.where(is_real, far, partner - k)
    row_k = lax.broadcasted_iota(jnp.int32, (offsets, F), 0) + first_offset

    def copies(block):
        columns = pl.ds(pl.multiple_of(block * CHANNEL_BLOCK, CHANNEL_BLOCK), CHANNEL_BLOCK)
        return [
            pltpu.make_async_copy(
                out.at[part].reshape(offsets, pitch, F).at[:, columns, :],
                out_hbm.at[:, columns, pl.ds(part * F, F)],
                sems.at[block, part],
            )
            for part in range(2)
        ]

    def one_block(block, carry):
        for il in range(CHANNEL_BLOCK):
            i = block * CHANNEL_BLOCK + il
            at = i + first_offset % width
            pick = jnp.concatenate(
                [
                    jnp.where(shift_re == at, 1.0, 0.0),
                    jnp.where(shift_im == at, -1.0, 0.0),
                ],
                axis=0,
            ).astype(jnp.bfloat16)
            x = jnp.concatenate(
                [products[half, pl.ds(i, F, stride=pitch), :] for half in range(2)], axis=1
            ).astype(jnp.bfloat16)
            y = lax.dot_general(
                pick, x, (((1,), (1,)), ((), ())), preferred_element_type=jnp.float32
            )
            inside = jnp.where(row_k < reach_ref[i], scale, 0.0)
            for part in range(2):
                out[part, pl.ds(i, offsets, stride=pitch), :] = (
                    y[part * offsets : (part + 1) * offsets] * inside
                )
        for copy in copies(block):
            copy.start()
        return carry

    blocks = width // CHANNEL_BLOCK
    lax.fori_loop(0, blocks, one_block, 0)

    def finish(block, carry):
        for copy in copies(block):
            copy.wait()
        return carry

    lax.fori_loop(0, blocks, finish, 0)


def stacked(own, buffers, groups, codes_of, reach, offsets, windows):
    bins, width, _ = own.shape
    chunk_windows, lanes = buffers[0].shape[-2:]
    pitch = width + PITCH_PAD
    return pl.pallas_call(
        functools.partial(stack_kernel, 1.0 / math.sqrt(windows), groups, codes_of),
        out_shape=jax.ShapeDtypeStruct((offsets, width, 2 * F), jnp.float32),
        in_specs=[SMEM] + [VMEM] * (1 + len(buffers)),
        out_specs=ANY,
        scratch_shapes=[
            pltpu.VMEM((2, len(groups), bins, chunk_windows, lanes), jnp.bfloat16),
            pltpu.VMEM((2, bins * pitch, lanes), jnp.float32),
            pltpu.VMEM((2, offsets * pitch, F), jnp.float32),
            pltpu.SemaphoreType.DMA((width // CHANNEL_BLOCK, 2)),
        ],
        compiler_params=pltpu.CompilerParams(vmem_limit_bytes=28 * MIB),
        cost_estimate=SMALL,
        name="stack",
    )(reach, own, *buffers)


def send(array, pairs):
    return lax.ppermute(array, AXES, pairs)


def pairs_of(n_win, n_chan, target):
    pairs = []
    for z in range(n_win):
        for c in range(n_chan):
            to = target(z, c)
            if to is not None:
                pairs.append((c * n_win + z, to * n_win + z))
    return pairs


def after(array, *others):
    return lax.optimization_barrier((array, *others))[0]


def direct_partners(pieces, hops, n_win, n_chan):
    buffers = []
    for piece in pieces:
        buffers.append(send(piece, pairs_of(n_win, n_chan, lambda z, c: (c - hops[z]) % n_chan)))
        buffers.append(
            send(piece, pairs_of(n_win, n_chan, lambda z, c: (c - hops[z] - 1) % n_chan))
        )
    groups = [[(2 * n, None), (2 * n + 1, None)] for n in range(len(pieces))]
    return own_rows(pieces), buffers, groups, lambda: (0, 1, 0, 1)


def square_codes():
    z, c = lax.axis_index("win"), lax.axis_index("chan")
    core, x = c & 1, (c >> 1) & 1
    onward = jnp.where((z == 0) | (x == 0) | ((z < 3) & (core == 1)), 1, 0)
    odd_next = jnp.where(x == 0, 1, 2)
    even_next = jnp.where(z == 0, odd_next, 2)
    next_code = jnp.where(core == 0, even_next, jnp.where(z == 3, 2, odd_next))
    outgoing = jnp.where(core == 0, jnp.where(z < 2, next_code, 1), jnp.where(z < 2, 0, next_code))
    first = jnp.where(z == 0, 0, jnp.where(z == 2, next_code, 3))
    second = jnp.where(z == 1, next_code, jnp.where(z == 3, 1, 3))
    is_late = (z == 3) & (core == 0)
    outgoing_late = jnp.where(is_late, 3, outgoing)
    second_last = jnp.where(is_late, 4, second)
    return onward, outgoing, outgoing_late, (first, second, first, second_last)


def square_partners(pieces, n_win, n_chan):
    def pairs(target):
        return pairs_of(n_win, n_chan, lambda z, c: target(z, c, c % 2, c // 2 % 2))

    def first_target(z, c, core, x):
        if z == 3:
            return c ^ 4
        if z == 0:
            return c ^ 2 if core == 0 else None
        if core == 1:
            return c ^ 2
        return c ^ 4 if z == 2 or x == 0 else None

    def second_target(z, c, core, x):
        if z == 3:
            return c ^ 2 if core == 1 else None
        if z == 0:
            return c ^ 4 if core == 0 and x == 1 else None
        if core == 0:
            return c ^ 2
        return c ^ 4 if x == 1 else None

    def swap(code_of, groups):
        return send(choose(code_of, groups), pairs(lambda z, c, core, x: c ^ 1))

    count = len(pieces)
    half = count // 2
    firsts, seconds = [], []

    def second_move(slot, arrived):
        relay = choose(lambda: square_codes()[0], [(pieces[slot], arrived)])[0]
        seconds.append(send(relay, pairs(second_target)))
        return relay

    for slot, piece in enumerate(pieces):
        last = slot == count - 1
        if slot >= 2:
            piece = after(piece, firsts[slot - 2])
        firsts.append(
            send(
                piece,
                pairs(
                    lambda z, c, core, x: (
                        None if last and z == 3 and core == 0 else first_target(z, c, core, x)
                    )
                ),
            )
        )
        if slot:
            arrived = firsts[slot - 1]
            arrived = after(arrived, *seconds[-1:])
            second_move(slot - 1, arrived)
    held = list(zip(pieces, firsts, seconds))
    own = own_rows(pieces)
    held[0] = (*held[0][:2], after(held[0][2], firsts[-1]))
    swapped_early = swap(lambda: square_codes()[1], held[:half])
    arrived = after(firsts[-1], own)
    relay = second_move(count - 1, arrived)
    held.append((pieces[-1], firsts[-1], seconds[-1]))
    late = send(
        after(pieces[-1], relay),
        pairs(lambda z, c, core, x: c ^ 4 if z == 3 and core == 0 else None),
    )
    late_groups = [(*group, group[1]) for group in held[half:-1]] + [(*held[-1], late)]
    swapped_late = swap(lambda: square_codes()[2], late_groups)
    buffers = [buffer for group in held for buffer in group] + [swapped_early, swapped_late, late]
    groups = []
    for n in range(count):
        swapped = (3 * count, n) if n < half else (3 * count + 1, n - half)
        groups.append([(3 * n, None), (3 * n + 1, None), (3 * n + 2, None), swapped])
    groups[-1].append((3 * count + 2, None))
    return own, buffers, groups, lambda: square_codes()[3]


def on_device(traces, valid, reach):
    width = traces.shape[1]
    n_win, n_chan = lax.axis_size("win"), lax.axis_size("chan")
    offsets = BAND // n_win
    hops = [z * offsets // width for z in range(n_win)]
    pieces = [whitened_chunk(traces, valid)]
    while len(pieces) < n_win:
        ring = [(z, (z + 1) % n_win) for z in range(n_win)]
        pieces.append(lax.ppermute(pieces[-1], "win", ring))
    if n_chan == 8 and hops == list(range(4)):
        own, buffers, groups, codes_of = square_partners(pieces, n_win, n_chan)
    else:
        own, buffers, groups, codes_of = direct_partners(pieces, hops, n_win, n_chan)
    return stacked(own, buffers, groups, codes_of, reach, offsets, traces.shape[0] * n_win)


def solution(mesh):
    in_specs = (P("win", "chan", None), P("win", "chan"), P("chan"))
    out_specs = P("win", "chan", None)
    return jax.shard_map(
        on_device, mesh=mesh, in_specs=in_specs, out_specs=out_specs, check_vma=False
    )
```

```python
import functools
import math

import jax
import jax.numpy as jnp
import numpy as np
from jax import lax
from jax.experimental import pallas as pl
from jax.experimental.pallas import tpu as pltpu
from jax.sharding import PartitionSpec as P

F = 128
FIRST = 16
BAND = 256
AXES = ("chan", "win")
CHANNEL_BLOCK = 8
WHITEN_BLOCKS = 4
PITCH_PAD = 8
MIB = 1024 * 1024
VMEM = pl.BlockSpec(memory_space=pltpu.VMEM)
FEW_MIB = pltpu.CompilerParams(vmem_limit_bytes=4 * MIB)
WHOLE_VMEM = pltpu.CompilerParams(vmem_limit_bytes=62 * MIB)
SMEM = pl.BlockSpec(memory_space=pltpu.SMEM)
SMALL = pl.CostEstimate(flops=1, bytes_accessed=1, transcendentals=0)
ANY = pl.BlockSpec(memory_space=pl.ANY)


def make_table(samples):
    t_int = np.arange(samples, dtype=np.int64)
    j_int = np.arange(F, dtype=np.int64) + FIRST
    angle = 2.0 * np.pi / samples * (j_int[:, None] * t_int[None, :] % samples)
    hann = 0.5 - 0.5 * np.cos(2.0 * np.pi / samples * t_int)
    rows = np.concatenate([hann * np.cos(angle), -hann * np.sin(angle)], axis=0)
    return jnp.asarray(rows.astype(np.float32)).astype(jnp.bfloat16)


def whiten_kernel(table_hbm, traces_hbm, valid_hbm, out_ref, table, traces, valid, rows, sems):
    windows, width, samples = traces.shape
    block = windows // WHITEN_BLOCKS if windows % (2 * WHITEN_BLOCKS) == 0 else windows
    copies = [
        pltpu.make_async_copy(table_hbm, table, sems.at[0]),
        pltpu.make_async_copy(valid_hbm, valid, sems.at[1]),
    ]
    for n in range(windows // block):
        part = pl.ds(n * block, block)
        copies.append(
            pltpu.make_async_copy(traces_hbm.at[part], traces.at[part], sems.at[2 + n])
        )
    for copy in copies:
        copy.start()
    copies[0].wait()
    copies[1].wait()
    for w in range(0, windows, 2):
        if w % block == 0:
            copies[2 + w // block].wait()
        spectra = lax.dot_general(
            table[...],
            traces[w : w + 2].reshape(2 * width, samples),
            (((1,), (1,)), ((), ())),
            preferred_element_type=jnp.float32,
        )
        re, im = spectra[:F], spectra[F:]
        power = re * re + im * im
        level = jnp.sqrt(jnp.mean(power, axis=0, keepdims=True) + 1e-06)
        usable = jnp.concatenate([valid[w : w + 1, :], valid[w + 1 : w + 2, :]], axis=1)
        factor = usable.astype(jnp.float32) / (jnp.sqrt(power) + 0.1 * level)
        re, im = re * factor, im * factor
        for k in range(2):
            half = slice(k * width, (k + 1) * width)
            rows[pl.ds(w + k, F, stride=windows), :] = jnp.concatenate(
                [re[:, half], im[:, half]], axis=1
            )
    out_ref[...] = rows[...].reshape(out_ref.shape).astype(jnp.bfloat16)


def whitened_chunk(traces, valid):
    windows, width, samples = traces.shape
    return pl.pallas_call(
        whiten_kernel,
        out_shape=jax.ShapeDtypeStruct((F, windows, 2 * width), jnp.bfloat16),
        in_specs=[ANY] * 3,
        out_specs=VMEM,
        scratch_shapes=[
            pltpu.VMEM((2 * F, samples), jnp.bfloat16),
            pltpu.VMEM(traces.shape, traces.dtype),
            pltpu.VMEM(valid.shape, valid.dtype),
            pltpu.VMEM((F * windows, 2 * width), jnp.float32),
            pltpu.SemaphoreType.DMA((2 + WHITEN_BLOCKS,)),
        ],
        compiler_params=WHOLE_VMEM,
        cost_estimate=pl.CostEstimate(
            flops=4 * F * traces.size, bytes_accessed=2 * traces.size, transcendentals=0
        ),
        name="whiten",
    )(make_table(samples), traces, valid)


def copy_chosen(code, refs, put):
    for index, ref in enumerate(refs):

        @pl.when(code == index)
        def _(ref=ref):
            put(ref)


def choose_kernel(code_of, groups, *refs):
    out_ref = refs[-1]
    per_group = (len(refs) - 1) // groups
    code = code_of()
    for g in range(groups):

        def put(ref, g=g):
            out_ref[g] = ref[...]

        copy_chosen(code, refs[g * per_group : (g + 1) * per_group], put)


def choose(code_of, groups):
    operands = [buffer for group in groups for buffer in group]
    return pl.pallas_call(
        functools.partial(choose_kernel, code_of, len(groups)),
        out_shape=jax.ShapeDtypeStruct((len(groups), *groups[0][0].shape), jnp.bfloat16),
        in_specs=[VMEM] * len(operands),
        out_specs=VMEM,
        compiler_params=FEW_MIB,
        cost_estimate=SMALL,
        name="choose",
    )(*operands)


def own_kernel(*refs):
    out_ref = refs[-1]
    width = out_ref.shape[1]

    def one_bin(f, carry):
        turned = jnp.concatenate([ref[f] for ref in refs[:-1]], axis=0).T
        out_ref[f] = jnp.concatenate([turned[:width], turned[width:]], axis=1)
        return carry

    lax.fori_loop(0, out_ref.shape[0], one_bin, 0, unroll=8)


def own_rows(pieces):
    bins, windows, lanes = pieces[0].shape
    return pl.pallas_call(
        own_kernel,
        out_shape=jax.ShapeDtypeStruct(
            (bins, lanes // 2, 2 * windows * len(pieces)), jnp.bfloat16
        ),
        in_specs=[VMEM] * len(pieces),
        out_specs=VMEM,
        compiler_params=FEW_MIB,
        cost_estimate=SMALL,
        name="own_rows",
    )(*pieces)


def stack_kernel(scale, groups, codes_of, reach_ref, own, *refs):
    buffers, (out_hbm, partners, products, out, sems) = refs[:-5], refs[-5:]
    bins, width, _ = own.shape
    lanes = 2 * width
    offsets = out_hbm.shape[0]
    pitch = products.shape[1] // bins
    slots = len(groups)
    first_offset = lax.axis_index("win") * offsets
    codes = codes_of()
    for slot, group in enumerate(groups):
        for which in range(2):
            candidates = [
                buffers[number] if index is None else buffers[number].at[index]
                for number, index in group
            ]

            def put(ref, slot=slot, which=which):
                partners[which, slot] = ref[...]

            copy_chosen(codes[which if slot < slots - 1 else 2 + which], candidates, put)

    def one_bin(f, carry):
        tops = [
            jnp.concatenate([partners[which, slot, f] for slot in range(slots)], axis=0)
            for which in range(2)
        ]
        bottoms = [jnp.concatenate([b[:, width:], -b[:, :width]], axis=1) for b in tops]
        right = jnp.concatenate(
            [jnp.concatenate(tops, axis=1), jnp.concatenate(bottoms, axis=1)], axis=0
        )
        both = jnp.dot(own[f], right, preferred_element_type=jnp.float32)
        row = pl.multiple_of(f * pitch, 8)
        for half in range(2):
            products[half, pl.ds(row, width), :] = both[:, half * lanes : (half + 1) * lanes]
        return carry

    lax.fori_loop(0, bins, one_bin, 0, unroll=8)

    lane = lax.broadcasted_iota(jnp.int32, (offsets, 2 * lanes), 1)
    k = lax.broadcasted_iota(jnp.int32, (offsets, 2 * lanes), 0)
    partner = lane % width + jnp.where(lane >= lanes, width, 0)
    is_real = lane % lanes < width
    far = 4 * lanes
    shift_re = jnp.where(is_real, partner - k, far)
    shift_im = jnp.where(is_real, far, partner - k)
    row_k = lax.broadcasted_iota(jnp.int32, (offsets, F), 0) + first_offset

    def copies(block):
        columns = pl.ds(pl.multiple_of(block * CHANNEL_BLOCK, CHANNEL_BLOCK), CHANNEL_BLOCK)
        return [
            pltpu.make_async_copy(
                out.at[part].reshape(offsets, pitch, F).at[:, columns, :],
                out_hbm.at[:, columns, pl.ds(part * F, F)],
                sems.at[block, part],
            )
            for part in range(2)
        ]

    def one_block(block, carry):
        for il in range(CHANNEL_BLOCK):
            i = block * CHANNEL_BLOCK + il
            at = i + first_offset % width
            pick = jnp.concatenate(
                [
                    jnp.where(shift_re == at, 1.0, 0.0),
                    jnp.where(shift_im == at, -1.0, 0.0),
                ],
                axis=0,
            ).astype(jnp.bfloat16)
            x = jnp.concatenate(
                [products[half, pl.ds(i, F, stride=pitch), :] for half in range(2)], axis=1
            ).astype(jnp.bfloat16)
            y = lax.dot_general(
                pick, x, (((1,), (1,)), ((), ())), preferred_element_type=jnp.float32
            )
            inside = jnp.where(row_k < reach_ref[i], scale, 0.0)
            for part in range(2):
                out[part, pl.ds(i, offsets, stride=pitch), :] = (
                    y[part * offsets : (part + 1) * offsets] * inside
                )
        for copy in copies(block):
            copy.start()
        return carry

    blocks = width // CHANNEL_BLOCK
    lax.fori_loop(0, blocks, one_block, 0)

    def finish(block, carry):
        for copy in copies(block):
            copy.wait()
        return carry

    lax.fori_loop(0, blocks, finish, 0)


def stacked(own, buffers, groups, codes_of, reach, offsets, windows):
    bins, width, _ = own.shape
    chunk_windows, lanes = buffers[0].shape[-2:]
    pitch = width + PITCH_PAD
    return pl.pallas_call(
        functools.partial(stack_kernel, 1.0 / math.sqrt(windows), groups, codes_of),
        out_shape=jax.ShapeDtypeStruct((offsets, width, 2 * F), jnp.float32),
        in_specs=[SMEM] + [VMEM] * (1 + len(buffers)),
        out_specs=ANY,
        scratch_shapes=[
            pltpu.VMEM((2, len(groups), bins, chunk_windows, lanes), jnp.bfloat16),
            pltpu.VMEM((2, bins * pitch, lanes), jnp.float32),
            pltpu.VMEM((2, offsets * pitch, F), jnp.float32),
            pltpu.SemaphoreType.DMA((width // CHANNEL_BLOCK, 2)),
        ],
        compiler_params=pltpu.CompilerParams(vmem_limit_bytes=28 * MIB),
        cost_estimate=SMALL,
        name="stack",
    )(reach, own, *buffers)


def send(array, pairs):
    return lax.ppermute(array, AXES, pairs)


def pairs_of(n_win, n_chan, target):
    pairs = []
    for z in range(n_win):
        for c in range(n_chan):
            to = target(z, c)
            if to is not None:
                pairs.append((c * n_win + z, to * n_win + z))
    return pairs


def after(array, *others):
    return lax.optimization_barrier((array, *others))[0]


def direct_partners(pieces, hops, n_win, n_chan):
    buffers = []
    for piece in pieces:
        buffers.append(send(piece, pairs_of(n_win, n_chan, lambda z, c: (c - hops[z]) % n_chan)))
        buffers.append(
            send(piece, pairs_of(n_win, n_chan, lambda z, c: (c - hops[z] - 1) % n_chan))
        )
    groups = [[(2 * n, None), (2 * n + 1, None)] for n in range(len(pieces))]
    return own_rows(pieces), buffers, groups, lambda: (0, 1, 0, 1)


def square_codes():
    z, c = lax.axis_index("win"), lax.axis_index("chan")
    core, x = c & 1, (c >> 1) & 1
    onward = jnp.where((z == 0) | (x == 0) | ((z < 3) & (core == 1)), 1, 0)
    odd_next = jnp.where(x == 0, 1, 2)
    even_next = jnp.where(z == 0, odd_next, 2)
    next_code = jnp.where(core == 0, even_next, jnp.where(z == 3, 2, odd_next))
    outgoing = jnp.where(core == 0, jnp.where(z < 2, next_code, 1), jnp.where(z < 2, 0, next_code))
    first = jnp.where(z == 0, 0, jnp.where(z == 2, next_code, 3))
    second = jnp.where(z == 1, next_code, jnp.where(z == 3, 1, 3))
    is_late = (z == 3) & (core == 0)
    outgoing_late = jnp.where(is_late, 3, outgoing)
    second_last = jnp.where(is_late, 4, second)
    return onward, outgoing, outgoing_late, (first, second, first, second_last)


def square_partners(pieces, n_win, n_chan):
    def pairs(target):
        return pairs_of(n_win, n_chan, lambda z, c: target(z, c, c % 2, c // 2 % 2))

    def first_target(z, c, core, x):
        if z == 3:
            return c ^ 4
        if z == 0:
            return c ^ 2 if core == 0 else None
        if core == 1:
            return c ^ 2
        return c ^ 4 if z == 2 or x == 0 else None

    def second_target(z, c, core, x):
        if z == 3:
            return c ^ 2 if core == 1 else None
        if z == 0:
            return c ^ 4 if core == 0 and x == 1 else None
        if core == 0:
            return c ^ 2
        return c ^ 4 if x == 1 else None

    def swap(code_of, groups):
        return send(choose(code_of, groups), pairs(lambda z, c, core, x: c ^ 1))

    count = len(pieces)
    half = count // 2
    firsts, seconds = [], []

    def second_move(slot, arrived, *others):
        relay = choose(lambda: square_codes()[0], [(pieces[slot], arrived)])[0]
        relay = after(relay, *others)
        seconds.append(send(relay, pairs(second_target)))
        return relay

    for slot, piece in enumerate(pieces):
        last = slot == count - 1

        firsts.append(
            send(
                piece,
                pairs(
                    lambda z, c, core, x: (
                        None if last and z == 3 and core == 0 else first_target(z, c, core, x)
                    )
                ),
            )
        )
        if slot:
            second_move(slot - 1, after(firsts[slot - 1], pieces[slot]), *seconds[-1:])
    held = list(zip(pieces, firsts, seconds))
    own = own_rows(pieces)
    held[0] = (*held[0][:2], after(held[0][2], firsts[-1]))
    swapped_early = swap(lambda: square_codes()[1], held[:half])
    relay = second_move(count - 1, after(firsts[-1], own))
    held.append((pieces[-1], firsts[-1], seconds[-1]))
    late = send(
        after(pieces[-1], relay),
        pairs(lambda z, c, core, x: c ^ 4 if z == 3 and core == 0 else None),
    )
    late_groups = [(*group, group[1]) for group in held[half:-1]] + [(*held[-1], late)]
    swapped_late = swap(lambda: square_codes()[2], late_groups)
    buffers = [buffer for group in held for buffer in group] + [swapped_early, swapped_late, late]
    groups = []
    for n in range(count):
        swapped = (3 * count, n) if n < half else (3 * count + 1, n - half)
        groups.append([(3 * n, None), (3 * n + 1, None), (3 * n + 2, None), swapped])
    groups[-1].append((3 * count + 2, None))
    return own, buffers, groups, lambda: square_codes()[3]


def on_device(traces, valid, reach):
    width = traces.shape[1]
    n_win, n_chan = lax.axis_size("win"), lax.axis_size("chan")
    offsets = BAND // n_win
    hops = [z * offsets // width for z in range(n_win)]
    pieces = [whitened_chunk(traces, valid)]
    while len(pieces) < n_win:
        ring = [(z, (z + 1) % n_win) for z in range(n_win)]
        pieces.append(lax.ppermute(pieces[-1], "win", ring))
    if n_chan == 8 and hops == list(range(4)):
        own, buffers, groups, codes_of = square_partners(pieces, n_win, n_chan)
    else:
        own, buffers, groups, codes_of = direct_partners(pieces, hops, n_win, n_chan)
    return stacked(own, buffers, groups, codes_of, reach, offsets, traces.shape[0] * n_win)


def solution(mesh):
    in_specs = (P("win", "chan", None), P("win", "chan"), P("chan"))
    out_specs = P("win", "chan", None)
    return jax.shard_map(
        on_device, mesh=mesh, in_specs=in_specs, out_specs=out_specs, check_vma=False
    )
```

```python
import functools
import math

import jax
import jax.numpy as jnp
import numpy as np
from jax import lax
from jax.experimental import pallas as pl
from jax.experimental.pallas import tpu as pltpu
from jax.sharding import PartitionSpec as P

F = 128
FIRST = 16
BAND = 256
AXES = ("chan", "win")
CHANNEL_BLOCK = 8
WHITEN_BLOCKS = 4
PITCH_PAD = 8
MIB = 1024 * 1024
VMEM = pl.BlockSpec(memory_space=pltpu.VMEM)
FEW_MIB = pltpu.CompilerParams(vmem_limit_bytes=4 * MIB)
WHOLE_VMEM = pltpu.CompilerParams(vmem_limit_bytes=62 * MIB)
SMEM = pl.BlockSpec(memory_space=pltpu.SMEM)
SMALL = pl.CostEstimate(flops=1, bytes_accessed=1, transcendentals=0)
ANY = pl.BlockSpec(memory_space=pl.ANY)


def make_table(samples):
    t_int = np.arange(samples, dtype=np.int64)
    j_int = np.arange(F, dtype=np.int64) + FIRST
    angle = 2.0 * np.pi / samples * (j_int[:, None] * t_int[None, :] % samples)
    hann = 0.5 - 0.5 * np.cos(2.0 * np.pi / samples * t_int)
    rows = np.concatenate([hann * np.cos(angle), -hann * np.sin(angle)], axis=0)
    return jnp.asarray(rows.astype(np.float32)).astype(jnp.bfloat16)


def whiten_kernel(table_hbm, traces_hbm, valid_hbm, out_ref, table, traces, valid, rows, sems):
    windows, width, samples = traces.shape
    block = windows // WHITEN_BLOCKS if windows % (2 * WHITEN_BLOCKS) == 0 else windows
    copies = [
        pltpu.make_async_copy(table_hbm, table, sems.at[0]),
        pltpu.make_async_copy(valid_hbm, valid, sems.at[1]),
    ]
    for n in range(windows // block):
        part = pl.ds(n * block, block)
        copies.append(
            pltpu.make_async_copy(traces_hbm.at[part], traces.at[part], sems.at[2 + n])
        )
    for copy in copies:
        copy.start()
    copies[0].wait()
    copies[1].wait()
    for w in range(0, windows, 2):
        if w % block == 0:
            copies[2 + w // block].wait()
        spectra = lax.dot_general(
            table[...],
            traces[w : w + 2].reshape(2 * width, samples),
            (((1,), (1,)), ((), ())),
            preferred_element_type=jnp.float32,
        )
        re, im = spectra[:F], spectra[F:]
        power = re * re + im * im
        level = jnp.sqrt(jnp.mean(power, axis=0, keepdims=True) + 1e-06)
        usable = jnp.concatenate([valid[w : w + 1, :], valid[w + 1 : w + 2, :]], axis=1)
        factor = usable.astype(jnp.float32) / (jnp.sqrt(power) + 0.1 * level)
        re, im = re * factor, im * factor
        for k in range(2):
            half = slice(k * width, (k + 1) * width)
            rows[pl.ds(w + k, F, stride=windows), :] = jnp.concatenate(
                [re[:, half], im[:, half]], axis=1
            )
    out_ref[...] = rows[...].reshape(out_ref.shape).astype(jnp.bfloat16)


def whitened_chunk(traces, valid):
    windows, width, samples = traces.shape
    return pl.pallas_call(
        whiten_kernel,
        out_shape=jax.ShapeDtypeStruct((F, windows, 2 * width), jnp.bfloat16),
        in_specs=[ANY] * 3,
        out_specs=VMEM,
        scratch_shapes=[
            pltpu.VMEM((2 * F, samples), jnp.bfloat16),
            pltpu.VMEM(traces.shape, traces.dtype),
            pltpu.VMEM(valid.shape, valid.dtype),
            pltpu.VMEM((F * windows, 2 * width), jnp.float32),
            pltpu.SemaphoreType.DMA((2 + WHITEN_BLOCKS,)),
        ],
        compiler_params=WHOLE_VMEM,
        cost_estimate=pl.CostEstimate(
            flops=4 * F * traces.size, bytes_accessed=2 * traces.size, transcendentals=0
        ),
        name="whiten",
    )(make_table(samples), traces, valid)


def copy_chosen(code, refs, put):
    for index, ref in enumerate(refs):

        @pl.when(code == index)
        def _(ref=ref):
            put(ref)


def choose_kernel(code_of, groups, *refs):
    out_ref = refs[-1]
    per_group = (len(refs) - 1) // groups
    codes = code_of()
    for g in range(groups):

        def put(ref, g=g):
            out_ref[g] = ref[...]

        copy_chosen(codes[g], refs[g * per_group : (g + 1) * per_group], put)


def choose(code_of, groups):
    operands = [buffer for group in groups for buffer in group]
    return pl.pallas_call(
        functools.partial(choose_kernel, code_of, len(groups)),
        out_shape=jax.ShapeDtypeStruct((len(groups), *groups[0][0].shape), jnp.bfloat16),
        in_specs=[VMEM] * len(operands),
        out_specs=VMEM,
        compiler_params=FEW_MIB,
        cost_estimate=SMALL,
        name="choose",
    )(*operands)


def own_kernel(*refs):
    out_ref = refs[-1]
    width = out_ref.shape[1]

    def one_bin(f, carry):
        turned = jnp.concatenate([ref[f] for ref in refs[:-1]], axis=0).T
        out_ref[f] = jnp.concatenate([turned[:width], turned[width:]], axis=1)
        return carry

    lax.fori_loop(0, out_ref.shape[0], one_bin, 0, unroll=8)


def own_rows(pieces):
    bins, windows, lanes = pieces[0].shape
    return pl.pallas_call(
        own_kernel,
        out_shape=jax.ShapeDtypeStruct(
            (bins, lanes // 2, 2 * windows * len(pieces)), jnp.bfloat16
        ),
        in_specs=[VMEM] * len(pieces),
        out_specs=VMEM,
        compiler_params=FEW_MIB,
        cost_estimate=SMALL,
        name="own_rows",
    )(*pieces)


def stack_kernel(scale, groups, codes_of, reach_ref, own, *refs):
    buffers, (out_hbm, partners, products, out, sems) = refs[:-5], refs[-5:]
    bins, width, _ = own.shape
    lanes = 2 * width
    offsets = out_hbm.shape[0]
    pitch = products.shape[1] // bins
    slots = len(groups)
    first_offset = lax.axis_index("win") * offsets
    codes = codes_of()
    for slot, group in enumerate(groups):
        for which in range(2):
            candidates = [
                buffers[number] if index is None else buffers[number].at[index]
                for number, index in group
            ]

            def put(ref, slot=slot, which=which):
                partners[which, slot] = ref[...]

            copy_chosen(codes[which if slot < slots - 1 else 2 + which], candidates, put)

    def one_bin(f, carry):
        tops = [
            jnp.concatenate([partners[which, slot, f] for slot in range(slots)], axis=0)
            for which in range(2)
        ]
        bottoms = [jnp.concatenate([b[:, width:], -b[:, :width]], axis=1) for b in tops]
        right = jnp.concatenate(
            [jnp.concatenate(tops, axis=1), jnp.concatenate(bottoms, axis=1)], axis=0
        )
        both = jnp.dot(own[f], right, preferred_element_type=jnp.float32)
        row = pl.multiple_of(f * pitch, 8)
        for half in range(2):
            products[half, pl.ds(row, width), :] = both[:, half * lanes : (half + 1) * lanes]
        return carry

    lax.fori_loop(0, bins, one_bin, 0, unroll=8)

    lane = lax.broadcasted_iota(jnp.int32, (offsets, 2 * lanes), 1)
    k = lax.broadcasted_iota(jnp.int32, (offsets, 2 * lanes), 0)
    partner = lane % width + jnp.where(lane >= lanes, width, 0)
    is_real = lane % lanes < width
    far = 4 * lanes
    shift_re = jnp.where(is_real, partner - k, far)
    shift_im = jnp.where(is_real, far, partner - k)
    row_k = lax.broadcasted_iota(jnp.int32, (offsets, F), 0) + first_offset

    def copies(block):
        columns = pl.ds(pl.multiple_of(block * CHANNEL_BLOCK, CHANNEL_BLOCK), CHANNEL_BLOCK)
        return [
            pltpu.make_async_copy(
                out.at[part].reshape(offsets, pitch, F).at[:, columns, :],
                out_hbm.at[:, columns, pl.ds(part * F, F)],
                sems.at[block, part],
            )
            for part in range(2)
        ]

    def one_block(block, carry):
        for il in range(CHANNEL_BLOCK):
            i = block * CHANNEL_BLOCK + il
            at = i + first_offset % width
            pick = jnp.concatenate(
                [
                    jnp.where(shift_re == at, 1.0, 0.0),
                    jnp.where(shift_im == at, -1.0, 0.0),
                ],
                axis=0,
            ).astype(jnp.bfloat16)
            x = jnp.concatenate(
                [products[half, pl.ds(i, F, stride=pitch), :] for half in range(2)], axis=1
            ).astype(jnp.bfloat16)
            y = lax.dot_general(
                pick, x, (((1,), (1,)), ((), ())), preferred_element_type=jnp.float32
            )
            inside = jnp.where(row_k < reach_ref[i], scale, 0.0)
            for part in range(2):
                out[part, pl.ds(i, offsets, stride=pitch), :] = (
                    y[part * offsets : (part + 1) * offsets] * inside
                )
        for copy in copies(block):
            copy.start()
        return carry

    blocks = width // CHANNEL_BLOCK
    lax.fori_loop(0, blocks, one_block, 0)

    def finish(block, carry):
        for copy in copies(block):
            copy.wait()
        return carry

    lax.fori_loop(0, blocks, finish, 0)


def stacked(own, buffers, groups, codes_of, reach, offsets, windows):
    bins, width, _ = own.shape
    chunk_windows, lanes = buffers[0].shape[-2:]
    pitch = width + PITCH_PAD
    return pl.pallas_call(
        functools.partial(stack_kernel, 1.0 / math.sqrt(windows), groups, codes_of),
        out_shape=jax.ShapeDtypeStruct((offsets, width, 2 * F), jnp.float32),
        in_specs=[SMEM] + [VMEM] * (1 + len(buffers)),
        out_specs=ANY,
        scratch_shapes=[
            pltpu.VMEM((2, len(groups), bins, chunk_windows, lanes), jnp.bfloat16),
            pltpu.VMEM((2, bins * pitch, lanes), jnp.float32),
            pltpu.VMEM((2, offsets * pitch, F), jnp.float32),
            pltpu.SemaphoreType.DMA((width // CHANNEL_BLOCK, 2)),
        ],
        compiler_params=pltpu.CompilerParams(vmem_limit_bytes=28 * MIB),
        cost_estimate=SMALL,
        name="stack",
    )(reach, own, *buffers)


def send(array, pairs):
    return lax.ppermute(array, AXES, pairs)


def pairs_of(n_win, n_chan, target):
    pairs = []
    for z in range(n_win):
        for c in range(n_chan):
            to = target(z, c)
            if to is not None:
                pairs.append((c * n_win + z, to * n_win + z))
    return pairs


def after(array, *others):
    return lax.optimization_barrier((array, *others))[0]


def direct_partners(pieces, hops, n_win, n_chan):
    buffers = []
    for piece in pieces:
        buffers.append(send(piece, pairs_of(n_win, n_chan, lambda z, c: (c - hops[z]) % n_chan)))
        buffers.append(
            send(piece, pairs_of(n_win, n_chan, lambda z, c: (c - hops[z] - 1) % n_chan))
        )
    groups = [[(2 * n, None), (2 * n + 1, None)] for n in range(len(pieces))]
    return own_rows(pieces), buffers, groups, lambda: (0, 1, 0, 1)


def square_codes(last):
    z, c = lax.axis_index("win"), lax.axis_index("chan")
    core, x = c & 1, (c >> 1) & 1
    if last:
        onward = jnp.where((z == 0) | (x == 0) | ((z < 3) & (core == 1)), 1, 0)
        odd_next = jnp.where(x == 0, 1, 2)
        even_next = jnp.where(z == 0, odd_next, 2)
        next_code = jnp.where(core == 0, even_next, jnp.where(z == 3, 2, odd_next))
        is_late = (z == 3) & (core == 0)
    else:
        onward = jnp.where(x == 0, 1, 0)
        next_code = jnp.int32(2)
        is_late = jnp.bool_(False)
    outgoing = jnp.where(
        core == 0,
        jnp.where(z < 2, next_code, jnp.where(is_late, 3, 1)),
        jnp.where(z < 2, 0, next_code),
    )
    first = jnp.where(z == 0, 0, jnp.where(z == 2, next_code, 3))
    second = jnp.where(z == 1, next_code, jnp.where(z == 3, jnp.where(is_late, 4, 1), 3))
    return onward, outgoing, first, second


def square_partners(pieces, n_win, n_chan):
    def pairs(target):
        return pairs_of(n_win, n_chan, lambda z, c: target(z, c, c % 2, c // 2 % 2))

    def crosses(z, core):
        return core == 0 if z == 0 else core == 1 if z == 3 else True

    def first_target(z, c, core, x):
        needed = z == 3 or (z == 2 and core == 0) or (x == 0 and crosses(z, core))
        return c ^ 4 if needed else None

    def second_target(z, c, core, x):
        return c ^ 2 if crosses(z, core) else None

    def first_target_last(z, c, core, x):
        if z == 3:
            return c ^ 4 if core == 1 else None
        if z == 0:
            return c ^ 2 if core == 0 else None
        if core == 1:
            return c ^ 2
        return c ^ 4 if z == 2 or x == 0 else None

    def second_target_last(z, c, core, x):
        if z == 3:
            return c ^ 2 if core == 1 else None
        if z == 0:
            return c ^ 4 if core == 0 and x == 1 else None
        if core == 0:
            return c ^ 2
        return c ^ 4 if x == 1 else None

    def swap(code_of, groups):
        return send(choose(code_of, groups), pairs(lambda z, c, core, x: c ^ 1))

    count = len(pieces)
    half = count // 2
    firsts, seconds = [], []

    def second_move(slot, arrived, *others):
        last = slot == count - 1
        relay = choose(lambda: (square_codes(last)[0],), [(pieces[slot], arrived)])[0]
        target = second_target_last if last else second_target
        seconds.append(send(after(relay, *others), pairs(target)))
        return relay

    for slot, piece in enumerate(pieces):
        target = first_target_last if slot == count - 1 else first_target
        firsts.append(send(piece, pairs(target)))
        if slot:
            second_move(slot - 1, after(firsts[slot - 1], piece), *seconds[-1:])
    held = list(zip(pieces, firsts, seconds))
    own = own_rows(pieces)
    held[0] = (*held[0][:2], after(held[0][2], firsts[-1]))
    swapped_early = swap(lambda: (square_codes(False)[1],) * half, held[:half])
    relay = second_move(count - 1, after(firsts[-1], own))
    held.append((pieces[-1], firsts[-1], seconds[-1]))
    late = send(
        after(pieces[-1], relay),
        pairs(lambda z, c, core, x: c ^ 4 if z == 3 and core == 0 else None),
    )

    def late_codes():
        plain = square_codes(False)[1]
        return (plain,) * (count - half - 1) + (square_codes(True)[1],)

    late_groups = [(*group, group[1]) for group in held[half:-1]] + [(*held[-1], late)]
    swapped_late = swap(late_codes, late_groups)
    buffers = [buffer for group in held for buffer in group] + [swapped_early, swapped_late, late]
    groups = []
    for n in range(count):
        swapped = (3 * count, n) if n < half else (3 * count + 1, n - half)
        groups.append([(3 * n, None), (3 * n + 1, None), (3 * n + 2, None), swapped])
    groups[-1].append((3 * count + 2, None))
    return own, buffers, groups, lambda: square_codes(False)[2:] + square_codes(True)[2:]


def on_device(traces, valid, reach):
    width = traces.shape[1]
    n_win, n_chan = lax.axis_size("win"), lax.axis_size("chan")
    offsets = BAND // n_win
    hops = [z * offsets // width for z in range(n_win)]
    pieces = [whitened_chunk(traces, valid)]
    while len(pieces) < n_win:
        ring = [(z, (z + 1) % n_win) for z in range(n_win)]
        pieces.append(lax.ppermute(pieces[-1], "win", ring))
    if n_chan == 8 and hops == list(range(4)):
        own, buffers, groups, codes_of = square_partners(pieces, n_win, n_chan)
    else:
        own, buffers, groups, codes_of = direct_partners(pieces, hops, n_win, n_chan)
    return stacked(own, buffers, groups, codes_of, reach, offsets, traces.shape[0] * n_win)


def solution(mesh):
    in_specs = (P("win", "chan", None), P("win", "chan"), P("chan"))
    out_specs = P("win", "chan", None)
    return jax.shard_map(
        on_device, mesh=mesh, in_specs=in_specs, out_specs=out_specs, check_vma=False
    )
```

```python
import functools
import math

import jax
import jax.numpy as jnp
import numpy as np
from jax import lax
from jax.experimental import pallas as pl
from jax.experimental.pallas import tpu as pltpu
from jax.sharding import PartitionSpec as P

F = 128
FIRST = 16
BAND = 256
AXES = ("chan", "win")
CHANNEL_BLOCK = 8
WHITEN_BLOCKS = 4
PITCH_PAD = 8
MIB = 1024 * 1024
VMEM = pl.BlockSpec(memory_space=pltpu.VMEM)
FEW_MIB = pltpu.CompilerParams(vmem_limit_bytes=4 * MIB)
WHOLE_VMEM = pltpu.CompilerParams(vmem_limit_bytes=62 * MIB)
SMEM = pl.BlockSpec(memory_space=pltpu.SMEM)
SMALL = pl.CostEstimate(flops=1, bytes_accessed=1, transcendentals=0)
ANY = pl.BlockSpec(memory_space=pl.ANY)


def make_table(samples):
    t_int = np.arange(samples, dtype=np.int64)
    j_int = np.arange(F, dtype=np.int64) + FIRST
    angle = 2.0 * np.pi / samples * (j_int[:, None] * t_int[None, :] % samples)
    hann = 0.5 - 0.5 * np.cos(2.0 * np.pi / samples * t_int)
    rows = np.concatenate([hann * np.cos(angle), -hann * np.sin(angle)], axis=0)
    return jnp.asarray(rows.astype(np.float32)).astype(jnp.bfloat16)


def whiten_kernel(table_hbm, traces_hbm, valid_hbm, out_ref, table, traces, valid, rows, sems):
    windows, width, samples = traces.shape
    block = windows // WHITEN_BLOCKS if windows % (2 * WHITEN_BLOCKS) == 0 else windows
    copies = [
        pltpu.make_async_copy(table_hbm, table, sems.at[0]),
        pltpu.make_async_copy(valid_hbm, valid, sems.at[1]),
    ]
    for n in range(windows // block):
        part = pl.ds(n * block, block)
        copies.append(
            pltpu.make_async_copy(traces_hbm.at[part], traces.at[part], sems.at[2 + n])
        )
    for copy in copies:
        copy.start()
    copies[0].wait()
    copies[1].wait()
    for w in range(0, windows, 2):
        if w % block == 0:
            copies[2 + w // block].wait()
        spectra = lax.dot_general(
            table[...],
            traces[w : w + 2].reshape(2 * width, samples),
            (((1,), (1,)), ((), ())),
            preferred_element_type=jnp.float32,
        )
        re, im = spectra[:F], spectra[F:]
        power = re * re + im * im
        level = jnp.sqrt(jnp.mean(power, axis=0, keepdims=True) + 1e-06)
        usable = jnp.concatenate([valid[w : w + 1, :], valid[w + 1 : w + 2, :]], axis=1)
        factor = usable.astype(jnp.float32) / (jnp.sqrt(power) + 0.1 * level)
        re, im = re * factor, im * factor
        for k in range(2):
            half = slice(k * width, (k + 1) * width)
            rows[pl.ds(w + k, F, stride=windows), :] = jnp.concatenate(
                [re[:, half], im[:, half]], axis=1
            )
    out_ref[...] = rows[...].reshape(out_ref.shape).astype(jnp.bfloat16)


def whitened_chunk(traces, valid):
    windows, width, samples = traces.shape
    return pl.pallas_call(
        whiten_kernel,
        out_shape=jax.ShapeDtypeStruct((F, windows, 2 * width), jnp.bfloat16),
        in_specs=[ANY] * 3,
        out_specs=VMEM,
        scratch_shapes=[
            pltpu.VMEM((2 * F, samples), jnp.bfloat16),
            pltpu.VMEM(traces.shape, traces.dtype),
            pltpu.VMEM(valid.shape, valid.dtype),
            pltpu.VMEM((F * windows, 2 * width), jnp.float32),
            pltpu.SemaphoreType.DMA((2 + WHITEN_BLOCKS,)),
        ],
        compiler_params=WHOLE_VMEM,
        cost_estimate=pl.CostEstimate(
            flops=4 * F * traces.size, bytes_accessed=2 * traces.size, transcendentals=0
        ),
        name="whiten",
    )(make_table(samples), traces, valid)


def copy_chosen(code, refs, put):
    for index, ref in enumerate(refs):

        @pl.when(code == index)
        def _(ref=ref):
            put(ref)


def choose_kernel(code_of, groups, *refs):
    out_ref = refs[-1]
    per_group = (len(refs) - 1) // groups
    codes = code_of()
    for g in range(groups):

        def put(ref, g=g):
            out_ref[g] = ref[...]

        copy_chosen(codes[g], refs[g * per_group : (g + 1) * per_group], put)


def choose(code_of, groups):
    operands = [buffer for group in groups for buffer in group]
    return pl.pallas_call(
        functools.partial(choose_kernel, code_of, len(groups)),
        out_shape=jax.ShapeDtypeStruct((len(groups), *groups[0][0].shape), jnp.bfloat16),
        in_specs=[VMEM] * len(operands),
        out_specs=VMEM,
        compiler_params=FEW_MIB,
        cost_estimate=SMALL,
        name="choose",
    )(*operands)


def own_kernel(*refs):
    out_ref = refs[-1]
    width = out_ref.shape[1]

    def one_bin(f, carry):
        turned = jnp.concatenate([ref[f] for ref in refs[:-1]], axis=0).T
        out_ref[f] = jnp.concatenate([turned[:width], turned[width:]], axis=1)
        return carry

    lax.fori_loop(0, out_ref.shape[0], one_bin, 0, unroll=8)


def own_rows(pieces):
    bins, windows, lanes = pieces[0].shape
    return pl.pallas_call(
        own_kernel,
        out_shape=jax.ShapeDtypeStruct(
            (bins, lanes // 2, 2 * windows * len(pieces)), jnp.bfloat16
        ),
        in_specs=[VMEM] * len(pieces),
        out_specs=VMEM,
        compiler_params=FEW_MIB,
        cost_estimate=SMALL,
        name="own_rows",
    )(*pieces)


def stack_kernel(scale, groups, codes_of, reach_ref, own, *refs):
    buffers, (out_hbm, partners, products, out, sems) = refs[:-5], refs[-5:]
    bins, width, _ = own.shape
    lanes = 2 * width
    offsets = out_hbm.shape[0]
    pitch = products.shape[1] // bins
    slots = len(groups)
    first_offset = lax.axis_index("win") * offsets
    codes = codes_of()
    for slot, group in enumerate(groups):
        for which in range(2):
            candidates = [
                buffers[number] if index is None else buffers[number].at[index]
                for number, index in group
            ]

            def put(ref, slot=slot, which=which):
                partners[which, slot] = ref[...]

            copy_chosen(codes[which if slot < slots - 1 else 2 + which], candidates, put)

    def one_bin(f, carry):
        tops = [
            jnp.concatenate([partners[which, slot, f] for slot in range(slots)], axis=0)
            for which in range(2)
        ]
        bottoms = [jnp.concatenate([b[:, width:], -b[:, :width]], axis=1) for b in tops]
        right = jnp.concatenate(
            [jnp.concatenate(tops, axis=1), jnp.concatenate(bottoms, axis=1)], axis=0
        )
        both = jnp.dot(own[f], right, preferred_element_type=jnp.float32)
        row = pl.multiple_of(f * pitch, 8)
        for half in range(2):
            products[half, pl.ds(row, width), :] = both[:, half * lanes : (half + 1) * lanes]
        return carry

    lax.fori_loop(0, bins, one_bin, 0, unroll=8)

    lane = lax.broadcasted_iota(jnp.int32, (offsets, 2 * lanes), 1)
    k = lax.broadcasted_iota(jnp.int32, (offsets, 2 * lanes), 0)
    partner = lane % width + jnp.where(lane >= lanes, width, 0)
    is_real = lane % lanes < width
    far = 4 * lanes
    shift_re = jnp.where(is_real, partner - k, far)
    shift_im = jnp.where(is_real, far, partner - k)
    row_k = lax.broadcasted_iota(jnp.int32, (offsets, F), 0) + first_offset

    def copies(block):
        columns = pl.ds(pl.multiple_of(block * CHANNEL_BLOCK, CHANNEL_BLOCK), CHANNEL_BLOCK)
        return [
            pltpu.make_async_copy(
                out.at[part].reshape(offsets, pitch, F).at[:, columns, :],
                out_hbm.at[:, columns, pl.ds(part * F, F)],
                sems.at[block, part],
            )
            for part in range(2)
        ]

    def one_block(block, carry):
        for il in range(CHANNEL_BLOCK):
            i = block * CHANNEL_BLOCK + il
            at = i + first_offset % width
            pick = jnp.concatenate(
                [
                    jnp.where(shift_re == at, 1.0, 0.0),
                    jnp.where(shift_im == at, -1.0, 0.0),
                ],
                axis=0,
            ).astype(jnp.bfloat16)
            x = jnp.concatenate(
                [products[half, pl.ds(i, F, stride=pitch), :] for half in range(2)], axis=1
            ).astype(jnp.bfloat16)
            y = lax.dot_general(
                pick, x, (((1,), (1,)), ((), ())), preferred_element_type=jnp.float32
            )
            inside = jnp.where(row_k < reach_ref[i], scale, 0.0)
            for part in range(2):
                out[part, pl.ds(i, offsets, stride=pitch), :] = (
                    y[part * offsets : (part + 1) * offsets] * inside
                )
        for copy in copies(block):
            copy.start()
        return carry

    blocks = width // CHANNEL_BLOCK
    lax.fori_loop(0, blocks, one_block, 0)

    def finish(block, carry):
        for copy in copies(block):
            copy.wait()
        return carry

    lax.fori_loop(0, blocks, finish, 0)


def stacked(own, buffers, groups, codes_of, reach, offsets, windows):
    bins, width, _ = own.shape
    chunk_windows, lanes = buffers[0].shape[-2:]
    pitch = width + PITCH_PAD
    return pl.pallas_call(
        functools.partial(stack_kernel, 1.0 / math.sqrt(windows), groups, codes_of),
        out_shape=jax.ShapeDtypeStruct((offsets, width, 2 * F), jnp.float32),
        in_specs=[SMEM] + [VMEM] * (1 + len(buffers)),
        out_specs=ANY,
        scratch_shapes=[
            pltpu.VMEM((2, len(groups), bins, chunk_windows, lanes), jnp.bfloat16),
            pltpu.VMEM((2, bins * pitch, lanes), jnp.float32),
            pltpu.VMEM((2, offsets * pitch, F), jnp.float32),
            pltpu.SemaphoreType.DMA((width // CHANNEL_BLOCK, 2)),
        ],
        compiler_params=pltpu.CompilerParams(vmem_limit_bytes=28 * MIB),
        cost_estimate=SMALL,
        name="stack",
    )(reach, own, *buffers)


def send(array, pairs):
    return lax.ppermute(array, AXES, pairs)


def pairs_of(n_win, n_chan, target):
    pairs = []
    for z in range(n_win):
        for c in range(n_chan):
            to = target(z, c)
            if to is not None:
                pairs.append((c * n_win + z, to * n_win + z))
    return pairs


def after(array, *others):
    return lax.optimization_barrier((array, *others))[0]


def direct_partners(piece, hops, n_win, n_chan):
    pieces = [piece]
    while len(pieces) < n_win:
        ring = [(z, (z + 1) % n_win) for z in range(n_win)]
        pieces.append(lax.ppermute(pieces[-1], "win", ring))
    buffers = []
    for piece in pieces:
        buffers.append(send(piece, pairs_of(n_win, n_chan, lambda z, c: (c - hops[z]) % n_chan)))
        buffers.append(
            send(piece, pairs_of(n_win, n_chan, lambda z, c: (c - hops[z] - 1) % n_chan))
        )
    groups = [[(2 * n, None), (2 * n + 1, None)] for n in range(len(pieces))]
    return own_rows(pieces), buffers, groups, lambda: (0, 1, 0, 1)


def square_codes():
    z, c = lax.axis_index("win"), lax.axis_index("chan")
    core, x = c & 1, (c >> 1) & 1
    onward = jnp.where((z == 0) | (x == 0) | ((z < 3) & (core == 1)), 1, 0)
    odd_next = jnp.where(x == 0, 1, 2)
    even_next = jnp.where(z == 0, odd_next, 2)
    next_code = jnp.where(core == 0, even_next, jnp.where(z == 3, 2, odd_next))
    across = jnp.where((z == 3) & (core == 0), 3, 1)
    outgoing = jnp.where(
        core == 0, jnp.where(z < 2, next_code, across), jnp.where(z < 2, 0, next_code)
    )
    first = jnp.where(z == 0, 0, jnp.where(z == 2, next_code, 4))
    second = jnp.where(z == 1, next_code, jnp.where(z == 3, across, 4))
    return onward, outgoing, first, second


def square_partners(piece_zero, n_win, n_chan):
    def pairs(target):
        return pairs_of(n_win, n_chan, lambda z, c: target(z, c, c % 2, c // 2 % 2))

    def first_target(z, c, core, x):
        if z == 3:
            return c ^ 4 if core == 1 else None
        if z == 0:
            return c ^ 2 if core == 0 else None
        if core == 1:
            return c ^ 2
        return c ^ 4 if z == 2 or x == 0 else None

    def second_target(z, c, core, x):
        if z == 3:
            return c ^ 2 if core == 1 else None
        if z == 0:
            return c ^ 4 if core == 0 and x == 1 else None
        if core == 0:
            return c ^ 2
        return c ^ 4 if x == 1 else None

    def late_target(z, c, core, x):
        return c ^ 4 if z == 3 and core == 0 else None

    def swap(code_of, groups):
        return send(choose(code_of, groups), pairs(lambda z, c, core, x: c ^ 1))

    count = n_win
    half = count // 2
    pieces = []
    held, relays = [], []
    piece = piece_zero
    for slot in range(count):
        last = slot == count - 1
        if slot:
            piece = lax.ppermute(piece, "win", [(z, (z + 1) % n_win) for z in range(n_win)])
        pieces.append(piece)
        moved = send(after(piece, *[]), pairs(first_target))
        arrived = after(moved, *(held[-1][2:] if held else []))
        if last:
            own = own_rows(pieces)
            held[0] = (*held[0][:2], after(held[0][2], moved), held[0][3])
            swapped_early = swap(lambda: square_codes()[1:2] * half, held[:half])
            arrived = after(arrived, own)
        relay = choose(lambda: square_codes()[:1], [(piece, arrived)])[0]
        relays.append(relay)
        relayed = send(after(relay, *(held[-1][2:] if held else [])), pairs(second_target))
        late = send(after(piece, relay), pairs(late_target))
        held.append((piece, moved, relayed, late))
    swapped_late = swap(lambda: square_codes()[1:2] * (count - half), held[half:])
    buffers = [buffer for group in held for buffer in group] + [swapped_early, swapped_late]
    groups = []
    for n in range(count):
        swapped = (4 * count, n) if n < half else (4 * count + 1, n - half)
        groups.append([*((4 * n + k, None) for k in range(4)), swapped])
    return own, buffers, groups, lambda: square_codes()[2:] * 2


def on_device(traces, valid, reach):
    width = traces.shape[1]
    n_win, n_chan = lax.axis_size("win"), lax.axis_size("chan")
    offsets = BAND // n_win
    hops = [z * offsets // width for z in range(n_win)]
    piece = whitened_chunk(traces, valid)
    if n_chan == 8 and hops == list(range(4)):
        own, buffers, groups, codes_of = square_partners(piece, n_win, n_chan)
    else:
        own, buffers, groups, codes_of = direct_partners(piece, hops, n_win, n_chan)
    return stacked(own, buffers, groups, codes_of, reach, offsets, traces.shape[0] * n_win)


def solution(mesh):
    in_specs = (P("win", "chan", None), P("win", "chan"), P("chan"))
    out_specs = P("win", "chan", None)
    return jax.shard_map(
        on_device, mesh=mesh, in_specs=in_specs, out_specs=out_specs, check_vma=False
    )
```

```python
import functools
import math

import jax
import jax.numpy as jnp
import numpy as np
from jax import lax
from jax.experimental import pallas as pl
from jax.experimental.pallas import tpu as pltpu
from jax.sharding import PartitionSpec as P

F = 128
FIRST = 16
BAND = 256
AXES = ("chan", "win")
CHANNEL_BLOCK = 8
WHITEN_BLOCKS = 4
PITCH_PAD = 8
MIB = 1024 * 1024
VMEM = pl.BlockSpec(memory_space=pltpu.VMEM)
FEW_MIB = pltpu.CompilerParams(vmem_limit_bytes=4 * MIB)
WHOLE_VMEM = pltpu.CompilerParams(vmem_limit_bytes=62 * MIB)
SMEM = pl.BlockSpec(memory_space=pltpu.SMEM)
SMALL = pl.CostEstimate(flops=1, bytes_accessed=1, transcendentals=0)
ANY = pl.BlockSpec(memory_space=pl.ANY)


def make_table(samples):
    t_int = np.arange(samples, dtype=np.int64)
    j_int = np.arange(F, dtype=np.int64) + FIRST
    angle = 2.0 * np.pi / samples * (j_int[:, None] * t_int[None, :] % samples)
    hann = 0.5 - 0.5 * np.cos(2.0 * np.pi / samples * t_int)
    rows = np.concatenate([hann * np.cos(angle), -hann * np.sin(angle)], axis=0)
    return jnp.asarray(rows.astype(np.float32)).astype(jnp.bfloat16)


def whiten_kernel(table_hbm, traces_hbm, valid_hbm, out_ref, table, traces, valid, rows, sems):
    windows, width, samples = traces.shape
    block = windows // WHITEN_BLOCKS if windows % (2 * WHITEN_BLOCKS) == 0 else windows
    copies = [
        pltpu.make_async_copy(table_hbm, table, sems.at[0]),
        pltpu.make_async_copy(valid_hbm, valid, sems.at[1]),
    ]
    for n in range(windows // block):
        part = pl.ds(n * block, block)
        copies.append(
            pltpu.make_async_copy(traces_hbm.at[part], traces.at[part], sems.at[2 + n])
        )
    for copy in copies:
        copy.start()
    copies[0].wait()
    copies[1].wait()
    for w in range(0, windows, 2):
        if w % block == 0:
            copies[2 + w // block].wait()
        spectra = lax.dot_general(
            table[...],
            traces[w : w + 2].reshape(2 * width, samples),
            (((1,), (1,)), ((), ())),
            preferred_element_type=jnp.float32,
        )
        re, im = spectra[:F], spectra[F:]
        power = re * re + im * im
        level = jnp.sqrt(jnp.mean(power, axis=0, keepdims=True) + 1e-06)
        usable = jnp.concatenate([valid[w : w + 1, :], valid[w + 1 : w + 2, :]], axis=1)
        factor = usable.astype(jnp.float32) / (jnp.sqrt(power) + 0.1 * level)
        re, im = re * factor, im * factor
        for k in range(2):
            half = slice(k * width, (k + 1) * width)
            rows[pl.ds(w + k, F, stride=windows), :] = jnp.concatenate(
                [re[:, half], im[:, half]], axis=1
            )
    out_ref[...] = rows[...].reshape(out_ref.shape).astype(jnp.bfloat16)


def whitened_chunk(traces, valid):
    windows, width, samples = traces.shape
    return pl.pallas_call(
        whiten_kernel,
        out_shape=jax.ShapeDtypeStruct((F, windows, 2 * width), jnp.bfloat16),
        in_specs=[ANY] * 3,
        out_specs=VMEM,
        scratch_shapes=[
            pltpu.VMEM((2 * F, samples), jnp.bfloat16),
            pltpu.VMEM(traces.shape, traces.dtype),
            pltpu.VMEM(valid.shape, valid.dtype),
            pltpu.VMEM((F * windows, 2 * width), jnp.float32),
            pltpu.SemaphoreType.DMA((2 + WHITEN_BLOCKS,)),
        ],
        compiler_params=WHOLE_VMEM,
        cost_estimate=pl.CostEstimate(
            flops=4 * F * traces.size, bytes_accessed=2 * traces.size, transcendentals=0
        ),
        name="whiten",
    )(make_table(samples), traces, valid)


def copy_chosen(code, refs, put):
    for index, ref in enumerate(refs):

        @pl.when(code == index)
        def _(ref=ref):
            put(ref)


def choose_kernel(code_of, groups, *refs):
    out_ref = refs[-1]
    per_group = (len(refs) - 1) // groups
    code = code_of()
    for g in range(groups):

        def put(ref, g=g):
            out_ref[g] = ref[...]

        copy_chosen(code, refs[g * per_group : (g + 1) * per_group], put)


def choose(code_of, groups):
    operands = [buffer for group in groups for buffer in group]
    return pl.pallas_call(
        functools.partial(choose_kernel, code_of, len(groups)),
        out_shape=jax.ShapeDtypeStruct((len(groups), *groups[0][0].shape), jnp.bfloat16),
        in_specs=[VMEM] * len(operands),
        out_specs=VMEM,
        compiler_params=FEW_MIB,
        cost_estimate=SMALL,
        name="choose",
    )(*operands)


def own_kernel(*refs):
    out_ref = refs[-1]
    width = out_ref.shape[1]

    def one_bin(f, carry):
        turned = jnp.concatenate([ref[f] for ref in refs[:-1]], axis=0).T
        out_ref[f] = jnp.concatenate([turned[:width], turned[width:]], axis=1)
        return carry

    lax.fori_loop(0, out_ref.shape[0], one_bin, 0, unroll=8)


def own_rows(pieces):
    bins, windows, lanes = pieces[0].shape
    return pl.pallas_call(
        own_kernel,
        out_shape=jax.ShapeDtypeStruct(
            (bins, lanes // 2, 2 * windows * len(pieces)), jnp.bfloat16
        ),
        in_specs=[VMEM] * len(pieces),
        out_specs=VMEM,
        compiler_params=FEW_MIB,
        cost_estimate=SMALL,
        name="own_rows",
    )(*pieces)


def stack_kernel(scale, groups, codes_of, reach_ref, own, *refs):
    buffers, (out_hbm, partners, products, out, sems) = refs[:-5], refs[-5:]
    bins, width, _ = own.shape
    lanes = 2 * width
    offsets = out_hbm.shape[0]
    pitch = products.shape[0] // bins
    slots = len(groups)
    first_offset = lax.axis_index("win") * offsets
    codes = codes_of()
    for slot, group in enumerate(groups):
        for which in range(2):
            candidates = [
                buffers[number] if index is None else buffers[number].at[index]
                for number, index in group
            ]

            def put(ref, slot=slot, which=which):
                partners[which, slot] = ref[...]

            copy_chosen(codes[which if slot < slots - 1 else 2 + which], candidates, put)

    first = first_offset % width
    lane = lax.broadcasted_iota(jnp.int32, (width, lanes), 1)
    in_first = lane % width >= lax.broadcasted_iota(jnp.int32, (width, lanes), 0) + first

    def one_bin(f, carry):
        tops = [
            jnp.concatenate([partners[which, slot, f] for slot in range(slots)], axis=0)
            for which in range(2)
        ]
        bottoms = [jnp.concatenate([b[:, width:], -b[:, :width]], axis=1) for b in tops]
        right = jnp.concatenate(
            [jnp.concatenate(tops, axis=1), jnp.concatenate(bottoms, axis=1)], axis=0
        )
        both = jnp.dot(own[f], right, preferred_element_type=jnp.float32)
        row = pl.multiple_of(f * pitch, 8)
        products[pl.ds(row, width), :] = jnp.where(in_first, both[:, :lanes], both[:, lanes:])
        return carry

    lax.fori_loop(0, bins, one_bin, 0, unroll=8)

    lane = lax.broadcasted_iota(jnp.int32, (offsets, lanes), 1)
    shift = (lane + offsets * width - lax.broadcasted_iota(jnp.int32, (offsets, lanes), 0)) % width
    shift_re = jnp.where(lane < width, shift, width)
    shift_im = jnp.where(lane < width, width, shift)
    row_k = lax.broadcasted_iota(jnp.int32, (offsets, F), 0) + first_offset

    def copies(block):
        columns = pl.ds(pl.multiple_of(block * CHANNEL_BLOCK, CHANNEL_BLOCK), CHANNEL_BLOCK)
        return [
            pltpu.make_async_copy(
                out.at[part].reshape(offsets, pitch, F).at[:, columns, :],
                out_hbm.at[:, columns, pl.ds(part * F, F)],
                sems.at[block, part],
            )
            for part in range(2)
        ]

    def one_block(block, carry):
        for il in range(CHANNEL_BLOCK):
            i = block * CHANNEL_BLOCK + il
            at = (i + first) % width
            pick = jnp.concatenate(
                [
                    jnp.where(shift_re == at, 1.0, 0.0),
                    jnp.where(shift_im == at, -1.0, 0.0),
                ],
                axis=0,
            ).astype(jnp.bfloat16)
            x = products[pl.ds(i, F, stride=pitch), :].astype(jnp.bfloat16)
            y = lax.dot_general(
                pick, x, (((1,), (1,)), ((), ())), preferred_element_type=jnp.float32
            )
            inside = jnp.where(row_k < reach_ref[i], scale, 0.0)
            for part in range(2):
                out[part, pl.ds(i, offsets, stride=pitch), :] = (
                    y[part * offsets : (part + 1) * offsets] * inside
                )
        for copy in copies(block):
            copy.start()
        return carry

    blocks = width // CHANNEL_BLOCK
    lax.fori_loop(0, blocks, one_block, 0)

    def finish(block, carry):
        for copy in copies(block):
            copy.wait()
        return carry

    lax.fori_loop(0, blocks, finish, 0)


def stacked(own, buffers, groups, codes_of, reach, offsets, windows):
    bins, width, _ = own.shape
    chunk_windows, lanes = buffers[0].shape[-2:]
    pitch = width + PITCH_PAD
    return pl.pallas_call(
        functools.partial(stack_kernel, 1.0 / math.sqrt(windows), groups, codes_of),
        out_shape=jax.ShapeDtypeStruct((offsets, width, 2 * F), jnp.float32),
        in_specs=[SMEM] + [VMEM] * (1 + len(buffers)),
        out_specs=ANY,
        scratch_shapes=[
            pltpu.VMEM((2, len(groups), bins, chunk_windows, lanes), jnp.bfloat16),
            pltpu.VMEM((bins * pitch, lanes), jnp.float32),
            pltpu.VMEM((2, offsets * pitch, F), jnp.float32),
            pltpu.SemaphoreType.DMA((width // CHANNEL_BLOCK, 2)),
        ],
        compiler_params=pltpu.CompilerParams(vmem_limit_bytes=28 * MIB),
        cost_estimate=SMALL,
        name="stack",
    )(reach, own, *buffers)


def send(array, pairs):
    return lax.ppermute(array, AXES, pairs)


def pairs_of(n_win, n_chan, target):
    pairs = []
    for z in range(n_win):
        for c in range(n_chan):
            to = target(z, c)
            if to is not None:
                pairs.append((c * n_win + z, to * n_win + z))
    return pairs


def after(array, *others):
    return lax.optimization_barrier((array, *others))[0]


def direct_partners(pieces, hops, n_win, n_chan):
    buffers = []
    for piece in pieces:
        buffers.append(send(piece, pairs_of(n_win, n_chan, lambda z, c: (c - hops[z]) % n_chan)))
        buffers.append(
            send(piece, pairs_of(n_win, n_chan, lambda z, c: (c - hops[z] - 1) % n_chan))
        )
    groups = [[(2 * n, None), (2 * n + 1, None)] for n in range(len(pieces))]
    return own_rows(pieces), buffers, groups, lambda: (0, 1, 0, 1)


def square_codes():
    z, c = lax.axis_index("win"), lax.axis_index("chan")
    core, x = c & 1, (c >> 1) & 1
    onward = jnp.where((z == 0) | (x == 0) | ((z < 3) & (core == 1)), 1, 0)
    odd_next = jnp.where(x == 0, 1, 2)
    even_next = jnp.where(z == 0, odd_next, 2)
    next_code = jnp.where(core == 0, even_next, jnp.where(z == 3, 2, odd_next))
    outgoing = jnp.where(core == 0, jnp.where(z < 2, next_code, 1), jnp.where(z < 2, 0, next_code))
    first = jnp.where(z == 0, 0, jnp.where(z == 2, next_code, 3))
    second = jnp.where(z == 1, next_code, jnp.where(z == 3, 1, 3))
    is_late = (z == 3) & (core == 0)
    outgoing_late = jnp.where(is_late, 3, outgoing)
    second_last = jnp.where(is_late, 4, second)
    return onward, outgoing, outgoing_late, (first, second, first, second_last)


def square_partners(pieces, n_win, n_chan):
    def pairs(target):
        return pairs_of(n_win, n_chan, lambda z, c: target(z, c, c % 2, c // 2 % 2))

    def first_target(z, c, core, x):
        if z == 3:
            return c ^ 4
        if z == 0:
            return c ^ 2 if core == 0 else None
        if core == 1:
            return c ^ 2
        return c ^ 4 if z == 2 or x == 0 else None

    def second_target(z, c, core, x):
        if z == 3:
            return c ^ 2 if core == 1 else None
        if z == 0:
            return c ^ 4 if core == 0 and x == 1 else None
        if core == 0:
            return c ^ 2
        return c ^ 4 if x == 1 else None

    def swap(code_of, groups):
        return send(choose(code_of, groups), pairs(lambda z, c, core, x: c ^ 1))

    count = len(pieces)
    half = count // 2
    firsts, seconds = [], []

    def second_move(slot, arrived):
        relay = choose(lambda: square_codes()[0], [(pieces[slot], arrived)])[0]
        seconds.append(send(relay, pairs(second_target)))
        return relay

    for slot, piece in enumerate(pieces):
        last = slot == count - 1
        if slot >= 2:
            piece = after(piece, firsts[slot - 2])
        firsts.append(
            send(
                piece,
                pairs(
                    lambda z, c, core, x: (
                        None if last and z == 3 and core == 0 else first_target(z, c, core, x)
                    )
                ),
            )
        )
        if slot:
            arrived = firsts[slot - 1]
            arrived = after(arrived, *seconds[-1:])
            second_move(slot - 1, arrived)
    held = list(zip(pieces, firsts, seconds))
    own = own_rows(pieces)
    held[0] = (*held[0][:2], after(held[0][2], firsts[-1]))
    swapped_early = swap(lambda: square_codes()[1], held[:half])
    arrived = after(firsts[-1], own)
    relay = second_move(count - 1, arrived)
    held.append((pieces[-1], firsts[-1], seconds[-1]))
    late = send(
        after(pieces[-1], relay),
        pairs(lambda z, c, core, x: c ^ 4 if z == 3 and core == 0 else None),
    )
    late_groups = [(*group, group[1]) for group in held[half:-1]] + [(*held[-1], late)]
    swapped_late = swap(lambda: square_codes()[2], late_groups)
    buffers = [buffer for group in held for buffer in group] + [swapped_early, swapped_late, late]
    groups = []
    for n in range(count):
        swapped = (3 * count, n) if n < half else (3 * count + 1, n - half)
        groups.append([(3 * n, None), (3 * n + 1, None), (3 * n + 2, None), swapped])
    groups[-1].append((3 * count + 2, None))
    return own, buffers, groups, lambda: square_codes()[3]


def on_device(traces, valid, reach):
    width = traces.shape[1]
    n_win, n_chan = lax.axis_size("win"), lax.axis_size("chan")
    offsets = BAND // n_win
    hops = [z * offsets // width for z in range(n_win)]
    pieces = [whitened_chunk(traces, valid)]
    while len(pieces) < n_win:
        ring = [(z, (z + 1) % n_win) for z in range(n_win)]
        pieces.append(lax.ppermute(pieces[-1], "win", ring))
    if n_chan == 8 and hops == list(range(4)):
        own, buffers, groups, codes_of = square_partners(pieces, n_win, n_chan)
    else:
        own, buffers, groups, codes_of = direct_partners(pieces, hops, n_win, n_chan)
    return stacked(own, buffers, groups, codes_of, reach, offsets, traces.shape[0] * n_win)


def solution(mesh):
    in_specs = (P("win", "chan", None), P("win", "chan"), P("chan"))
    out_specs = P("win", "chan", None)
    return jax.shard_map(
        on_device, mesh=mesh, in_specs=in_specs, out_specs=out_specs, check_vma=False
    )
```

```python
import functools
import math

import jax
import jax.numpy as jnp
import numpy as np
from jax import lax
from jax.experimental import pallas as pl
from jax.experimental.pallas import tpu as pltpu
from jax.sharding import PartitionSpec as P

F = 128
FIRST = 16
BAND = 256
AXES = ("chan", "win")
SUBLANES = 8
BLOCK_TILES = 2
WHITEN_BLOCKS = 4
PITCH_PAD = 8
MIB = 1024 * 1024
VMEM = pl.BlockSpec(memory_space=pltpu.VMEM)
FEW_MIB = pltpu.CompilerParams(vmem_limit_bytes=4 * MIB)
WHOLE_VMEM = pltpu.CompilerParams(vmem_limit_bytes=62 * MIB)
SMEM = pl.BlockSpec(memory_space=pltpu.SMEM)
SMALL = pl.CostEstimate(flops=1, bytes_accessed=1, transcendentals=0)
ANY = pl.BlockSpec(memory_space=pl.ANY)


def make_table(samples):
    t_int = np.arange(samples, dtype=np.int64)
    j_int = np.arange(F, dtype=np.int64) + FIRST
    angle = 2.0 * np.pi / samples * (j_int[:, None] * t_int[None, :] % samples)
    hann = 0.5 - 0.5 * np.cos(2.0 * np.pi / samples * t_int)
    rows = np.concatenate([hann * np.cos(angle), -hann * np.sin(angle)], axis=0)
    return jnp.asarray(rows.astype(np.float32)).astype(jnp.bfloat16)


def whiten_kernel(table_hbm, traces_hbm, valid_hbm, out_ref, table, traces, valid, rows, sems):
    windows, width, samples = traces.shape
    block = windows // WHITEN_BLOCKS if windows % (2 * WHITEN_BLOCKS) == 0 else windows
    copies = [
        pltpu.make_async_copy(table_hbm, table, sems.at[0]),
        pltpu.make_async_copy(valid_hbm, valid, sems.at[1]),
    ]
    for n in range(windows // block):
        part = pl.ds(n * block, block)
        copies.append(
            pltpu.make_async_copy(traces_hbm.at[part], traces.at[part], sems.at[2 + n])
        )
    for copy in copies:
        copy.start()
    copies[0].wait()
    copies[1].wait()
    for w in range(0, windows, 2):
        if w % block == 0:
            copies[2 + w // block].wait()
        spectra = lax.dot_general(
            table[...],
            traces[w : w + 2].reshape(2 * width, samples),
            (((1,), (1,)), ((), ())),
            preferred_element_type=jnp.float32,
        )
        re, im = spectra[:F], spectra[F:]
        power = re * re + im * im
        level = jnp.sqrt(jnp.mean(power, axis=0, keepdims=True) + 1e-06)
        usable = jnp.concatenate([valid[w : w + 1, :], valid[w + 1 : w + 2, :]], axis=1)
        factor = usable.astype(jnp.float32) / (jnp.sqrt(power) + 0.1 * level)
        re, im = re * factor, im * factor
        for k in range(2):
            half = slice(k * width, (k + 1) * width)
            rows[pl.ds(w + k, F, stride=windows), :] = jnp.concatenate(
                [re[:, half], im[:, half]], axis=1
            )
    out_ref[...] = rows[...].reshape(out_ref.shape).astype(jnp.bfloat16)


def whitened_chunk(traces, valid):
    windows, width, samples = traces.shape
    return pl.pallas_call(
        whiten_kernel,
        out_shape=jax.ShapeDtypeStruct((F, windows, 2 * width), jnp.bfloat16),
        in_specs=[ANY] * 3,
        out_specs=VMEM,
        scratch_shapes=[
            pltpu.VMEM((2 * F, samples), jnp.bfloat16),
            pltpu.VMEM(traces.shape, traces.dtype),
            pltpu.VMEM(valid.shape, valid.dtype),
            pltpu.VMEM((F * windows, 2 * width), jnp.float32),
            pltpu.SemaphoreType.DMA((2 + WHITEN_BLOCKS,)),
        ],
        compiler_params=WHOLE_VMEM,
        cost_estimate=pl.CostEstimate(
            flops=4 * F * traces.size, bytes_accessed=2 * traces.size, transcendentals=0
        ),
        name="whiten",
    )(make_table(samples), traces, valid)


def copy_chosen(code, refs, put):
    for index, ref in enumerate(refs):

        @pl.when(code == index)
        def _(ref=ref):
            put(ref)


def choose_kernel(code_of, groups, *refs):
    out_ref = refs[-1]
    per_group = (len(refs) - 1) // groups
    code = code_of()
    for g in range(groups):

        def put(ref, g=g):
            out_ref[g] = ref[...]

        copy_chosen(code, refs[g * per_group : (g + 1) * per_group], put)


def choose(code_of, groups):
    operands = [buffer for group in groups for buffer in group]
    return pl.pallas_call(
        functools.partial(choose_kernel, code_of, len(groups)),
        out_shape=jax.ShapeDtypeStruct((len(groups), *groups[0][0].shape), jnp.bfloat16),
        in_specs=[VMEM] * len(operands),
        out_specs=VMEM,
        compiler_params=FEW_MIB,
        cost_estimate=SMALL,
        name="choose",
    )(*operands)


def own_kernel(*refs):
    out_ref = refs[-1]
    width = out_ref.shape[1]

    def one_bin(f, carry):
        turned = jnp.concatenate([ref[f] for ref in refs[:-1]], axis=0).T
        out_ref[f] = jnp.concatenate([turned[:width], turned[width:]], axis=1)
        return carry

    lax.fori_loop(0, out_ref.shape[0], one_bin, 0, unroll=8)


def own_rows(pieces):
    bins, windows, lanes = pieces[0].shape
    return pl.pallas_call(
        own_kernel,
        out_shape=jax.ShapeDtypeStruct(
            (bins, lanes // 2, 2 * windows * len(pieces)), jnp.bfloat16
        ),
        in_specs=[VMEM] * len(pieces),
        out_specs=VMEM,
        compiler_params=FEW_MIB,
        cost_estimate=SMALL,
        name="own_rows",
    )(*pieces)


def stack_kernel(scale, groups, codes_of, reach_ref, own, *refs):
    buffers, (out_hbm, partners, products, out, sems) = refs[:-5], refs[-5:]
    bins, width, _ = own.shape
    lanes = 2 * width
    offsets = out_hbm.shape[0]
    pitch = products.shape[0] // bins
    slots = len(groups)
    first_offset = lax.axis_index("win") * offsets
    codes = codes_of()
    for slot, group in enumerate(groups):
        for which in range(2):
            candidates = [
                buffers[number] if index is None else buffers[number].at[index]
                for number, index in group
            ]

            def put(ref, slot=slot, which=which):
                partners[which, slot] = ref[...]

            copy_chosen(codes[which if slot < slots - 1 else 2 + which], candidates, put)

    first = first_offset % width
    lane = lax.broadcasted_iota(jnp.int32, (width, lanes), 1)
    in_first = lane % width >= lax.broadcasted_iota(jnp.int32, (width, lanes), 0) + first

    def one_bin(f, carry):
        tops = [
            jnp.concatenate([partners[which, slot, f] for slot in range(slots)], axis=0)
            for which in range(2)
        ]
        bottoms = [jnp.concatenate([b[:, width:], -b[:, :width]], axis=1) for b in tops]
        right = jnp.concatenate(
            [jnp.concatenate(tops, axis=1), jnp.concatenate(bottoms, axis=1)], axis=0
        )
        both = jnp.dot(own[f], right, preferred_element_type=jnp.float32)
        row = pl.multiple_of(f * pitch, 8)
        products[pl.ds(row, width), :] = jnp.where(in_first, both[:, :lanes], both[:, lanes:])
        return carry

    lax.fori_loop(0, bins, one_bin, 0, unroll=16)

    lane = lax.broadcasted_iota(jnp.int32, (offsets, lanes), 1)
    shift = (lane + offsets * width - lax.broadcasted_iota(jnp.int32, (offsets, lanes), 0)) % width
    shift_re = jnp.where(lane < width, shift, width)
    shift_im = jnp.where(lane < width, width, shift)
    row_k = lax.broadcasted_iota(jnp.int32, (offsets, F), 0) + first_offset

    tiles = out.shape[1]
    rows = out.reshape(offsets * tiles * 2 * SUBLANES, F)

    def copy(block):
        part = pl.ds(block * BLOCK_TILES, BLOCK_TILES)
        return pltpu.make_async_copy(out.at[:, part], out_hbm.at[:, part], sems.at[block])

    def one_block(block, carry):
        for tile in range(BLOCK_TILES):
            for sublane in range(SUBLANES):
                i = (block * BLOCK_TILES + tile) * SUBLANES + sublane
                at = (i + first) % width
                pick = jnp.concatenate(
                    [
                        jnp.where(shift_re == at, 1.0, 0.0),
                        jnp.where(shift_im == at, -1.0, 0.0),
                    ],
                    axis=0,
                ).astype(jnp.bfloat16)
                x = products[pl.ds(i, F, stride=pitch), :].astype(jnp.bfloat16)
                y = lax.dot_general(
                    pick, x, (((1,), (1,)), ((), ())), preferred_element_type=jnp.float32
                )
                inside = jnp.where(row_k < reach_ref[i], scale, 0.0)
                for part in range(2):
                    row = ((block * BLOCK_TILES + tile) * 2 + part) * SUBLANES + sublane
                    rows[pl.ds(row, offsets, stride=tiles * 2 * SUBLANES), :] = (
                        y[part * offsets : (part + 1) * offsets] * inside
                    )
        copy(block).start()
        return carry

    blocks = tiles // BLOCK_TILES
    lax.fori_loop(0, blocks, one_block, 0)

    def finish(block, carry):
        copy(block).wait()
        return carry

    lax.fori_loop(0, blocks, finish, 0)


def stacked(own, buffers, groups, codes_of, reach, offsets, windows):
    bins, width, _ = own.shape
    chunk_windows, lanes = buffers[0].shape[-2:]
    pitch = width + PITCH_PAD
    tiles = width // SUBLANES
    out = (offsets, tiles, 2, SUBLANES, F)
    result = pl.pallas_call(
        functools.partial(stack_kernel, 1.0 / math.sqrt(windows), groups, codes_of),
        out_shape=jax.ShapeDtypeStruct(out, jnp.float32),
        in_specs=[SMEM] + [VMEM] * (1 + len(buffers)),
        out_specs=ANY,
        scratch_shapes=[
            pltpu.VMEM((2, len(groups), bins, chunk_windows, lanes), jnp.bfloat16),
            pltpu.VMEM((bins * pitch, lanes), jnp.float32),
            pltpu.VMEM(out, jnp.float32),
            pltpu.SemaphoreType.DMA((tiles // BLOCK_TILES,)),
        ],
        compiler_params=pltpu.CompilerParams(vmem_limit_bytes=28 * MIB),
        cost_estimate=SMALL,
        name="stack",
    )(reach, own, *buffers)
    return result.transpose(0, 1, 3, 2, 4).reshape(offsets, width, 2 * F)


def send(array, pairs):
    return lax.ppermute(array, AXES, pairs)


def pairs_of(n_win, n_chan, target):
    pairs = []
    for z in range(n_win):
        for c in range(n_chan):
            to = target(z, c)
            if to is not None:
                pairs.append((c * n_win + z, to * n_win + z))
    return pairs


def after(array, *others):
    return lax.optimization_barrier((array, *others))[0]


def direct_partners(pieces, hops, n_win, n_chan):
    buffers = []
    for piece in pieces:
        buffers.append(send(piece, pairs_of(n_win, n_chan, lambda z, c: (c - hops[z]) % n_chan)))
        buffers.append(
            send(piece, pairs_of(n_win, n_chan, lambda z, c: (c - hops[z] - 1) % n_chan))
        )
    groups = [[(2 * n, None), (2 * n + 1, None)] for n in range(len(pieces))]
    return own_rows(pieces), buffers, groups, lambda: (0, 1, 0, 1)


def square_codes():
    z, c = lax.axis_index("win"), lax.axis_index("chan")
    core, x = c & 1, (c >> 1) & 1
    onward = jnp.where((z == 0) | (x == 0) | ((z < 3) & (core == 1)), 1, 0)
    odd_next = jnp.where(x == 0, 1, 2)
    even_next = jnp.where(z == 0, odd_next, 2)
    next_code = jnp.where(core == 0, even_next, jnp.where(z == 3, 2, odd_next))
    outgoing = jnp.where(core == 0, jnp.where(z < 2, next_code, 1), jnp.where(z < 2, 0, next_code))
    first = jnp.where(z == 0, 0, jnp.where(z == 2, next_code, 3))
    second = jnp.where(z == 1, next_code, jnp.where(z == 3, 1, 3))
    is_late = (z == 3) & (core == 0)
    outgoing_late = jnp.where(is_late, 3, outgoing)
    second_last = jnp.where(is_late, 4, second)
    return onward, outgoing, outgoing_late, (first, second, first, second_last)


def square_partners(pieces, n_win, n_chan):
    def pairs(target):
        return pairs_of(n_win, n_chan, lambda z, c: target(z, c, c % 2, c // 2 % 2))

    def first_target(z, c, core, x):
        if z == 3:
            return c ^ 4
        if z == 0:
            return c ^ 2 if core == 0 else None
        if core == 1:
            return c ^ 2
        return c ^ 4 if z == 2 or x == 0 else None

    def second_target(z, c, core, x):
        if z == 3:
            return c ^ 2 if core == 1 else None
        if z == 0:
            return c ^ 4 if core == 0 and x == 1 else None
        if core == 0:
            return c ^ 2
        return c ^ 4 if x == 1 else None

    def swap(code_of, groups):
        return send(choose(code_of, groups), pairs(lambda z, c, core, x: c ^ 1))

    count = len(pieces)
    half = count // 2
    firsts, seconds = [], []

    def second_move(slot, arrived):
        relay = choose(lambda: square_codes()[0], [(pieces[slot], arrived)])[0]
        seconds.append(send(relay, pairs(second_target)))
        return relay

    for slot, piece in enumerate(pieces):
        last = slot == count - 1
        if slot >= 2:
            piece = after(piece, firsts[slot - 2])
        firsts.append(
            send(
                piece,
                pairs(
                    lambda z, c, core, x: (
                        None if last and z == 3 and core == 0 else first_target(z, c, core, x)
                    )
                ),
            )
        )
        if slot:
            arrived = firsts[slot - 1]
            arrived = after(arrived, *seconds[-1:])
            second_move(slot - 1, arrived)
    held = list(zip(pieces, firsts, seconds))
    own = own_rows(pieces)
    held[0] = (*held[0][:2], after(held[0][2], firsts[-1]))
    swapped_early = swap(lambda: square_codes()[1], held[:half])
    arrived = after(firsts[-1], own)
    relay = second_move(count - 1, arrived)
    held.append((pieces[-1], firsts[-1], seconds[-1]))
    late = send(
        after(pieces[-1], relay),
        pairs(lambda z, c, core, x: c ^ 4 if z == 3 and core == 0 else None),
    )
    late_groups = [(*group, group[1]) for group in held[half:-1]] + [(*held[-1], late)]
    swapped_late = swap(lambda: square_codes()[2], late_groups)
    buffers = [buffer for group in held for buffer in group] + [swapped_early, swapped_late, late]
    groups = []
    for n in range(count):
        swapped = (3 * count, n) if n < half else (3 * count + 1, n - half)
        groups.append([(3 * n, None), (3 * n + 1, None), (3 * n + 2, None), swapped])
    groups[-1].append((3 * count + 2, None))
    return own, buffers, groups, lambda: square_codes()[3]


def on_device(traces, valid, reach):
    width = traces.shape[1]
    n_win, n_chan = lax.axis_size("win"), lax.axis_size("chan")
    offsets = BAND // n_win
    hops = [z * offsets // width for z in range(n_win)]
    pieces = [whitened_chunk(traces, valid)]
    while len(pieces) < n_win:
        ring = [(z, (z + 1) % n_win) for z in range(n_win)]
        pieces.append(lax.ppermute(pieces[-1], "win", ring))
    if n_chan == 8 and hops == list(range(4)):
        own, buffers, groups, codes_of = square_partners(pieces, n_win, n_chan)
    else:
        own, buffers, groups, codes_of = direct_partners(pieces, hops, n_win, n_chan)
    return stacked(own, buffers, groups, codes_of, reach, offsets, traces.shape[0] * n_win)


def solution(mesh):
    in_specs = (P("win", "chan", None), P("win", "chan"), P("chan"))
    out_specs = P("win", "chan", None)
    return jax.shard_map(
        on_device, mesh=mesh, in_specs=in_specs, out_specs=out_specs, check_vma=False
    )
```

```python
import functools
import math

import jax
import jax.numpy as jnp
import numpy as np
from jax import lax
from jax.experimental import pallas as pl
from jax.experimental.pallas import tpu as pltpu
from jax.sharding import PartitionSpec as P

F = 128
FIRST = 16
BAND = 256
AXES = ("chan", "win")
CHANNEL_BLOCK = 8
GROUP = 4
WHITEN_BLOCKS = 4
PITCH_PAD = 8
MIB = 1024 * 1024
VMEM = pl.BlockSpec(memory_space=pltpu.VMEM)
FEW_MIB = pltpu.CompilerParams(vmem_limit_bytes=4 * MIB)
WHOLE_VMEM = pltpu.CompilerParams(vmem_limit_bytes=62 * MIB)
SMEM = pl.BlockSpec(memory_space=pltpu.SMEM)
SMALL = pl.CostEstimate(flops=1, bytes_accessed=1, transcendentals=0)
ANY = pl.BlockSpec(memory_space=pl.ANY)


def make_table(samples):
    t_int = np.arange(samples, dtype=np.int64)
    j_int = np.arange(F, dtype=np.int64) + FIRST
    angle = 2.0 * np.pi / samples * (j_int[:, None] * t_int[None, :] % samples)
    hann = 0.5 - 0.5 * np.cos(2.0 * np.pi / samples * t_int)
    rows = np.concatenate([hann * np.cos(angle), -hann * np.sin(angle)], axis=0)
    return jnp.asarray(rows.astype(np.float32)).astype(jnp.bfloat16)


def whiten_kernel(table_hbm, traces_hbm, valid_hbm, out_ref, table, traces, valid, rows, sems):
    windows, width, samples = traces.shape
    block = windows // WHITEN_BLOCKS if windows % (2 * WHITEN_BLOCKS) == 0 else windows
    copies = [
        pltpu.make_async_copy(table_hbm, table, sems.at[0]),
        pltpu.make_async_copy(valid_hbm, valid, sems.at[1]),
    ]
    for n in range(windows // block):
        part = pl.ds(n * block, block)
        copies.append(
            pltpu.make_async_copy(traces_hbm.at[part], traces.at[part], sems.at[2 + n])
        )
    for copy in copies:
        copy.start()
    copies[0].wait()
    copies[1].wait()
    for w in range(0, windows, 2):
        if w % block == 0:
            copies[2 + w // block].wait()
        spectra = lax.dot_general(
            table[...],
            traces[w : w + 2].reshape(2 * width, samples),
            (((1,), (1,)), ((), ())),
            preferred_element_type=jnp.float32,
        )
        re, im = spectra[:F], spectra[F:]
        power = re * re + im * im
        level = jnp.sqrt(jnp.mean(power, axis=0, keepdims=True) + 1e-06)
        usable = jnp.concatenate([valid[w : w + 1, :], valid[w + 1 : w + 2, :]], axis=1)
        factor = usable.astype(jnp.float32) / (jnp.sqrt(power) + 0.1 * level)
        re, im = re * factor, im * factor
        for k in range(2):
            half = slice(k * width, (k + 1) * width)
            rows[pl.ds(w + k, F, stride=windows), :] = jnp.concatenate(
                [re[:, half], im[:, half]], axis=1
            )
    out_ref[...] = rows[...].reshape(out_ref.shape).astype(jnp.bfloat16)


def whitened_chunk(traces, valid):
    windows, width, samples = traces.shape
    return pl.pallas_call(
        whiten_kernel,
        out_shape=jax.ShapeDtypeStruct((F, windows, 2 * width), jnp.bfloat16),
        in_specs=[ANY] * 3,
        out_specs=VMEM,
        scratch_shapes=[
            pltpu.VMEM((2 * F, samples), jnp.bfloat16),
            pltpu.VMEM(traces.shape, traces.dtype),
            pltpu.VMEM(valid.shape, valid.dtype),
            pltpu.VMEM((F * windows, 2 * width), jnp.float32),
            pltpu.SemaphoreType.DMA((2 + WHITEN_BLOCKS,)),
        ],
        compiler_params=WHOLE_VMEM,
        cost_estimate=pl.CostEstimate(
            flops=4 * F * traces.size, bytes_accessed=2 * traces.size, transcendentals=0
        ),
        name="whiten",
    )(make_table(samples), traces, valid)


def copy_chosen(code, refs, put):
    for index, ref in enumerate(refs):

        @pl.when(code == index)
        def _(ref=ref):
            put(ref)


def choose_kernel(code_of, groups, *refs):
    out_ref = refs[-1]
    per_group = (len(refs) - 1) // groups
    code = code_of()
    for g in range(groups):

        def put(ref, g=g):
            out_ref[g] = ref[...]

        copy_chosen(code, refs[g * per_group : (g + 1) * per_group], put)


def choose(code_of, groups):
    operands = [buffer for group in groups for buffer in group]
    return pl.pallas_call(
        functools.partial(choose_kernel, code_of, len(groups)),
        out_shape=jax.ShapeDtypeStruct((len(groups), *groups[0][0].shape), jnp.bfloat16),
        in_specs=[VMEM] * len(operands),
        out_specs=VMEM,
        compiler_params=FEW_MIB,
        cost_estimate=SMALL,
        name="choose",
    )(*operands)


def own_kernel(*refs):
    out_ref = refs[-1]
    width = out_ref.shape[1]

    def one_bin(f, carry):
        turned = jnp.concatenate([ref[f] for ref in refs[:-1]], axis=0).T
        out_ref[f] = jnp.concatenate([turned[:width], turned[width:]], axis=1)
        return carry

    lax.fori_loop(0, out_ref.shape[0], one_bin, 0, unroll=8)


def own_rows(pieces):
    bins, windows, lanes = pieces[0].shape
    return pl.pallas_call(
        own_kernel,
        out_shape=jax.ShapeDtypeStruct(
            (bins, lanes // 2, 2 * windows * len(pieces)), jnp.bfloat16
        ),
        in_specs=[VMEM] * len(pieces),
        out_specs=VMEM,
        compiler_params=FEW_MIB,
        cost_estimate=SMALL,
        name="own_rows",
    )(*pieces)


def stack_kernel(scale, groups, codes_of, reach_ref, own, *refs):
    buffers, (out_hbm, partners, products, out, sems) = refs[:-5], refs[-5:]
    bins, width, _ = own.shape
    lanes = 2 * width
    offsets = out_hbm.shape[0]
    pitch = products.shape[0] // bins
    slots = len(groups)
    first_offset = lax.axis_index("win") * offsets
    codes = codes_of()
    for slot, group in enumerate(groups):
        for which in range(2):
            candidates = [
                buffers[number] if index is None else buffers[number].at[index]
                for number, index in group
            ]

            def put(ref, slot=slot, which=which):
                partners[which, slot] = ref[...]

            copy_chosen(codes[which if slot < slots - 1 else 2 + which], candidates, put)

    first = first_offset % width
    lane = lax.broadcasted_iota(jnp.int32, (width, lanes), 1)
    in_first = lane % width >= lax.broadcasted_iota(jnp.int32, (width, lanes), 0) + first

    def products_of(f):
        tops = [
            jnp.concatenate([partners[which, slot, f] for slot in range(slots)], axis=0)
            for which in range(2)
        ]
        bottoms = [jnp.concatenate([b[:, width:], -b[:, :width]], axis=1) for b in tops]
        right = jnp.concatenate(
            [jnp.concatenate(tops, axis=1), jnp.concatenate(bottoms, axis=1)], axis=0
        )
        both = jnp.dot(own[f], right, preferred_element_type=jnp.float32)
        return jnp.where(in_first, both[:, :lanes], both[:, lanes:])

    def one_group(group, carry):
        results = [products_of(group * GROUP + n) for n in range(GROUP)]
        for n, result in enumerate(results):
            row = pl.multiple_of((group * GROUP + n) * pitch, 8)
            products[pl.ds(row, width), :] = result
        return carry

    lax.fori_loop(0, bins // GROUP, one_group, 0, unroll=2)

    lane = lax.broadcasted_iota(jnp.int32, (offsets, lanes), 1)
    shift = (lane + offsets * width - lax.broadcasted_iota(jnp.int32, (offsets, lanes), 0)) % width
    shift_re = jnp.where(lane < width, shift, width)
    shift_im = jnp.where(lane < width, width, shift)
    row_k = lax.broadcasted_iota(jnp.int32, (offsets, F), 0) + first_offset

    def copies(block):
        columns = pl.ds(pl.multiple_of(block * CHANNEL_BLOCK, CHANNEL_BLOCK), CHANNEL_BLOCK)
        return [
            pltpu.make_async_copy(
                out.at[part].reshape(offsets, pitch, F).at[:, columns, :],
                out_hbm.at[:, columns, pl.ds(part * F, F)],
                sems.at[block, part],
            )
            for part in range(2)
        ]

    def picked(i):
        at = (i + first) % width
        pick = jnp.concatenate(
            [jnp.where(shift_re == at, 1.0, 0.0), jnp.where(shift_im == at, -1.0, 0.0)], axis=0
        ).astype(jnp.bfloat16)
        x = products[pl.ds(i, F, stride=pitch), :].astype(jnp.bfloat16)
        y = lax.dot_general(
            pick, x, (((1,), (1,)), ((), ())), preferred_element_type=jnp.float32
        )
        inside = jnp.where(row_k < reach_ref[i], scale, 0.0)
        return [y[part * offsets : (part + 1) * offsets] * inside for part in range(2)]

    def one_block(block, carry):
        for begin in range(0, CHANNEL_BLOCK, GROUP):
            channels = [block * CHANNEL_BLOCK + begin + n for n in range(GROUP)]
            results = [picked(i) for i in channels]
            for i, result in zip(channels, results):
                for part in range(2):
                    out[part, pl.ds(i, offsets, stride=pitch), :] = result[part]
        for copy in copies(block):
            copy.start()
        return carry

    blocks = width // CHANNEL_BLOCK
    lax.fori_loop(0, blocks, one_block, 0)

    def finish(block, carry):
        for copy in copies(block):
            copy.wait()
        return carry

    lax.fori_loop(0, blocks, finish, 0)


def stacked(own, buffers, groups, codes_of, reach, offsets, windows):
    bins, width, _ = own.shape
    chunk_windows, lanes = buffers[0].shape[-2:]
    pitch = width + PITCH_PAD
    return pl.pallas_call(
        functools.partial(stack_kernel, 1.0 / math.sqrt(windows), groups, codes_of),
        out_shape=jax.ShapeDtypeStruct((offsets, width, 2 * F), jnp.float32),
        in_specs=[SMEM] + [VMEM] * (1 + len(buffers)),
        out_specs=ANY,
        scratch_shapes=[
            pltpu.VMEM((2, len(groups), bins, chunk_windows, lanes), jnp.bfloat16),
            pltpu.VMEM((bins * pitch, lanes), jnp.float32),
            pltpu.VMEM((2, offsets * pitch, F), jnp.float32),
            pltpu.SemaphoreType.DMA((width // CHANNEL_BLOCK, 2)),
        ],
        compiler_params=pltpu.CompilerParams(vmem_limit_bytes=28 * MIB),
        cost_estimate=SMALL,
        name="stack",
    )(reach, own, *buffers)


def send(array, pairs):
    return lax.ppermute(array, AXES, pairs)


def pairs_of(n_win, n_chan, target):
    pairs = []
    for z in range(n_win):
        for c in range(n_chan):
            to = target(z, c)
            if to is not None:
                pairs.append((c * n_win + z, to * n_win + z))
    return pairs


def after(array, *others):
    return lax.optimization_barrier((array, *others))[0]


def direct_partners(pieces, hops, n_win, n_chan):
    buffers = []
    for piece in pieces:
        buffers.append(send(piece, pairs_of(n_win, n_chan, lambda z, c: (c - hops[z]) % n_chan)))
        buffers.append(
            send(piece, pairs_of(n_win, n_chan, lambda z, c: (c - hops[z] - 1) % n_chan))
        )
    groups = [[(2 * n, None), (2 * n + 1, None)] for n in range(len(pieces))]
    return own_rows(pieces), buffers, groups, lambda: (0, 1, 0, 1)


def square_codes():
    z, c = lax.axis_index("win"), lax.axis_index("chan")
    core, x = c & 1, (c >> 1) & 1
    onward = jnp.where((z == 0) | (x == 0) | ((z < 3) & (core == 1)), 1, 0)
    odd_next = jnp.where(x == 0, 1, 2)
    even_next = jnp.where(z == 0, odd_next, 2)
    next_code = jnp.where(core == 0, even_next, jnp.where(z == 3, 2, odd_next))
    outgoing = jnp.where(core == 0, jnp.where(z < 2, next_code, 1), jnp.where(z < 2, 0, next_code))
    first = jnp.where(z == 0, 0, jnp.where(z == 2, next_code, 3))
    second = jnp.where(z == 1, next_code, jnp.where(z == 3, 1, 3))
    is_late = (z == 3) & (core == 0)
    outgoing_late = jnp.where(is_late, 3, outgoing)
    second_last = jnp.where(is_late, 4, second)
    return onward, outgoing, outgoing_late, (first, second, first, second_last)


def square_partners(pieces, n_win, n_chan):
    def pairs(target):
        return pairs_of(n_win, n_chan, lambda z, c: target(z, c, c % 2, c // 2 % 2))

    def first_target(z, c, core, x):
        if z == 3:
            return c ^ 4
        if z == 0:
            return c ^ 2 if core == 0 else None
        if core == 1:
            return c ^ 2
        return c ^ 4 if z == 2 or x == 0 else None

    def second_target(z, c, core, x):
        if z == 3:
            return c ^ 2 if core == 1 else None
        if z == 0:
            return c ^ 4 if core == 0 and x == 1 else None
        if core == 0:
            return c ^ 2
        return c ^ 4 if x == 1 else None

    def swap(code_of, groups):
        return send(choose(code_of, groups), pairs(lambda z, c, core, x: c ^ 1))

    count = len(pieces)
    half = count // 2
    firsts, seconds = [], []

    def second_move(slot, arrived):
        relay = choose(lambda: square_codes()[0], [(pieces[slot], arrived)])[0]
        seconds.append(send(relay, pairs(second_target)))
        return relay

    for slot, piece in enumerate(pieces):
        last = slot == count - 1
        if slot >= 2:
            piece = after(piece, firsts[slot - 2])
        firsts.append(
            send(
                piece,
                pairs(
                    lambda z, c, core, x: (
                        None if last and z == 3 and core == 0 else first_target(z, c, core, x)
                    )
                ),
            )
        )
        if slot:
            arrived = firsts[slot - 1]
            arrived = after(arrived, *seconds[-1:])
            second_move(slot - 1, arrived)
    held = list(zip(pieces, firsts, seconds))
    own = own_rows(pieces)
    held[0] = (*held[0][:2], after(held[0][2], firsts[-1]))
    swapped_early = swap(lambda: square_codes()[1], held[:half])
    arrived = after(firsts[-1], own)
    relay = second_move(count - 1, arrived)
    held.append((pieces[-1], firsts[-1], seconds[-1]))
    late = send(
        after(pieces[-1], relay),
        pairs(lambda z, c, core, x: c ^ 4 if z == 3 and core == 0 else None),
    )
    late_groups = [(*group, group[1]) for group in held[half:-1]] + [(*held[-1], late)]
    swapped_late = swap(lambda: square_codes()[2], late_groups)
    buffers = [buffer for group in held for buffer in group] + [swapped_early, swapped_late, late]
    groups = []
    for n in range(count):
        swapped = (3 * count, n) if n < half else (3 * count + 1, n - half)
        groups.append([(3 * n, None), (3 * n + 1, None), (3 * n + 2, None), swapped])
    groups[-1].append((3 * count + 2, None))
    return own, buffers, groups, lambda: square_codes()[3]


def on_device(traces, valid, reach):
    width = traces.shape[1]
    n_win, n_chan = lax.axis_size("win"), lax.axis_size("chan")
    offsets = BAND // n_win
    hops = [z * offsets // width for z in range(n_win)]
    pieces = [whitened_chunk(traces, valid)]
    while len(pieces) < n_win:
        ring = [(z, (z + 1) % n_win) for z in range(n_win)]
        pieces.append(lax.ppermute(pieces[-1], "win", ring))
    if n_chan == 8 and hops == list(range(4)):
        own, buffers, groups, codes_of = square_partners(pieces, n_win, n_chan)
    else:
        own, buffers, groups, codes_of = direct_partners(pieces, hops, n_win, n_chan)
    return stacked(own, buffers, groups, codes_of, reach, offsets, traces.shape[0] * n_win)


def solution(mesh):
    in_specs = (P("win", "chan", None), P("win", "chan"), P("chan"))
    out_specs = P("win", "chan", None)
    return jax.shard_map(
        on_device, mesh=mesh, in_specs=in_specs, out_specs=out_specs, check_vma=False
    )
```

```python
import functools
import math

import jax
import jax.numpy as jnp
import numpy as np
from jax import lax
from jax.experimental import pallas as pl
from jax.experimental.pallas import tpu as pltpu
from jax.sharding import PartitionSpec as P

F = 128
FIRST = 16
BAND = 256
AXES = ("chan", "win")
CHANNEL_BLOCK = 8
GROUP = 4
WHITEN_BLOCKS = 4
PITCH_PAD = 8
MIB = 1024 * 1024
VMEM = pl.BlockSpec(memory_space=pltpu.VMEM)
FEW_MIB = pltpu.CompilerParams(vmem_limit_bytes=4 * MIB)
WHOLE_VMEM = pltpu.CompilerParams(vmem_limit_bytes=62 * MIB)
SMEM = pl.BlockSpec(memory_space=pltpu.SMEM)
SMALL = pl.CostEstimate(flops=1, bytes_accessed=1, transcendentals=0)
ANY = pl.BlockSpec(memory_space=pl.ANY)


def make_table(samples):
    t_int = np.arange(samples, dtype=np.int64)
    j_int = np.arange(F, dtype=np.int64) + FIRST
    angle = 2.0 * np.pi / samples * (j_int[:, None] * t_int[None, :] % samples)
    hann = 0.5 - 0.5 * np.cos(2.0 * np.pi / samples * t_int)
    rows = np.concatenate([hann * np.cos(angle), -hann * np.sin(angle)], axis=0)
    return jnp.asarray(rows.astype(np.float32)).astype(jnp.bfloat16)


def whiten_kernel(table_hbm, traces_hbm, valid_hbm, out_ref, table, traces, valid, rows, sems):
    windows, width, samples = traces.shape
    block = windows // WHITEN_BLOCKS if windows % (2 * WHITEN_BLOCKS) == 0 else windows
    copies = [
        pltpu.make_async_copy(table_hbm, table, sems.at[0]),
        pltpu.make_async_copy(valid_hbm, valid, sems.at[1]),
    ]
    for n in range(windows // block):
        part = pl.ds(n * block, block)
        copies.append(
            pltpu.make_async_copy(traces_hbm.at[part], traces.at[part], sems.at[2 + n])
        )
    for copy in copies:
        copy.start()
    copies[0].wait()
    copies[1].wait()
    for w in range(0, windows, 2):
        if w % block == 0:
            copies[2 + w // block].wait()
        spectra = lax.dot_general(
            table[...],
            traces[w : w + 2].reshape(2 * width, samples),
            (((1,), (1,)), ((), ())),
            preferred_element_type=jnp.float32,
        )
        re, im = spectra[:F], spectra[F:]
        power = re * re + im * im
        level = jnp.sqrt(jnp.mean(power, axis=0, keepdims=True) + 1e-06)
        usable = jnp.concatenate([valid[w : w + 1, :], valid[w + 1 : w + 2, :]], axis=1)
        factor = usable.astype(jnp.float32) / (jnp.sqrt(power) + 0.1 * level)
        re, im = re * factor, im * factor
        for k in range(2):
            half = slice(k * width, (k + 1) * width)
            rows[pl.ds(w + k, F, stride=windows), :] = jnp.concatenate(
                [re[:, half], im[:, half]], axis=1
            )
    out_ref[...] = rows[...].reshape(out_ref.shape).astype(jnp.bfloat16)


def whitened_chunk(traces, valid):
    windows, width, samples = traces.shape
    return pl.pallas_call(
        whiten_kernel,
        out_shape=jax.ShapeDtypeStruct((F, windows, 2 * width), jnp.bfloat16),
        in_specs=[ANY] * 3,
        out_specs=VMEM,
        scratch_shapes=[
            pltpu.VMEM((2 * F, samples), jnp.bfloat16),
            pltpu.VMEM(traces.shape, traces.dtype),
            pltpu.VMEM(valid.shape, valid.dtype),
            pltpu.VMEM((F * windows, 2 * width), jnp.float32),
            pltpu.SemaphoreType.DMA((2 + WHITEN_BLOCKS,)),
        ],
        compiler_params=WHOLE_VMEM,
        cost_estimate=pl.CostEstimate(
            flops=4 * F * traces.size, bytes_accessed=2 * traces.size, transcendentals=0
        ),
        name="whiten",
    )(make_table(samples), traces, valid)


def copy_chosen(code, refs, put):
    for index, ref in enumerate(refs):

        @pl.when(code == index)
        def _(ref=ref):
            put(ref)


def choose_kernel(code_of, groups, *refs):
    out_ref = refs[-1]
    per_group = (len(refs) - 1) // groups
    codes = code_of()
    for g in range(groups):

        def put(ref, g=g):
            out_ref[g] = ref[...]

        copy_chosen(codes[g], refs[g * per_group : (g + 1) * per_group], put)


def choose(code_of, groups):
    operands = [buffer for group in groups for buffer in group]
    return pl.pallas_call(
        functools.partial(choose_kernel, code_of, len(groups)),
        out_shape=jax.ShapeDtypeStruct((len(groups), *groups[0][0].shape), jnp.bfloat16),
        in_specs=[VMEM] * len(operands),
        out_specs=VMEM,
        compiler_params=FEW_MIB,
        cost_estimate=SMALL,
        name="choose",
    )(*operands)


def own_kernel(*refs):
    out_ref = refs[-1]
    width = out_ref.shape[1]

    def one_bin(f, carry):
        turned = jnp.concatenate([ref[f] for ref in refs[:-1]], axis=0).T
        out_ref[f] = jnp.concatenate([turned[:width], turned[width:]], axis=1)
        return carry

    lax.fori_loop(0, out_ref.shape[0], one_bin, 0, unroll=8)


def own_rows(pieces):
    bins, windows, lanes = pieces[0].shape
    return pl.pallas_call(
        own_kernel,
        out_shape=jax.ShapeDtypeStruct(
            (bins, lanes // 2, 2 * windows * len(pieces)), jnp.bfloat16
        ),
        in_specs=[VMEM] * len(pieces),
        out_specs=VMEM,
        compiler_params=FEW_MIB,
        cost_estimate=SMALL,
        name="own_rows",
    )(*pieces)


def stack_kernel(scale, groups, codes_of, reach_ref, own, *refs):
    buffers, (out_hbm, partners, products, out, sems) = refs[:-5], refs[-5:]
    bins, width, _ = own.shape
    lanes = 2 * width
    offsets = out_hbm.shape[0]
    pitch = products.shape[0] // bins
    slots = len(groups)
    first_offset = lax.axis_index("win") * offsets
    codes = codes_of()
    for slot, group in enumerate(groups):
        for which in range(2):
            candidates = [
                buffers[number] if index is None else buffers[number].at[index]
                for number, index in group
            ]

            def put(ref, slot=slot, which=which):
                partners[which, slot] = ref[...]

            copy_chosen(codes[which if slot < slots - 1 else 2 + which], candidates, put)

    first = first_offset % width
    lane = lax.broadcasted_iota(jnp.int32, (width, lanes), 1)
    in_first = lane % width >= lax.broadcasted_iota(jnp.int32, (width, lanes), 0) + first

    def products_of(f):
        tops = [
            jnp.concatenate([partners[which, slot, f] for slot in range(slots)], axis=0)
            for which in range(2)
        ]
        bottoms = [jnp.concatenate([b[:, width:], -b[:, :width]], axis=1) for b in tops]
        right = jnp.concatenate(
            [jnp.concatenate(tops, axis=1), jnp.concatenate(bottoms, axis=1)], axis=0
        )
        both = jnp.dot(own[f], right, preferred_element_type=jnp.float32)
        return jnp.where(in_first, both[:, :lanes], both[:, lanes:])

    def one_group(group, carry):
        results = [products_of(group * GROUP + n) for n in range(GROUP)]
        for n, result in enumerate(results):
            row = pl.multiple_of((group * GROUP + n) * pitch, 8)
            products[pl.ds(row, width), :] = result
        return carry

    lax.fori_loop(0, bins // GROUP, one_group, 0, unroll=2)

    lane = lax.broadcasted_iota(jnp.int32, (offsets, lanes), 1)
    shift = (lane + offsets * width - lax.broadcasted_iota(jnp.int32, (offsets, lanes), 0)) % width
    shift_re = jnp.where(lane < width, shift, width)
    shift_im = jnp.where(lane < width, width, shift)
    row_k = lax.broadcasted_iota(jnp.int32, (offsets, F), 0) + first_offset

    def copies(block):
        columns = pl.ds(pl.multiple_of(block * CHANNEL_BLOCK, CHANNEL_BLOCK), CHANNEL_BLOCK)
        return [
            pltpu.make_async_copy(
                out.at[part].reshape(offsets, pitch, F).at[:, columns, :],
                out_hbm.at[:, columns, pl.ds(part * F, F)],
                sems.at[block, part],
            )
            for part in range(2)
        ]

    def picked(i):
        at = (i + first) % width
        pick = jnp.concatenate(
            [jnp.where(shift_re == at, 1.0, 0.0), jnp.where(shift_im == at, -1.0, 0.0)], axis=0
        ).astype(jnp.bfloat16)
        x = products[pl.ds(i, F, stride=pitch), :].astype(jnp.bfloat16)
        y = lax.dot_general(
            pick, x, (((1,), (1,)), ((), ())), preferred_element_type=jnp.float32
        )
        inside = jnp.where(row_k < reach_ref[i], scale, 0.0)
        return [y[part * offsets : (part + 1) * offsets] * inside for part in range(2)]

    def one_block(block, carry):
        for begin in range(0, CHANNEL_BLOCK, GROUP):
            channels = [block * CHANNEL_BLOCK + begin + n for n in range(GROUP)]
            results = [picked(i) for i in channels]
            for i, result in zip(channels, results):
                for part in range(2):
                    out[part, pl.ds(i, offsets, stride=pitch), :] = result[part]
        for copy in copies(block):
            copy.start()
        return carry

    blocks = width // CHANNEL_BLOCK
    lax.fori_loop(0, blocks, one_block, 0)

    def finish(block, carry):
        for copy in copies(block):
            copy.wait()
        return carry

    lax.fori_loop(0, blocks, finish, 0)


def stacked(own, buffers, groups, codes_of, reach, offsets, windows):
    bins, width, _ = own.shape
    chunk_windows, lanes = buffers[0].shape[-2:]
    pitch = width + PITCH_PAD
    return pl.pallas_call(
        functools.partial(stack_kernel, 1.0 / math.sqrt(windows), groups, codes_of),
        out_shape=jax.ShapeDtypeStruct((offsets, width, 2 * F), jnp.float32),
        in_specs=[SMEM] + [VMEM] * (1 + len(buffers)),
        out_specs=ANY,
        scratch_shapes=[
            pltpu.VMEM((2, len(groups), bins, chunk_windows, lanes), jnp.bfloat16),
            pltpu.VMEM((bins * pitch, lanes), jnp.float32),
            pltpu.VMEM((2, offsets * pitch, F), jnp.float32),
            pltpu.SemaphoreType.DMA((width // CHANNEL_BLOCK, 2)),
        ],
        compiler_params=pltpu.CompilerParams(vmem_limit_bytes=28 * MIB),
        cost_estimate=SMALL,
        name="stack",
    )(reach, own, *buffers)


def send(array, pairs):
    return lax.ppermute(array, AXES, pairs)


def pairs_of(n_win, n_chan, target):
    pairs = []
    for z in range(n_win):
        for c in range(n_chan):
            to = target(z, c)
            if to is not None:
                pairs.append((c * n_win + z, to * n_win + z))
    return pairs


def after(array, *others):
    return lax.optimization_barrier((array, *others))[0]


def direct_partners(piece, hops, n_win, n_chan):
    pieces = [piece]
    while len(pieces) < n_win:
        ring = [(z, (z + 1) % n_win) for z in range(n_win)]
        pieces.append(lax.ppermute(pieces[-1], "win", ring))
    buffers = []
    for piece in pieces:
        buffers.append(send(piece, pairs_of(n_win, n_chan, lambda z, c: (c - hops[z]) % n_chan)))
        buffers.append(
            send(piece, pairs_of(n_win, n_chan, lambda z, c: (c - hops[z] - 1) % n_chan))
        )
    groups = [[(2 * n, None), (2 * n + 1, None)] for n in range(len(pieces))]
    return own_rows(pieces), buffers, groups, lambda: (0, 1, 0, 1)


def square_codes():
    z, c = lax.axis_index("win"), lax.axis_index("chan")
    core, x = c & 1, (c >> 1) & 1
    onward = jnp.where((z == 0) | (x == 0) | ((z < 3) & (core == 1)), 1, 0)
    odd_next = jnp.where(x == 0, 1, 2)
    even_next = jnp.where(z == 0, odd_next, 2)
    next_code = jnp.where(core == 0, even_next, jnp.where(z == 3, 2, odd_next))
    across = jnp.where((z == 3) & (core == 0), 3, 1)
    outgoing = jnp.where(
        core == 0, jnp.where(z < 2, next_code, across), jnp.where(z < 2, 0, next_code)
    )
    first = jnp.where(z == 0, 0, jnp.where(z == 2, next_code, 4))
    second = jnp.where(z == 1, next_code, jnp.where(z == 3, across, 4))
    return onward, outgoing, first, second


def square_partners(piece_zero, n_win, n_chan):
    def pairs(target):
        return pairs_of(n_win, n_chan, lambda z, c: target(z, c, c % 2, c // 2 % 2))

    def first_target(z, c, core, x):
        if z == 3:
            return c ^ 4
        if z == 0:
            return c ^ 2 if core == 0 else None
        if core == 1:
            return c ^ 2
        return c ^ 4 if z == 2 or x == 0 else None

    def early_target(z, c, core, x):
        return None if z == 3 and core == 0 else first_target(z, c, core, x)

    def second_target(z, c, core, x):
        if z == 3:
            return c ^ 2 if core == 1 else None
        if z == 0:
            return c ^ 4 if core == 0 and x == 1 else None
        if core == 0:
            return c ^ 2
        return c ^ 4 if x == 1 else None

    def late_target(z, c, core, x):
        return c ^ 4 if z == 3 and core == 0 else None

    def swap(code_of, groups):
        return send(choose(code_of, groups), pairs(lambda z, c, core, x: c ^ 1))

    count = n_win
    half = count // 2
    pieces = [piece_zero]
    for slot in range(1, count):
        ring = [(z, (z + 1) % n_win) for z in range(n_win)]
        pieces.append(lax.ppermute(pieces[-1], "win", ring))
    firsts, seconds, lates = [], [], []

    def first_move(slot, *others):
        in_parts = slot in (0, count - 1)
        target = early_target if in_parts else first_target
        firsts.append(send(after(pieces[slot], *others), pairs(target)))

    def second_move(slot, arrived, *others):
        relay = choose(lambda: square_codes()[:1], [(pieces[slot], arrived)])[0]
        seconds.append(send(after(relay, *others), pairs(second_target)))
        if slot in (0, count - 1):
            lates.append(send(after(pieces[slot], relay), pairs(late_target)))
        else:
            lates.append(firsts[slot])
        return relay

    first_move(0)
    relay = second_move(0, firsts[0])
    first_move(1, *(seconds[0], lates[0]))
    for slot in range(2, count):
        first_move(slot, *())
        second_move(slot - 1, after(firsts[slot - 1], pieces[slot]), seconds[-1])
    own = own_rows(pieces)
    held = list(zip(pieces, firsts, seconds, lates))
    held[0] = (*held[0][:2], after(held[0][2], firsts[-1]), held[0][3])
    swapped_early = swap(lambda: square_codes()[1:2] * half, held[:half])
    second_move(count - 1, after(firsts[-1], own), *())
    held.append((pieces[-1], firsts[-1], seconds[-1], lates[-1]))
    swapped_late = swap(lambda: square_codes()[1:2] * (count - half), held[half:])
    buffers = [buffer for group in held for buffer in group] + [swapped_early, swapped_late]
    groups = []
    for n in range(count):
        swapped = (4 * count, n) if n < half else (4 * count + 1, n - half)
        groups.append([*((4 * n + k, None) for k in range(4)), swapped])
    return own, buffers, groups, lambda: square_codes()[2:] * 2


def on_device(traces, valid, reach):
    width = traces.shape[1]
    n_win, n_chan = lax.axis_size("win"), lax.axis_size("chan")
    offsets = BAND // n_win
    hops = [z * offsets // width for z in range(n_win)]
    piece = whitened_chunk(traces, valid)
    if n_chan == 8 and hops == list(range(4)):
        own, buffers, groups, codes_of = square_partners(piece, n_win, n_chan)
    else:
        own, buffers, groups, codes_of = direct_partners(piece, hops, n_win, n_chan)
    return stacked(own, buffers, groups, codes_of, reach, offsets, traces.shape[0] * n_win)


def solution(mesh):
    in_specs = (P("win", "chan", None), P("win", "chan"), P("chan"))
    out_specs = P("win", "chan", None)
    return jax.shard_map(
        on_device, mesh=mesh, in_specs=in_specs, out_specs=out_specs, check_vma=False
    )
```

```python
import functools
import math

import jax
import jax.numpy as jnp
import numpy as np
from jax import lax
from jax.experimental import pallas as pl
from jax.experimental.pallas import tpu as pltpu
from jax.sharding import PartitionSpec as P

F = 128
FIRST = 16
BAND = 256
AXES = ("chan", "win")
CHANNEL_BLOCK = 8
GROUP = 4
WHITEN_BLOCKS = 4
PITCH_PAD = 8
MIB = 1024 * 1024
VMEM = pl.BlockSpec(memory_space=pltpu.VMEM)
FEW_MIB = pltpu.CompilerParams(vmem_limit_bytes=4 * MIB)
WHOLE_VMEM = pltpu.CompilerParams(vmem_limit_bytes=62 * MIB)
SMEM = pl.BlockSpec(memory_space=pltpu.SMEM)
SMALL = pl.CostEstimate(flops=1, bytes_accessed=1, transcendentals=0)
ANY = pl.BlockSpec(memory_space=pl.ANY)


def make_table(samples):
    t_int = np.arange(samples, dtype=np.int64)
    j_int = np.arange(F, dtype=np.int64) + FIRST
    angle = 2.0 * np.pi / samples * (j_int[:, None] * t_int[None, :] % samples)
    hann = 0.5 - 0.5 * np.cos(2.0 * np.pi / samples * t_int)
    rows = np.concatenate([hann * np.cos(angle), -hann * np.sin(angle)], axis=0)
    return jnp.asarray(rows.astype(np.float32)).astype(jnp.bfloat16)


def whiten_kernel(table_hbm, traces_hbm, valid_hbm, out_ref, table, traces, valid, rows, sems):
    windows, width, samples = traces.shape
    block = windows // WHITEN_BLOCKS if windows % (2 * WHITEN_BLOCKS) == 0 else windows
    copies = [
        pltpu.make_async_copy(table_hbm, table, sems.at[0]),
        pltpu.make_async_copy(valid_hbm, valid, sems.at[1]),
    ]
    for n in range(windows // block):
        part = pl.ds(n * block, block)
        copies.append(
            pltpu.make_async_copy(traces_hbm.at[part], traces.at[part], sems.at[2 + n])
        )
    for copy in copies:
        copy.start()
    copies[0].wait()
    copies[1].wait()
    for w in range(0, windows, 2):
        if w % block == 0:
            copies[2 + w // block].wait()
        spectra = lax.dot_general(
            table[...],
            traces[w : w + 2].reshape(2 * width, samples),
            (((1,), (1,)), ((), ())),
            preferred_element_type=jnp.float32,
        )
        re, im = spectra[:F], spectra[F:]
        power = re * re + im * im
        level = jnp.sqrt(jnp.mean(power, axis=0, keepdims=True) + 1e-06)
        usable = jnp.concatenate([valid[w : w + 1, :], valid[w + 1 : w + 2, :]], axis=1)
        factor = usable.astype(jnp.float32) / (jnp.sqrt(power) + 0.1 * level)
        re, im = re * factor, im * factor
        for k in range(2):
            half = slice(k * width, (k + 1) * width)
            rows[pl.ds(w + k, F, stride=windows), :] = jnp.concatenate(
                [re[:, half], im[:, half]], axis=1
            )
    out_ref[...] = rows[...].reshape(out_ref.shape).astype(jnp.bfloat16)


def whitened_chunk(traces, valid):
    windows, width, samples = traces.shape
    return pl.pallas_call(
        whiten_kernel,
        out_shape=jax.ShapeDtypeStruct((F, windows, 2 * width), jnp.bfloat16),
        in_specs=[ANY] * 3,
        out_specs=VMEM,
        scratch_shapes=[
            pltpu.VMEM((2 * F, samples), jnp.bfloat16),
            pltpu.VMEM(traces.shape, traces.dtype),
            pltpu.VMEM(valid.shape, valid.dtype),
            pltpu.VMEM((F * windows, 2 * width), jnp.float32),
            pltpu.SemaphoreType.DMA((2 + WHITEN_BLOCKS,)),
        ],
        compiler_params=WHOLE_VMEM,
        cost_estimate=pl.CostEstimate(
            flops=4 * F * traces.size, bytes_accessed=2 * traces.size, transcendentals=0
        ),
        name="whiten",
    )(make_table(samples), traces, valid)


def copy_chosen(code, refs, put):
    for index, ref in enumerate(refs):

        @pl.when(code == index)
        def _(ref=ref):
            put(ref)


def choose_kernel(code_of, groups, *refs):
    out_ref = refs[-1]
    per_group = (len(refs) - 1) // groups
    code = code_of()
    for g in range(groups):

        def put(ref, g=g):
            out_ref[g] = ref[...]

        copy_chosen(code, refs[g * per_group : (g + 1) * per_group], put)


def choose(code_of, groups):
    operands = [buffer for group in groups for buffer in group]
    return pl.pallas_call(
        functools.partial(choose_kernel, code_of, len(groups)),
        out_shape=jax.ShapeDtypeStruct((len(groups), *groups[0][0].shape), jnp.bfloat16),
        in_specs=[VMEM] * len(operands),
        out_specs=VMEM,
        compiler_params=FEW_MIB,
        cost_estimate=SMALL,
        name="choose",
    )(*operands)


def own_kernel(*refs):
    out_ref = refs[-1]

    def one_bin(f, carry):
        out_ref[f] = jnp.concatenate([ref[f] for ref in refs[:-1]], axis=0).T
        return carry

    lax.fori_loop(0, out_ref.shape[0], one_bin, 0, unroll=8)


def own_rows(pieces):
    bins, windows, lanes = pieces[0].shape
    return pl.pallas_call(
        own_kernel,
        out_shape=jax.ShapeDtypeStruct(
            (bins, lanes, windows * len(pieces)), jnp.bfloat16
        ),
        in_specs=[VMEM] * len(pieces),
        out_specs=VMEM,
        compiler_params=FEW_MIB,
        cost_estimate=SMALL,
        name="own_rows",
    )(*pieces)


def stack_kernel(scale, groups, codes_of, reach_ref, own, *refs):
    buffers, (out_hbm, partners, products, out, sems) = refs[:-5], refs[-5:]
    bins, lanes, _ = own.shape
    width = lanes // 2
    offsets = out_hbm.shape[0]
    pitch = products.shape[0] // bins
    slots = len(groups)
    first_offset = lax.axis_index("win") * offsets
    codes = codes_of()
    for slot, group in enumerate(groups):
        for which in range(2):
            candidates = [
                buffers[number] if index is None else buffers[number].at[index]
                for number, index in group
            ]

            def put(ref, slot=slot, which=which):
                partners[which, slot] = ref[...]

            copy_chosen(codes[which if slot < slots - 1 else 2 + which], candidates, put)

    first = first_offset % width
    lane = lax.broadcasted_iota(jnp.int32, (width, lanes), 1)
    in_first = lane % width >= lax.broadcasted_iota(jnp.int32, (width, lanes), 0) + first

    sign = jnp.where(lane < width, 1.0, -1.0)

    def products_of(f):
        right = jnp.concatenate(
            [
                jnp.concatenate([partners[which, slot, f] for slot in range(slots)], axis=0)
                for which in range(2)
            ],
            axis=1,
        )
        both = jnp.dot(own[f], right, preferred_element_type=jnp.float32)
        with_re = jnp.where(in_first, both[:width, :lanes], both[:width, lanes:])
        with_im = jnp.where(in_first, both[width:, :lanes], both[width:, lanes:])
        return with_re + sign * pltpu.roll(with_im, width, 1)

    def one_group(group, carry):
        results = [products_of(group * GROUP + n) for n in range(GROUP)]
        for n, result in enumerate(results):
            row = pl.multiple_of((group * GROUP + n) * pitch, 8)
            products[pl.ds(row, width), :] = result
        return carry

    lax.fori_loop(0, bins // GROUP, one_group, 0, unroll=2)

    lane = lax.broadcasted_iota(jnp.int32, (offsets, lanes), 1)
    shift = (lane + offsets * width - lax.broadcasted_iota(jnp.int32, (offsets, lanes), 0)) % width
    shift_re = jnp.where(lane < width, shift, width)
    shift_im = jnp.where(lane < width, width, shift)
    row_k = lax.broadcasted_iota(jnp.int32, (offsets, F), 0) + first_offset

    def copies(block):
        columns = pl.ds(pl.multiple_of(block * CHANNEL_BLOCK, CHANNEL_BLOCK), CHANNEL_BLOCK)
        return [
            pltpu.make_async_copy(
                out.at[part].reshape(offsets, pitch, F).at[:, columns, :],
                out_hbm.at[:, columns, pl.ds(part * F, F)],
                sems.at[block, part],
            )
            for part in range(2)
        ]

    def picked(i):
        at = (i + first) % width
        pick = jnp.concatenate(
            [jnp.where(shift_re == at, 1.0, 0.0), jnp.where(shift_im == at, -1.0, 0.0)], axis=0
        ).astype(jnp.bfloat16)
        x = products[pl.ds(i, F, stride=pitch), :].astype(jnp.bfloat16)
        y = lax.dot_general(
            pick, x, (((1,), (1,)), ((), ())), preferred_element_type=jnp.float32
        )
        inside = jnp.where(row_k < reach_ref[i], scale, 0.0)
        return [y[part * offsets : (part + 1) * offsets] * inside for part in range(2)]

    def one_block(block, carry):
        for begin in range(0, CHANNEL_BLOCK, GROUP):
            channels = [block * CHANNEL_BLOCK + begin + n for n in range(GROUP)]
            results = [picked(i) for i in channels]
            for i, result in zip(channels, results):
                for part in range(2):
                    out[part, pl.ds(i, offsets, stride=pitch), :] = result[part]
        for copy in copies(block):
            copy.start()
        return carry

    blocks = width // CHANNEL_BLOCK
    lax.fori_loop(0, blocks, one_block, 0)

    def finish(block, carry):
        for copy in copies(block):
            copy.wait()
        return carry

    lax.fori_loop(0, blocks, finish, 0)


def stacked(own, buffers, groups, codes_of, reach, offsets, windows):
    bins, lanes, _ = own.shape
    width = lanes // 2
    chunk_windows = buffers[0].shape[-2]
    pitch = width + PITCH_PAD
    return pl.pallas_call(
        functools.partial(stack_kernel, 1.0 / math.sqrt(windows), groups, codes_of),
        out_shape=jax.ShapeDtypeStruct((offsets, width, 2 * F), jnp.float32),
        in_specs=[SMEM] + [VMEM] * (1 + len(buffers)),
        out_specs=ANY,
        scratch_shapes=[
            pltpu.VMEM((2, len(groups), bins, chunk_windows, lanes), jnp.bfloat16),
            pltpu.VMEM((bins * pitch, lanes), jnp.float32),
            pltpu.VMEM((2, offsets * pitch, F), jnp.float32),
            pltpu.SemaphoreType.DMA((width // CHANNEL_BLOCK, 2)),
        ],
        compiler_params=pltpu.CompilerParams(vmem_limit_bytes=28 * MIB),
        cost_estimate=SMALL,
        name="stack",
    )(reach, own, *buffers)


def send(array, pairs):
    return lax.ppermute(array, AXES, pairs)


def pairs_of(n_win, n_chan, target):
    pairs = []
    for z in range(n_win):
        for c in range(n_chan):
            to = target(z, c)
            if to is not None:
                pairs.append((c * n_win + z, to * n_win + z))
    return pairs


def after(array, *others):
    return lax.optimization_barrier((array, *others))[0]


def direct_partners(pieces, hops, n_win, n_chan):
    buffers = []
    for piece in pieces:
        buffers.append(send(piece, pairs_of(n_win, n_chan, lambda z, c: (c - hops[z]) % n_chan)))
        buffers.append(
            send(piece, pairs_of(n_win, n_chan, lambda z, c: (c - hops[z] - 1) % n_chan))
        )
    groups = [[(2 * n, None), (2 * n + 1, None)] for n in range(len(pieces))]
    return own_rows(pieces), buffers, groups, lambda: (0, 1, 0, 1)


def square_codes():
    z, c = lax.axis_index("win"), lax.axis_index("chan")
    core, x = c & 1, (c >> 1) & 1
    onward = jnp.where((z == 0) | (x == 0) | ((z < 3) & (core == 1)), 1, 0)
    odd_next = jnp.where(x == 0, 1, 2)
    even_next = jnp.where(z == 0, odd_next, 2)
    next_code = jnp.where(core == 0, even_next, jnp.where(z == 3, 2, odd_next))
    outgoing = jnp.where(core == 0, jnp.where(z < 2, next_code, 1), jnp.where(z < 2, 0, next_code))
    first = jnp.where(z == 0, 0, jnp.where(z == 2, next_code, 3))
    second = jnp.where(z == 1, next_code, jnp.where(z == 3, 1, 3))
    is_late = (z == 3) & (core == 0)
    outgoing_late = jnp.where(is_late, 3, outgoing)
    second_last = jnp.where(is_late, 4, second)
    return onward, outgoing, outgoing_late, (first, second, first, second_last)


def square_partners(pieces, n_win, n_chan):
    def pairs(target):
        return pairs_of(n_win, n_chan, lambda z, c: target(z, c, c % 2, c // 2 % 2))

    def first_target(z, c, core, x):
        if z == 3:
            return c ^ 4
        if z == 0:
            return c ^ 2 if core == 0 else None
        if core == 1:
            return c ^ 2
        return c ^ 4 if z == 2 or x == 0 else None

    def second_target(z, c, core, x):
        if z == 3:
            return c ^ 2 if core == 1 else None
        if z == 0:
            return c ^ 4 if core == 0 and x == 1 else None
        if core == 0:
            return c ^ 2
        return c ^ 4 if x == 1 else None

    def swap(code_of, groups):
        return send(choose(code_of, groups), pairs(lambda z, c, core, x: c ^ 1))

    count = len(pieces)
    half = count // 2
    firsts, seconds = [], []

    def second_move(slot, arrived):
        relay = choose(lambda: square_codes()[0], [(pieces[slot], arrived)])[0]
        seconds.append(send(relay, pairs(second_target)))
        return relay

    for slot, piece in enumerate(pieces):
        last = slot == count - 1
        if slot >= 2:
            piece = after(piece, firsts[slot - 2])
        firsts.append(
            send(
                piece,
                pairs(
                    lambda z, c, core, x: (
                        None if last and z == 3 and core == 0 else first_target(z, c, core, x)
                    )
                ),
            )
        )
        if slot:
            arrived = firsts[slot - 1]
            arrived = after(arrived, *seconds[-1:])
            second_move(slot - 1, arrived)
    held = list(zip(pieces, firsts, seconds))
    own = own_rows(pieces)
    held[0] = (*held[0][:2], after(held[0][2], firsts[-1]))
    swapped_early = swap(lambda: square_codes()[1], held[:half])
    arrived = after(firsts[-1], own)
    relay = second_move(count - 1, arrived)
    held.append((pieces[-1], firsts[-1], seconds[-1]))
    late = send(
        after(pieces[-1], relay),
        pairs(lambda z, c, core, x: c ^ 4 if z == 3 and core == 0 else None),
    )
    late_groups = [(*group, group[1]) for group in held[half:-1]] + [(*held[-1], late)]
    swapped_late = swap(lambda: square_codes()[2], late_groups)
    buffers = [buffer for group in held for buffer in group] + [swapped_early, swapped_late, late]
    groups = []
    for n in range(count):
        swapped = (3 * count, n) if n < half else (3 * count + 1, n - half)
        groups.append([(3 * n, None), (3 * n + 1, None), (3 * n + 2, None), swapped])
    groups[-1].append((3 * count + 2, None))
    return own, buffers, groups, lambda: square_codes()[3]


def on_device(traces, valid, reach):
    width = traces.shape[1]
    n_win, n_chan = lax.axis_size("win"), lax.axis_size("chan")
    offsets = BAND // n_win
    hops = [z * offsets // width for z in range(n_win)]
    pieces = [whitened_chunk(traces, valid)]
    while len(pieces) < n_win:
        ring = [(z, (z + 1) % n_win) for z in range(n_win)]
        pieces.append(lax.ppermute(pieces[-1], "win", ring))
    if n_chan == 8 and hops == list(range(4)):
        own, buffers, groups, codes_of = square_partners(pieces, n_win, n_chan)
    else:
        own, buffers, groups, codes_of = direct_partners(pieces, hops, n_win, n_chan)
    return stacked(own, buffers, groups, codes_of, reach, offsets, traces.shape[0] * n_win)


def solution(mesh):
    in_specs = (P("win", "chan", None), P("win", "chan"), P("chan"))
    out_specs = P("win", "chan", None)
    return jax.shard_map(
        on_device, mesh=mesh, in_specs=in_specs, out_specs=out_specs, check_vma=False
    )
```

```python
import functools
import math

import jax
import jax.numpy as jnp
import numpy as np
from jax import lax
from jax.experimental import pallas as pl
from jax.experimental.pallas import tpu as pltpu
from jax.sharding import PartitionSpec as P

F = 128
FIRST = 16
BAND = 256
AXES = ("chan", "win")
CHANNEL_BLOCK = 8
GROUP = 4
WHITEN_BLOCKS = 4
PITCH_PAD = 8
MIB = 1024 * 1024
VMEM = pl.BlockSpec(memory_space=pltpu.VMEM)
FEW_MIB = pltpu.CompilerParams(vmem_limit_bytes=4 * MIB)
WHOLE_VMEM = pltpu.CompilerParams(vmem_limit_bytes=62 * MIB)
SMEM = pl.BlockSpec(memory_space=pltpu.SMEM)
SMALL = pl.CostEstimate(flops=1, bytes_accessed=1, transcendentals=0)
ANY = pl.BlockSpec(memory_space=pl.ANY)


def make_table(samples):
    t_int = np.arange(samples, dtype=np.int64)
    j_int = np.arange(F, dtype=np.int64) + FIRST
    angle = 2.0 * np.pi / samples * (j_int[:, None] * t_int[None, :] % samples)
    hann = 0.5 - 0.5 * np.cos(2.0 * np.pi / samples * t_int)
    rows = np.concatenate([hann * np.cos(angle), -hann * np.sin(angle)], axis=0)
    return jnp.asarray(rows.astype(np.float32)).astype(jnp.bfloat16)


def whiten_kernel(table_hbm, traces_hbm, valid_hbm, out_ref, table, traces, valid, rows, sems):
    windows, width, samples = traces.shape
    block = windows // WHITEN_BLOCKS if windows % (2 * WHITEN_BLOCKS) == 0 else windows
    copies = [
        pltpu.make_async_copy(table_hbm, table, sems.at[0]),
        pltpu.make_async_copy(valid_hbm, valid, sems.at[1]),
    ]
    for n in range(windows // block):
        part = pl.ds(n * block, block)
        copies.append(
            pltpu.make_async_copy(traces_hbm.at[part], traces.at[part], sems.at[2 + n])
        )
    for copy in copies:
        copy.start()
    copies[0].wait()
    copies[1].wait()
    for w in range(0, windows, 2):
        if w % block == 0:
            copies[2 + w // block].wait()
        spectra = lax.dot_general(
            table[...],
            traces[w : w + 2].reshape(2 * width, samples),
            (((1,), (1,)), ((), ())),
            preferred_element_type=jnp.float32,
        )
        re, im = spectra[:F], spectra[F:]
        power = re * re + im * im
        level = jnp.sqrt(jnp.mean(power, axis=0, keepdims=True) + 1e-06)
        usable = jnp.concatenate([valid[w : w + 1, :], valid[w + 1 : w + 2, :]], axis=1)
        factor = usable.astype(jnp.float32) / (jnp.sqrt(power) + 0.1 * level)
        re, im = re * factor, im * factor
        for k in range(2):
            half = slice(k * width, (k + 1) * width)
            rows[pl.ds(w + k, F, stride=windows), :] = jnp.concatenate(
                [re[:, half], im[:, half]], axis=1
            )
    out_ref[...] = rows[...].reshape(out_ref.shape).astype(jnp.bfloat16)


def whitened_chunk(traces, valid):
    windows, width, samples = traces.shape
    return pl.pallas_call(
        whiten_kernel,
        out_shape=jax.ShapeDtypeStruct((F, windows, 2 * width), jnp.bfloat16),
        in_specs=[ANY] * 3,
        out_specs=VMEM,
        scratch_shapes=[
            pltpu.VMEM((2 * F, samples), jnp.bfloat16),
            pltpu.VMEM(traces.shape, traces.dtype),
            pltpu.VMEM(valid.shape, valid.dtype),
            pltpu.VMEM((F * windows, 2 * width), jnp.float32),
            pltpu.SemaphoreType.DMA((2 + WHITEN_BLOCKS,)),
        ],
        compiler_params=WHOLE_VMEM,
        cost_estimate=pl.CostEstimate(
            flops=4 * F * traces.size, bytes_accessed=2 * traces.size, transcendentals=0
        ),
        name="whiten",
    )(make_table(samples), traces, valid)


def copy_chosen(code, refs, put):
    for index, ref in enumerate(refs):

        @pl.when(code == index)
        def _(ref=ref):
            put(ref)


def choose_kernel(code_of, groups, *refs):
    out_ref = refs[-1]
    per_group = (len(refs) - 1) // groups
    code = code_of()
    for g in range(groups):

        def put(ref, g=g):
            out_ref[g] = ref[...]

        copy_chosen(code, refs[g * per_group : (g + 1) * per_group], put)


def choose(code_of, groups):
    operands = [buffer for group in groups for buffer in group]
    return pl.pallas_call(
        functools.partial(choose_kernel, code_of, len(groups)),
        out_shape=jax.ShapeDtypeStruct((len(groups), *groups[0][0].shape), jnp.bfloat16),
        in_specs=[VMEM] * len(operands),
        out_specs=VMEM,
        compiler_params=FEW_MIB,
        cost_estimate=SMALL,
        name="choose",
    )(*operands)


def own_kernel(*refs):
    out_ref = refs[-1]

    def one_bin(f, carry):
        out_ref[f] = jnp.concatenate([ref[f] for ref in refs[:-1]], axis=0).T
        return carry

    lax.fori_loop(0, out_ref.shape[0], one_bin, 0, unroll=8)


def own_rows(pieces):
    bins, windows, lanes = pieces[0].shape
    return pl.pallas_call(
        own_kernel,
        out_shape=jax.ShapeDtypeStruct(
            (bins, lanes, windows * len(pieces)), jnp.bfloat16
        ),
        in_specs=[VMEM] * len(pieces),
        out_specs=VMEM,
        compiler_params=FEW_MIB,
        cost_estimate=SMALL,
        name="own_rows",
    )(*pieces)


def stack_kernel(scale, groups, codes_of, reach_ref, own, *refs):
    buffers, (out_hbm, partners, products, rows, out, sems) = refs[:-6], refs[-6:]
    bins, lanes, _ = own.shape
    width = lanes // 2
    offsets = out_hbm.shape[0]
    pitch = products.shape[0] // bins
    channel_pitch = rows.shape[0] // width
    slots = len(groups)
    first_offset = lax.axis_index("win") * offsets
    codes = codes_of()
    for slot, group in enumerate(groups):
        for which in range(2):
            candidates = [
                buffers[number] if index is None else buffers[number].at[index]
                for number, index in group
            ]

            def put(ref, slot=slot, which=which):
                partners[which, slot] = ref[...]

            copy_chosen(codes[which if slot < slots - 1 else 2 + which], candidates, put)

    first = first_offset % width
    lane = lax.broadcasted_iota(jnp.int32, (width, lanes), 1)
    in_first = lane % width >= lax.broadcasted_iota(jnp.int32, (width, lanes), 0) + first

    sign = jnp.where(lane < width, 1.0, -1.0)

    def products_of(f):
        right = jnp.concatenate(
            [
                jnp.concatenate([partners[which, slot, f] for slot in range(slots)], axis=0)
                for which in range(2)
            ],
            axis=1,
        )
        both = jnp.dot(own[f], right, preferred_element_type=jnp.float32)
        with_re = jnp.where(in_first, both[:width, :lanes], both[:width, lanes:])
        with_im = jnp.where(in_first, both[width:, :lanes], both[width:, lanes:])
        return with_re + sign * pltpu.roll(with_im, width, 1)

    def one_group(group, carry):
        results = [products_of(group * GROUP + n) for n in range(GROUP)]
        for n, result in enumerate(results):
            row = pl.multiple_of((group * GROUP + n) * pitch, 8)
            products[pl.ds(row, width), :] = result
        return carry

    lax.fori_loop(0, bins // GROUP, one_group, 0, unroll=2)

    lane = lax.broadcasted_iota(jnp.int32, (offsets, lanes), 1)
    shift = (lane + offsets * width - lax.broadcasted_iota(jnp.int32, (offsets, lanes), 0)) % width
    shift_re = jnp.where(lane < width, shift, width)
    shift_im = jnp.where(lane < width, width, shift)
    row_k = lax.broadcasted_iota(jnp.int32, (offsets, F), 0) + first_offset

    def copies(block):
        columns = pl.ds(pl.multiple_of(block * CHANNEL_BLOCK, CHANNEL_BLOCK), CHANNEL_BLOCK)
        return [
            pltpu.make_async_copy(
                out.at[part, :, columns, :],
                out_hbm.at[:, columns, pl.ds(part * F, F)],
                sems.at[block, part],
            )
            for part in range(2)
        ]

    def picked(i):
        at = (i + first) % width
        pick = jnp.concatenate(
            [jnp.where(shift_re == at, 1.0, 0.0), jnp.where(shift_im == at, -1.0, 0.0)], axis=0
        ).astype(jnp.bfloat16)
        x = products[pl.ds(i, F, stride=pitch), :].astype(jnp.bfloat16)
        y = lax.dot_general(
            pick, x, (((1,), (1,)), ((), ())), preferred_element_type=jnp.float32
        )
        inside = jnp.where(row_k < reach_ref[i], scale, 0.0)
        return [y[part * offsets : (part + 1) * offsets] * inside for part in range(2)]

    def one_block(block, carry):
        for begin in range(0, CHANNEL_BLOCK, GROUP):
            channels = [block * CHANNEL_BLOCK + begin + n for n in range(GROUP)]
            results = [picked(i) for i in channels]
            for i, result in zip(channels, results):
                for part in range(2):
                    row = pl.multiple_of(i * channel_pitch + part * offsets, 8)
                    rows[pl.ds(row, offsets), :] = result[part]
        begin = block * CHANNEL_BLOCK
        columns = pl.ds(pl.multiple_of(begin, CHANNEL_BLOCK), CHANNEL_BLOCK)
        for part in range(2):
            for k in range(offsets):
                row = begin * channel_pitch + part * offsets + k
                out[part, k, columns, :] = rows[
                    pl.ds(row, CHANNEL_BLOCK, stride=channel_pitch), :
                ]
        for copy in copies(block):
            copy.start()
        return carry

    blocks = width // CHANNEL_BLOCK
    lax.fori_loop(0, blocks, one_block, 0)

    def finish(block, carry):
        for copy in copies(block):
            copy.wait()
        return carry

    lax.fori_loop(0, blocks, finish, 0)


def stacked(own, buffers, groups, codes_of, reach, offsets, windows):
    bins, lanes, _ = own.shape
    width = lanes // 2
    chunk_windows = buffers[0].shape[-2]
    pitch = width + PITCH_PAD
    return pl.pallas_call(
        functools.partial(stack_kernel, 1.0 / math.sqrt(windows), groups, codes_of),
        out_shape=jax.ShapeDtypeStruct((offsets, width, 2 * F), jnp.float32),
        in_specs=[SMEM] + [VMEM] * (1 + len(buffers)),
        out_specs=ANY,
        scratch_shapes=[
            pltpu.VMEM((2, len(groups), bins, chunk_windows, lanes), jnp.bfloat16),
            pltpu.VMEM((bins * pitch, lanes), jnp.float32),
            pltpu.VMEM((width * (2 * offsets + PITCH_PAD), F), jnp.float32),
            pltpu.VMEM((2, offsets, width, F), jnp.float32),
            pltpu.SemaphoreType.DMA((width // CHANNEL_BLOCK, 2)),
        ],
        compiler_params=pltpu.CompilerParams(vmem_limit_bytes=32 * MIB),
        cost_estimate=SMALL,
        name="stack",
    )(reach, own, *buffers)


def send(array, pairs):
    return lax.ppermute(array, AXES, pairs)


def pairs_of(n_win, n_chan, target):
    pairs = []
    for z in range(n_win):
        for c in range(n_chan):
            to = target(z, c)
            if to is not None:
                pairs.append((c * n_win + z, to * n_win + z))
    return pairs


def after(array, *others):
    return lax.optimization_barrier((array, *others))[0]


def direct_partners(pieces, hops, n_win, n_chan):
    buffers = []
    for piece in pieces:
        buffers.append(send(piece, pairs_of(n_win, n_chan, lambda z, c: (c - hops[z]) % n_chan)))
        buffers.append(
            send(piece, pairs_of(n_win, n_chan, lambda z, c: (c - hops[z] - 1) % n_chan))
        )
    groups = [[(2 * n, None), (2 * n + 1, None)] for n in range(len(pieces))]
    return own_rows(pieces), buffers, groups, lambda: (0, 1, 0, 1)


def square_codes():
    z, c = lax.axis_index("win"), lax.axis_index("chan")
    core, x = c & 1, (c >> 1) & 1
    onward = jnp.where((z == 0) | (x == 0) | ((z < 3) & (core == 1)), 1, 0)
    odd_next = jnp.where(x == 0, 1, 2)
    even_next = jnp.where(z == 0, odd_next, 2)
    next_code = jnp.where(core == 0, even_next, jnp.where(z == 3, 2, odd_next))
    outgoing = jnp.where(core == 0, jnp.where(z < 2, next_code, 1), jnp.where(z < 2, 0, next_code))
    first = jnp.where(z == 0, 0, jnp.where(z == 2, next_code, 3))
    second = jnp.where(z == 1, next_code, jnp.where(z == 3, 1, 3))
    is_late = (z == 3) & (core == 0)
    outgoing_late = jnp.where(is_late, 3, outgoing)
    second_last = jnp.where(is_late, 4, second)
    return onward, outgoing, outgoing_late, (first, second, first, second_last)


def square_partners(pieces, n_win, n_chan):
    def pairs(target):
        return pairs_of(n_win, n_chan, lambda z, c: target(z, c, c % 2, c // 2 % 2))

    def first_target(z, c, core, x):
        if z == 3:
            return c ^ 4
        if z == 0:
            return c ^ 2 if core == 0 else None
        if core == 1:
            return c ^ 2
        return c ^ 4 if z == 2 or x == 0 else None

    def second_target(z, c, core, x):
        if z == 3:
            return c ^ 2 if core == 1 else None
        if z == 0:
            return c ^ 4 if core == 0 and x == 1 else None
        if core == 0:
            return c ^ 2
        return c ^ 4 if x == 1 else None

    def swap(code_of, groups):
        return send(choose(code_of, groups), pairs(lambda z, c, core, x: c ^ 1))

    count = len(pieces)
    half = count // 2
    firsts, seconds = [], []

    def second_move(slot, arrived):
        relay = choose(lambda: square_codes()[0], [(pieces[slot], arrived)])[0]
        seconds.append(send(relay, pairs(second_target)))
        return relay

    for slot, piece in enumerate(pieces):
        last = slot == count - 1
        if slot >= 2:
            piece = after(piece, firsts[slot - 2])
        firsts.append(
            send(
                piece,
                pairs(
                    lambda z, c, core, x: (
                        None if last and z == 3 and core == 0 else first_target(z, c, core, x)
                    )
                ),
            )
        )
        if slot:
            arrived = firsts[slot - 1]
            arrived = after(arrived, *seconds[-1:])
            second_move(slot - 1, arrived)
    held = list(zip(pieces, firsts, seconds))
    own = own_rows(pieces)
    held[0] = (*held[0][:2], after(held[0][2], firsts[-1]))
    swapped_early = swap(lambda: square_codes()[1], held[:half])
    arrived = after(firsts[-1], own)
    relay = second_move(count - 1, arrived)
    held.append((pieces[-1], firsts[-1], seconds[-1]))
    late = send(
        after(pieces[-1], relay),
        pairs(lambda z, c, core, x: c ^ 4 if z == 3 and core == 0 else None),
    )
    late_groups = [(*group, group[1]) for group in held[half:-1]] + [(*held[-1], late)]
    swapped_late = swap(lambda: square_codes()[2], late_groups)
    buffers = [buffer for group in held for buffer in group] + [swapped_early, swapped_late, late]
    groups = []
    for n in range(count):
        swapped = (3 * count, n) if n < half else (3 * count + 1, n - half)
        groups.append([(3 * n, None), (3 * n + 1, None), (3 * n + 2, None), swapped])
    groups[-1].append((3 * count + 2, None))
    return own, buffers, groups, lambda: square_codes()[3]


def on_device(traces, valid, reach):
    width = traces.shape[1]
    n_win, n_chan = lax.axis_size("win"), lax.axis_size("chan")
    offsets = BAND // n_win
    hops = [z * offsets // width for z in range(n_win)]
    pieces = [whitened_chunk(traces, valid)]
    while len(pieces) < n_win:
        ring = [(z, (z + 1) % n_win) for z in range(n_win)]
        pieces.append(lax.ppermute(pieces[-1], "win", ring))
    if n_chan == 8 and hops == list(range(4)):
        own, buffers, groups, codes_of = square_partners(pieces, n_win, n_chan)
    else:
        own, buffers, groups, codes_of = direct_partners(pieces, hops, n_win, n_chan)
    return stacked(own, buffers, groups, codes_of, reach, offsets, traces.shape[0] * n_win)


def solution(mesh):
    in_specs = (P("win", "chan", None), P("win", "chan"), P("chan"))
    out_specs = P("win", "chan", None)
    return jax.shard_map(
        on_device, mesh=mesh, in_specs=in_specs, out_specs=out_specs, check_vma=False
    )
```

```python
import functools
import math

import jax
import jax.numpy as jnp
import numpy as np
from jax import lax
from jax.experimental import pallas as pl
from jax.experimental.pallas import tpu as pltpu
from jax.sharding import PartitionSpec as P

F = 128
FIRST = 16
BAND = 256
AXES = ("chan", "win")
CHANNEL_BLOCK = 8
MATMUL_DEPTH = 256
WHITEN_BLOCKS = 4
PITCH_PAD = 8
MIB = 1024 * 1024
VMEM = pl.BlockSpec(memory_space=pltpu.VMEM)
FEW_MIB = pltpu.CompilerParams(vmem_limit_bytes=4 * MIB)
WHOLE_VMEM = pltpu.CompilerParams(vmem_limit_bytes=62 * MIB)
SMEM = pl.BlockSpec(memory_space=pltpu.SMEM)
SMALL = pl.CostEstimate(flops=1, bytes_accessed=1, transcendentals=0)
ANY = pl.BlockSpec(memory_space=pl.ANY)


def make_table(samples):
    t_int = np.arange(samples, dtype=np.int64)
    j_int = np.arange(F, dtype=np.int64) + FIRST
    angle = 2.0 * np.pi / samples * (j_int[:, None] * t_int[None, :] % samples)
    hann = 0.5 - 0.5 * np.cos(2.0 * np.pi / samples * t_int)
    rows = np.concatenate([hann * np.cos(angle), -hann * np.sin(angle)], axis=0)
    return jnp.asarray(rows.astype(np.float32)).astype(jnp.bfloat16)


def whiten_kernel(table_hbm, traces_hbm, valid_hbm, out_ref, table, traces, valid, rows, sems):
    windows, width, samples = traces.shape
    block = windows // WHITEN_BLOCKS if windows % (2 * WHITEN_BLOCKS) == 0 else windows
    copies = [
        pltpu.make_async_copy(table_hbm, table, sems.at[0]),
        pltpu.make_async_copy(valid_hbm, valid, sems.at[1]),
    ]
    for n in range(windows // block):
        part = pl.ds(n * block, block)
        copies.append(
            pltpu.make_async_copy(traces_hbm.at[part], traces.at[part], sems.at[2 + n])
        )
    for copy in copies:
        copy.start()
    copies[0].wait()
    copies[1].wait()
    for w in range(0, windows, 2):
        if w % block == 0:
            copies[2 + w // block].wait()
        spectra = lax.dot_general(
            table[...],
            traces[w : w + 2].reshape(2 * width, samples),
            (((1,), (1,)), ((), ())),
            preferred_element_type=jnp.float32,
        )
        re, im = spectra[:F], spectra[F:]
        power = re * re + im * im
        level = jnp.sqrt(jnp.mean(power, axis=0, keepdims=True) + 1e-06)
        usable = jnp.concatenate([valid[w : w + 1, :], valid[w + 1 : w + 2, :]], axis=1)
        factor = usable.astype(jnp.float32) / (jnp.sqrt(power) + 0.1 * level)
        re, im = re * factor, im * factor
        for k in range(2):
            half = slice(k * width, (k + 1) * width)
            rows[pl.ds(w + k, F, stride=windows), :] = jnp.concatenate(
                [re[:, half], im[:, half]], axis=1
            )
    out_ref[...] = rows[...].reshape(out_ref.shape).astype(jnp.bfloat16)


def whitened_chunk(traces, valid):
    windows, width, samples = traces.shape
    return pl.pallas_call(
        whiten_kernel,
        out_shape=jax.ShapeDtypeStruct((F, windows, 2 * width), jnp.bfloat16),
        in_specs=[ANY] * 3,
        out_specs=VMEM,
        scratch_shapes=[
            pltpu.VMEM((2 * F, samples), jnp.bfloat16),
            pltpu.VMEM(traces.shape, traces.dtype),
            pltpu.VMEM(valid.shape, valid.dtype),
            pltpu.VMEM((F * windows, 2 * width), jnp.float32),
            pltpu.SemaphoreType.DMA((2 + WHITEN_BLOCKS,)),
        ],
        compiler_params=WHOLE_VMEM,
        cost_estimate=pl.CostEstimate(
            flops=4 * F * traces.size, bytes_accessed=2 * traces.size, transcendentals=0
        ),
        name="whiten",
    )(make_table(samples), traces, valid)


def copy_chosen(code, refs, put):
    for index, ref in enumerate(refs):

        @pl.when(code == index)
        def _(ref=ref):
            put(ref)


def choose_kernel(code_of, groups, *refs):
    out_ref = refs[-1]
    per_group = (len(refs) - 1) // groups
    code = code_of()
    for g in range(groups):

        def put(ref, g=g):
            out_ref[g] = ref[...]

        copy_chosen(code, refs[g * per_group : (g + 1) * per_group], put)


def choose(code_of, groups):
    operands = [buffer for group in groups for buffer in group]
    return pl.pallas_call(
        functools.partial(choose_kernel, code_of, len(groups)),
        out_shape=jax.ShapeDtypeStruct((len(groups), *groups[0][0].shape), jnp.bfloat16),
        in_specs=[VMEM] * len(operands),
        out_specs=VMEM,
        compiler_params=FEW_MIB,
        cost_estimate=SMALL,
        name="choose",
    )(*operands)


def own_kernel(*refs):
    out_ref = refs[-1]
    _, rows, depth = out_ref.shape
    lanes = refs[0].shape[-1]
    together = rows // lanes
    windows = depth // together

    def one_group(group, carry):
        for n in range(together):
            f = group * together + n
            turned = jnp.concatenate([ref[f] for ref in refs[:-1]], axis=0).T
            parts = [
                turned if m == n else jnp.zeros((lanes, windows), turned.dtype)
                for m in range(together)
            ]
            out_ref[group, n * lanes : (n + 1) * lanes, :] = jnp.concatenate(parts, axis=1)
        return carry

    lax.fori_loop(0, out_ref.shape[0], one_group, 0, unroll=2)


def own_rows(pieces):
    bins, windows, lanes = pieces[0].shape
    depth = windows * len(pieces)
    together = max(1, MATMUL_DEPTH // depth)
    return pl.pallas_call(
        own_kernel,
        out_shape=jax.ShapeDtypeStruct(
            (bins // together, together * lanes, together * depth), jnp.bfloat16
        ),
        in_specs=[VMEM] * len(pieces),
        out_specs=VMEM,
        compiler_params=FEW_MIB,
        cost_estimate=SMALL,
        name="own_rows",
    )(*pieces)


def stack_kernel(scale, groups, codes_of, reach_ref, own, *refs):
    buffers, (out_hbm, partners, products, out, sems) = refs[:-5], refs[-5:]
    _, _, bins, _, lanes = partners.shape
    width = lanes // 2
    together = bins // own.shape[0]
    offsets = out_hbm.shape[0]
    pitch = products.shape[0] // bins
    slots = len(groups)
    first_offset = lax.axis_index("win") * offsets
    codes = codes_of()
    for slot, group in enumerate(groups):
        for which in range(2):
            candidates = [
                buffers[number] if index is None else buffers[number].at[index]
                for number, index in group
            ]

            def put(ref, slot=slot, which=which):
                partners[which, slot] = ref[...]

            copy_chosen(codes[which if slot < slots - 1 else 2 + which], candidates, put)

    first = first_offset % width
    lane = lax.broadcasted_iota(jnp.int32, (width, lanes), 1)
    in_first = lane % width >= lax.broadcasted_iota(jnp.int32, (width, lanes), 0) + first

    sign = jnp.where(lane < width, 1.0, -1.0)

    def one_group(group, carry):
        bins_here = [group * together + n for n in range(together)]
        right = jnp.concatenate(
            [
                jnp.concatenate(
                    [partners[which, slot, f] for f in bins_here for slot in range(slots)], axis=0
                )
                for which in range(2)
            ],
            axis=1,
        )
        both = jnp.dot(own[group], right, preferred_element_type=jnp.float32)
        for n, f in enumerate(bins_here):
            re = both[2 * n * width : (2 * n + 1) * width]
            im = both[(2 * n + 1) * width : (2 * n + 2) * width]
            with_re = jnp.where(in_first, re[:, :lanes], re[:, lanes:])
            with_im = jnp.where(in_first, im[:, :lanes], im[:, lanes:])
            row = pl.multiple_of(f * pitch, 8)
            products[pl.ds(row, width), :] = with_re + sign * pltpu.roll(with_im, width, 1)
        return carry

    lax.fori_loop(0, own.shape[0], one_group, 0, unroll=2)

    lane = lax.broadcasted_iota(jnp.int32, (offsets, lanes), 1)
    shift = (lane + offsets * width - lax.broadcasted_iota(jnp.int32, (offsets, lanes), 0)) % width
    shift_re = jnp.where(lane < width, shift, width)
    shift_im = jnp.where(lane < width, width, shift)
    row_k = lax.broadcasted_iota(jnp.int32, (offsets, F), 0) + first_offset

    def copies(block):
        columns = pl.ds(pl.multiple_of(block * CHANNEL_BLOCK, CHANNEL_BLOCK), CHANNEL_BLOCK)
        return [
            pltpu.make_async_copy(
                out.at[part].reshape(offsets, pitch, F).at[:, columns, :],
                out_hbm.at[:, columns, pl.ds(part * F, F)],
                sems.at[block, part],
            )
            for part in range(2)
        ]

    def picked(i):
        at = (i + first) % width
        pick = jnp.concatenate(
            [jnp.where(shift_re == at, 1.0, 0.0), jnp.where(shift_im == at, -1.0, 0.0)], axis=0
        ).astype(jnp.bfloat16)
        return pick, products[pl.ds(i, F, stride=pitch), :].astype(jnp.bfloat16)

    def one_block(block, carry):
        for begin in range(0, CHANNEL_BLOCK, 2):
            channels = [block * CHANNEL_BLOCK + begin + n for n in range(2)]
            (pick0, x0), (pick1, x1) = [picked(i) for i in channels]
            none = jnp.zeros_like(pick0)
            pick = jnp.concatenate(
                [
                    jnp.concatenate([pick0, none], axis=1),
                    jnp.concatenate([none, pick1], axis=1),
                ],
                axis=0,
            )
            y = lax.dot_general(
                pick,
                jnp.concatenate([x0, x1], axis=1),
                (((1,), (1,)), ((), ())),
                preferred_element_type=jnp.float32,
            )
            for n, i in enumerate(channels):
                inside = jnp.where(row_k < reach_ref[i], scale, 0.0)
                for part in range(2):
                    begin_row = (2 * n + part) * offsets
                    out[part, pl.ds(i, offsets, stride=pitch), :] = (
                        y[begin_row : begin_row + offsets] * inside
                    )
        for copy in copies(block):
            copy.start()
        return carry

    blocks = width // CHANNEL_BLOCK
    lax.fori_loop(0, blocks, one_block, 0)

    def finish(block, carry):
        for copy in copies(block):
            copy.wait()
        return carry

    lax.fori_loop(0, blocks, finish, 0)


def stacked(own, buffers, groups, codes_of, reach, offsets, windows):
    bins, chunk_windows, lanes = buffers[0].shape
    width = lanes // 2
    pitch = width + PITCH_PAD
    return pl.pallas_call(
        functools.partial(stack_kernel, 1.0 / math.sqrt(windows), groups, codes_of),
        out_shape=jax.ShapeDtypeStruct((offsets, width, 2 * F), jnp.float32),
        in_specs=[SMEM] + [VMEM] * (1 + len(buffers)),
        out_specs=ANY,
        scratch_shapes=[
            pltpu.VMEM((2, len(groups), bins, chunk_windows, lanes), jnp.bfloat16),
            pltpu.VMEM((bins * pitch, lanes), jnp.float32),
            pltpu.VMEM((2, offsets * pitch, F), jnp.float32),
            pltpu.SemaphoreType.DMA((width // CHANNEL_BLOCK, 2)),
        ],
        compiler_params=pltpu.CompilerParams(vmem_limit_bytes=28 * MIB),
        cost_estimate=SMALL,
        name="stack",
    )(reach, own, *buffers)


def send(array, pairs):
    return lax.ppermute(array, AXES, pairs)


def pairs_of(n_win, n_chan, target):
    pairs = []
    for z in range(n_win):
        for c in range(n_chan):
            to = target(z, c)
            if to is not None:
                pairs.append((c * n_win + z, to * n_win + z))
    return pairs


def after(array, *others):
    return lax.optimization_barrier((array, *others))[0]


def direct_partners(pieces, hops, n_win, n_chan):
    buffers = []
    for piece in pieces:
        buffers.append(send(piece, pairs_of(n_win, n_chan, lambda z, c: (c - hops[z]) % n_chan)))
        buffers.append(
            send(piece, pairs_of(n_win, n_chan, lambda z, c: (c - hops[z] - 1) % n_chan))
        )
    groups = [[(2 * n, None), (2 * n + 1, None)] for n in range(len(pieces))]
    return own_rows(pieces), buffers, groups, lambda: (0, 1, 0, 1)


def square_codes():
    z, c = lax.axis_index("win"), lax.axis_index("chan")
    core, x = c & 1, (c >> 1) & 1
    onward = jnp.where((z == 0) | (x == 0) | ((z < 3) & (core == 1)), 1, 0)
    odd_next = jnp.where(x == 0, 1, 2)
    even_next = jnp.where(z == 0, odd_next, 2)
    next_code = jnp.where(core == 0, even_next, jnp.where(z == 3, 2, odd_next))
    outgoing = jnp.where(core == 0, jnp.where(z < 2, next_code, 1), jnp.where(z < 2, 0, next_code))
    first = jnp.where(z == 0, 0, jnp.where(z == 2, next_code, 3))
    second = jnp.where(z == 1, next_code, jnp.where(z == 3, 1, 3))
    is_late = (z == 3) & (core == 0)
    outgoing_late = jnp.where(is_late, 3, outgoing)
    second_last = jnp.where(is_late, 4, second)
    return onward, outgoing, outgoing_late, (first, second, first, second_last)


def square_partners(pieces, n_win, n_chan):
    def pairs(target):
        return pairs_of(n_win, n_chan, lambda z, c: target(z, c, c % 2, c // 2 % 2))

    def first_target(z, c, core, x):
        if z == 3:
            return c ^ 4
        if z == 0:
            return c ^ 2 if core == 0 else None
        if core == 1:
            return c ^ 2
        return c ^ 4 if z == 2 or x == 0 else None

    def second_target(z, c, core, x):
        if z == 3:
            return c ^ 2 if core == 1 else None
        if z == 0:
            return c ^ 4 if core == 0 and x == 1 else None
        if core == 0:
            return c ^ 2
        return c ^ 4 if x == 1 else None

    def swap(code_of, groups):
        return send(choose(code_of, groups), pairs(lambda z, c, core, x: c ^ 1))

    count = len(pieces)
    half = count // 2
    firsts, seconds = [], []

    def second_move(slot, arrived):
        relay = choose(lambda: square_codes()[0], [(pieces[slot], arrived)])[0]
        seconds.append(send(relay, pairs(second_target)))
        return relay

    for slot, piece in enumerate(pieces):
        last = slot == count - 1
        if slot >= 2:
            piece = after(piece, firsts[slot - 2])
        firsts.append(
            send(
                piece,
                pairs(
                    lambda z, c, core, x: (
                        None if last and z == 3 and core == 0 else first_target(z, c, core, x)
                    )
                ),
            )
        )
        if slot:
            arrived = firsts[slot - 1]
            arrived = after(arrived, *seconds[-1:])
            second_move(slot - 1, arrived)
    held = list(zip(pieces, firsts, seconds))
    own = own_rows(pieces)
    held[0] = (*held[0][:2], after(held[0][2], firsts[-1]))
    swapped_early = swap(lambda: square_codes()[1], held[:half])
    arrived = after(firsts[-1], own)
    relay = second_move(count - 1, arrived)
    held.append((pieces[-1], firsts[-1], seconds[-1]))
    late = send(
        after(pieces[-1], relay),
        pairs(lambda z, c, core, x: c ^ 4 if z == 3 and core == 0 else None),
    )
    late_groups = [(*group, group[1]) for group in held[half:-1]] + [(*held[-1], late)]
    swapped_late = swap(lambda: square_codes()[2], late_groups)
    buffers = [buffer for group in held for buffer in group] + [swapped_early, swapped_late, late]
    groups = []
    for n in range(count):
        swapped = (3 * count, n) if n < half else (3 * count + 1, n - half)
        groups.append([(3 * n, None), (3 * n + 1, None), (3 * n + 2, None), swapped])
    groups[-1].append((3 * count + 2, None))
    return own, buffers, groups, lambda: square_codes()[3]


def on_device(traces, valid, reach):
    width = traces.shape[1]
    n_win, n_chan = lax.axis_size("win"), lax.axis_size("chan")
    offsets = BAND // n_win
    hops = [z * offsets // width for z in range(n_win)]
    pieces = [whitened_chunk(traces, valid)]
    while len(pieces) < n_win:
        ring = [(z, (z + 1) % n_win) for z in range(n_win)]
        pieces.append(lax.ppermute(pieces[-1], "win", ring))
    if n_chan == 8 and hops == list(range(4)):
        own, buffers, groups, codes_of = square_partners(pieces, n_win, n_chan)
    else:
        own, buffers, groups, codes_of = direct_partners(pieces, hops, n_win, n_chan)
    return stacked(own, buffers, groups, codes_of, reach, offsets, traces.shape[0] * n_win)


def solution(mesh):
    in_specs = (P("win", "chan", None), P("win", "chan"), P("chan"))
    out_specs = P("win", "chan", None)
    return jax.shard_map(
        on_device, mesh=mesh, in_specs=in_specs, out_specs=out_specs, check_vma=False
    )
```

```python
import functools
import math

import jax
import jax.numpy as jnp
import numpy as np
from jax import lax
from jax.experimental import pallas as pl
from jax.experimental.pallas import tpu as pltpu
from jax.sharding import PartitionSpec as P

F = 128
FIRST = 16
BAND = 256
AXES = ("chan", "win")
CHANNEL_BLOCK = 8
GROUP = 4
PITCH_PAD = 8
MIB = 1024 * 1024
VMEM = pl.BlockSpec(memory_space=pltpu.VMEM)
FEW_MIB = pltpu.CompilerParams(vmem_limit_bytes=4 * MIB)
SMEM = pl.BlockSpec(memory_space=pltpu.SMEM)
SMALL = pl.CostEstimate(flops=1, bytes_accessed=1, transcendentals=0)
ANY = pl.BlockSpec(memory_space=pl.ANY)


def make_table(samples):
    t_int = np.arange(samples, dtype=np.int64)
    j_int = np.arange(F, dtype=np.int64) + FIRST
    angle = 2.0 * np.pi / samples * (j_int[:, None] * t_int[None, :] % samples)
    hann = 0.5 - 0.5 * np.cos(2.0 * np.pi / samples * t_int)
    rows = np.concatenate([hann * np.cos(angle), -hann * np.sin(angle)], axis=0)
    return jnp.asarray(rows.astype(np.float32)).astype(jnp.bfloat16)


def whiten_kernel(table, traces, valid, out_ref, rows):
    windows, width, samples = traces.shape
    for w in range(0, windows, 2):
        spectra = lax.dot_general(
            table[...],
            traces[w : w + 2].reshape(2 * width, samples),
            (((1,), (1,)), ((), ())),
            preferred_element_type=jnp.float32,
        )
        re, im = spectra[:F], spectra[F:]
        power = re * re + im * im
        level = jnp.sqrt(jnp.mean(power, axis=0, keepdims=True) + 1e-06)
        usable = jnp.concatenate([valid[w : w + 1, :], valid[w + 1 : w + 2, :]], axis=1)
        factor = usable.astype(jnp.float32) / (jnp.sqrt(power) + 0.1 * level)
        re, im = re * factor, im * factor
        for k in range(2):
            half = slice(k * width, (k + 1) * width)
            rows[pl.ds(w + k, F, stride=windows), :] = jnp.concatenate(
                [re[:, half], im[:, half]], axis=1
            )
    out_ref[...] = rows[...].reshape(out_ref.shape).astype(jnp.bfloat16)


def whitened_chunk(traces, valid):
    windows, width, samples = traces.shape
    return pl.pallas_call(
        whiten_kernel,
        out_shape=jax.ShapeDtypeStruct((F, windows, 2 * width), jnp.bfloat16),
        in_specs=[VMEM] * 3,
        out_specs=VMEM,
        scratch_shapes=[pltpu.VMEM((F * windows, 2 * width), jnp.float32)],
        compiler_params=FEW_MIB,
        cost_estimate=SMALL,
        name="whiten",
    )(make_table(samples), traces, valid)


def copy_chosen(code, refs, put):
    for index, ref in enumerate(refs):

        @pl.when(code == index)
        def _(ref=ref):
            put(ref)


def choose_kernel(code_of, groups, *refs):
    out_ref = refs[-1]
    per_group = (len(refs) - 1) // groups
    code = code_of()
    for g in range(groups):

        def put(ref, g=g):
            out_ref[g] = ref[...]

        copy_chosen(code, refs[g * per_group : (g + 1) * per_group], put)


def choose(code_of, groups):
    operands = [buffer for group in groups for buffer in group]
    return pl.pallas_call(
        functools.partial(choose_kernel, code_of, len(groups)),
        out_shape=jax.ShapeDtypeStruct((len(groups), *groups[0][0].shape), jnp.bfloat16),
        in_specs=[VMEM] * len(operands),
        out_specs=VMEM,
        compiler_params=FEW_MIB,
        cost_estimate=SMALL,
        name="choose",
    )(*operands)


def own_kernel(*refs):
    out_ref = refs[-1]

    def one_bin(f, carry):
        out_ref[f] = jnp.concatenate([ref[f] for ref in refs[:-1]], axis=0).T
        return carry

    lax.fori_loop(0, out_ref.shape[0], one_bin, 0, unroll=8)


def own_rows(pieces):
    bins, windows, lanes = pieces[0].shape
    return pl.pallas_call(
        own_kernel,
        out_shape=jax.ShapeDtypeStruct(
            (bins, lanes, windows * len(pieces)), jnp.bfloat16
        ),
        in_specs=[VMEM] * len(pieces),
        out_specs=VMEM,
        compiler_params=FEW_MIB,
        cost_estimate=SMALL,
        name="own_rows",
    )(*pieces)


def stack_kernel(scale, groups, codes_of, reach_ref, own, *refs):
    buffers, (out_hbm, partners, products, out, sems) = refs[:-5], refs[-5:]
    bins, lanes, _ = own.shape
    width = lanes // 2
    offsets = out_hbm.shape[0]
    pitch = products.shape[0] // bins
    slots = len(groups)
    first_offset = lax.axis_index("win") * offsets
    codes = codes_of()
    for slot, group in enumerate(groups):
        for which in range(2):
            candidates = [
                buffers[number] if index is None else buffers[number].at[index]
                for number, index in group
            ]

            def put(ref, slot=slot, which=which):
                partners[which, slot] = ref[...]

            copy_chosen(codes[which if slot < slots - 1 else 2 + which], candidates, put)

    first = first_offset % width
    lane = lax.broadcasted_iota(jnp.int32, (width, lanes), 1)
    in_first = lane % width >= lax.broadcasted_iota(jnp.int32, (width, lanes), 0) + first

    sign = jnp.where(lane < width, 1.0, -1.0)

    def products_of(f):
        right = jnp.concatenate(
            [
                jnp.concatenate([partners[which, slot, f] for slot in range(slots)], axis=0)
                for which in range(2)
            ],
            axis=1,
        )
        both = jnp.dot(own[f], right, preferred_element_type=jnp.float32)
        with_re = jnp.where(in_first, both[:width, :lanes], both[:width, lanes:])
        with_im = jnp.where(in_first, both[width:, :lanes], both[width:, lanes:])
        return with_re + sign * pltpu.roll(with_im, width, 1)

    def one_group(group, carry):
        results = [products_of(group * GROUP + n) for n in range(GROUP)]
        for n, result in enumerate(results):
            row = pl.multiple_of((group * GROUP + n) * pitch, 8)
            products[pl.ds(row, width), :] = result
        return carry

    lax.fori_loop(0, bins // GROUP, one_group, 0, unroll=2)

    lane = lax.broadcasted_iota(jnp.int32, (offsets, lanes), 1)
    shift = (lane + offsets * width - lax.broadcasted_iota(jnp.int32, (offsets, lanes), 0)) % width
    shift_re = jnp.where(lane < width, shift, width)
    shift_im = jnp.where(lane < width, width, shift)
    row_k = lax.broadcasted_iota(jnp.int32, (offsets, F), 0) + first_offset

    def copies(block):
        columns = pl.ds(pl.multiple_of(block * CHANNEL_BLOCK, CHANNEL_BLOCK), CHANNEL_BLOCK)
        return [
            pltpu.make_async_copy(
                out.at[part].reshape(offsets, pitch, F).at[:, columns, :],
                out_hbm.at[:, columns, pl.ds(part * F, F)],
                sems.at[block, part],
            )
            for part in range(2)
        ]

    def picked(i):
        at = (i + first) % width
        pick = jnp.concatenate(
            [jnp.where(shift_re == at, 1.0, 0.0), jnp.where(shift_im == at, -1.0, 0.0)], axis=0
        ).astype(jnp.bfloat16)
        x = products[pl.ds(i, F, stride=pitch), :].astype(jnp.bfloat16)
        y = lax.dot_general(
            pick, x, (((1,), (1,)), ((), ())), preferred_element_type=jnp.float32
        )
        inside = jnp.where(row_k < reach_ref[i], scale, 0.0)
        return [y[part * offsets : (part + 1) * offsets] * inside for part in range(2)]

    def one_block(block, carry):
        for begin in range(0, CHANNEL_BLOCK, GROUP):
            channels = [block * CHANNEL_BLOCK + begin + n for n in range(GROUP)]
            results = [picked(i) for i in channels]
            for i, result in zip(channels, results):
                for part in range(2):
                    out[part, pl.ds(i, offsets, stride=pitch), :] = result[part]
        for copy in copies(block):
            copy.start()
        return carry

    blocks = width // CHANNEL_BLOCK
    lax.fori_loop(0, blocks, one_block, 0)

    def finish(block, carry):
        for copy in copies(block):
            copy.wait()
        return carry

    lax.fori_loop(0, blocks, finish, 0)


def stacked(own, buffers, groups, codes_of, reach, offsets, windows):
    bins, lanes, _ = own.shape
    width = lanes // 2
    chunk_windows = buffers[0].shape[-2]
    pitch = width + PITCH_PAD
    return pl.pallas_call(
        functools.partial(stack_kernel, 1.0 / math.sqrt(windows), groups, codes_of),
        out_shape=jax.ShapeDtypeStruct((offsets, width, 2 * F), jnp.float32),
        in_specs=[SMEM] + [VMEM] * (1 + len(buffers)),
        out_specs=ANY,
        scratch_shapes=[
            pltpu.VMEM((2, len(groups), bins, chunk_windows, lanes), jnp.bfloat16),
            pltpu.VMEM((bins * pitch, lanes), jnp.float32),
            pltpu.VMEM((2, offsets * pitch, F), jnp.float32),
            pltpu.SemaphoreType.DMA((width // CHANNEL_BLOCK, 2)),
        ],
        compiler_params=pltpu.CompilerParams(vmem_limit_bytes=28 * MIB),
        cost_estimate=SMALL,
        name="stack",
    )(reach, own, *buffers)


def send(array, pairs):
    return lax.ppermute(array, AXES, pairs)


def pairs_of(n_win, n_chan, target):
    pairs = []
    for z in range(n_win):
        for c in range(n_chan):
            to = target(z, c)
            if to is not None:
                pairs.append((c * n_win + z, to * n_win + z))
    return pairs


def after(array, *others):
    return lax.optimization_barrier((array, *others))[0]


def direct_partners(pieces, hops, n_win, n_chan):
    buffers = []
    for piece in pieces:
        buffers.append(send(piece, pairs_of(n_win, n_chan, lambda z, c: (c - hops[z]) % n_chan)))
        buffers.append(
            send(piece, pairs_of(n_win, n_chan, lambda z, c: (c - hops[z] - 1) % n_chan))
        )
    groups = [[(2 * n, None), (2 * n + 1, None)] for n in range(len(pieces))]
    return own_rows(pieces), buffers, groups, lambda: (0, 1, 0, 1)


def square_codes():
    z, c = lax.axis_index("win"), lax.axis_index("chan")
    core, x = c & 1, (c >> 1) & 1
    onward = jnp.where((z == 0) | (x == 0) | ((z < 3) & (core == 1)), 1, 0)
    odd_next = jnp.where(x == 0, 1, 2)
    even_next = jnp.where(z == 0, odd_next, 2)
    next_code = jnp.where(core == 0, even_next, jnp.where(z == 3, 2, odd_next))
    outgoing = jnp.where(core == 0, jnp.where(z < 2, next_code, 1), jnp.where(z < 2, 0, next_code))
    first = jnp.where(z == 0, 0, jnp.where(z == 2, next_code, 3))
    second = jnp.where(z == 1, next_code, jnp.where(z == 3, 1, 3))
    is_late = (z == 3) & (core == 0)
    outgoing_late = jnp.where(is_late, 3, outgoing)
    second_last = jnp.where(is_late, 4, second)
    return onward, outgoing, outgoing_late, (first, second, first, second_last)


def square_partners(pieces, n_win, n_chan):
    def pairs(target):
        return pairs_of(n_win, n_chan, lambda z, c: target(z, c, c % 2, c // 2 % 2))

    def first_target(z, c, core, x):
        if z == 3:
            return c ^ 4
        if z == 0:
            return c ^ 2 if core == 0 else None
        if core == 1:
            return c ^ 2
        return c ^ 4 if z == 2 or x == 0 else None

    def second_target(z, c, core, x):
        if z == 3:
            return c ^ 2 if core == 1 else None
        if z == 0:
            return c ^ 4 if core == 0 and x == 1 else None
        if core == 0:
            return c ^ 2
        return c ^ 4 if x == 1 else None

    def swap(code_of, groups):
        return send(choose(code_of, groups), pairs(lambda z, c, core, x: c ^ 1))

    count = len(pieces)
    half = count // 2
    firsts, seconds = [], []

    def second_move(slot, arrived):
        relay = choose(lambda: square_codes()[0], [(pieces[slot], arrived)])[0]
        seconds.append(send(relay, pairs(second_target)))
        return relay

    for slot, piece in enumerate(pieces):
        last = slot == count - 1
        if slot >= 2:
            piece = after(piece, firsts[slot - 2])
        firsts.append(
            send(
                piece,
                pairs(
                    lambda z, c, core, x: (
                        None if last and z == 3 and core == 0 else first_target(z, c, core, x)
                    )
                ),
            )
        )
        if slot:
            arrived = firsts[slot - 1]
            arrived = after(arrived, *seconds[-1:])
            second_move(slot - 1, arrived)
    held = list(zip(pieces, firsts, seconds))
    own = own_rows(pieces)
    held[0] = (*held[0][:2], after(held[0][2], firsts[-1]))
    swapped_early = swap(lambda: square_codes()[1], held[:half])
    arrived = after(firsts[-1], own)
    relay = second_move(count - 1, arrived)
    held.append((pieces[-1], firsts[-1], seconds[-1]))
    late = send(
        after(pieces[-1], relay),
        pairs(lambda z, c, core, x: c ^ 4 if z == 3 and core == 0 else None),
    )
    late_groups = [(*group, group[1]) for group in held[half:-1]] + [(*held[-1], late)]
    swapped_late = swap(lambda: square_codes()[2], late_groups)
    buffers = [buffer for group in held for buffer in group] + [swapped_early, swapped_late, late]
    groups = []
    for n in range(count):
        swapped = (3 * count, n) if n < half else (3 * count + 1, n - half)
        groups.append([(3 * n, None), (3 * n + 1, None), (3 * n + 2, None), swapped])
    groups[-1].append((3 * count + 2, None))
    return own, buffers, groups, lambda: square_codes()[3]


def on_device(traces, valid, reach):
    width = traces.shape[1]
    n_win, n_chan = lax.axis_size("win"), lax.axis_size("chan")
    offsets = BAND // n_win
    hops = [z * offsets // width for z in range(n_win)]
    pieces = [whitened_chunk(traces, valid)]
    while len(pieces) < n_win:
        ring = [(z, (z + 1) % n_win) for z in range(n_win)]
        pieces.append(lax.ppermute(pieces[-1], "win", ring))
    if n_chan == 8 and hops == list(range(4)):
        own, buffers, groups, codes_of = square_partners(pieces, n_win, n_chan)
    else:
        own, buffers, groups, codes_of = direct_partners(pieces, hops, n_win, n_chan)
    return stacked(own, buffers, groups, codes_of, reach, offsets, traces.shape[0] * n_win)


def solution(mesh):
    in_specs = (P("win", "chan", None), P("win", "chan"), P("chan"))
    out_specs = P("win", "chan", None)
    return jax.shard_map(
        on_device, mesh=mesh, in_specs=in_specs, out_specs=out_specs, check_vma=False
    )
```

```python
import functools
import math

import jax
import jax.numpy as jnp
import numpy as np
from jax import lax
from jax.experimental import pallas as pl
from jax.experimental.pallas import tpu as pltpu
from jax.sharding import PartitionSpec as P

F = 128
FIRST = 16
BAND = 256
AXES = ("chan", "win")
CHANNEL_BLOCK = 8
GROUP = 4
PITCH_PAD = 8
MIB = 1024 * 1024
VMEM = pl.BlockSpec(memory_space=pltpu.VMEM)
FEW_MIB = pltpu.CompilerParams(vmem_limit_bytes=4 * MIB)
SMEM = pl.BlockSpec(memory_space=pltpu.SMEM)
SMALL = pl.CostEstimate(flops=1, bytes_accessed=1, transcendentals=0)
ANY = pl.BlockSpec(memory_space=pl.ANY)


def make_table(samples):
    t_int = np.arange(samples, dtype=np.int64)
    j_int = np.arange(F, dtype=np.int64) + FIRST
    angle = 2.0 * np.pi / samples * (j_int[:, None] * t_int[None, :] % samples)
    hann = 0.5 - 0.5 * np.cos(2.0 * np.pi / samples * t_int)
    rows = np.concatenate([hann * np.cos(angle), -hann * np.sin(angle)], axis=0)
    return jnp.asarray(rows.astype(np.float32)).astype(jnp.bfloat16)


def whiten_kernel(table, traces, valid, out_ref, rows):
    windows, width, samples = traces.shape
    for w in range(0, windows, 2):
        spectra = lax.dot_general(
            table[...],
            traces[w : w + 2].reshape(2 * width, samples),
            (((1,), (1,)), ((), ())),
            preferred_element_type=jnp.float32,
        )
        re, im = spectra[:F], spectra[F:]
        power = re * re + im * im
        level = jnp.sqrt(jnp.mean(power, axis=0, keepdims=True) + 1e-06)
        usable = jnp.concatenate([valid[w : w + 1, :], valid[w + 1 : w + 2, :]], axis=1)
        factor = usable.astype(jnp.float32) / (jnp.sqrt(power) + 0.1 * level)
        re, im = re * factor, im * factor
        for k in range(2):
            half = slice(k * width, (k + 1) * width)
            rows[pl.ds(w + k, F, stride=windows), :] = jnp.concatenate(
                [re[:, half], im[:, half]], axis=1
            )
    out_ref[...] = rows[...].reshape(out_ref.shape).astype(jnp.bfloat16)


def whitened_chunk(traces, valid):
    windows, width, samples = traces.shape
    return pl.pallas_call(
        whiten_kernel,
        out_shape=jax.ShapeDtypeStruct((F, windows, 2 * width), jnp.bfloat16),
        in_specs=[VMEM] * 3,
        out_specs=VMEM,
        scratch_shapes=[pltpu.VMEM((F * windows, 2 * width), jnp.float32)],
        compiler_params=FEW_MIB,
        cost_estimate=SMALL,
        name="whiten",
    )(make_table(samples), traces, valid)


def copy_chosen(code, refs, put):
    for index, ref in enumerate(refs):

        @pl.when(code == index)
        def _(ref=ref):
            put(ref)


def choose_kernel(code_of, groups, *refs):
    out_ref = refs[-1]
    per_group = (len(refs) - 1) // groups
    code = code_of()
    for g in range(groups):

        def put(ref, g=g):
            out_ref[g] = ref[...]

        copy_chosen(code, refs[g * per_group : (g + 1) * per_group], put)


def choose(code_of, groups):
    operands = [buffer for group in groups for buffer in group]
    return pl.pallas_call(
        functools.partial(choose_kernel, code_of, len(groups)),
        out_shape=jax.ShapeDtypeStruct((len(groups), *groups[0][0].shape), jnp.bfloat16),
        in_specs=[VMEM] * len(operands),
        out_specs=VMEM,
        compiler_params=FEW_MIB,
        cost_estimate=SMALL,
        name="choose",
    )(*operands)


def own_kernel(*refs):
    out_ref = refs[-1]

    def one_bin(f, carry):
        out_ref[f] = jnp.concatenate([ref[f] for ref in refs[:-1]], axis=0).T
        return carry

    lax.fori_loop(0, out_ref.shape[0], one_bin, 0, unroll=8)


def own_rows(pieces):
    bins, windows, lanes = pieces[0].shape
    return pl.pallas_call(
        own_kernel,
        out_shape=jax.ShapeDtypeStruct(
            (bins, lanes, windows * len(pieces)), jnp.bfloat16
        ),
        in_specs=[VMEM] * len(pieces),
        out_specs=VMEM,
        compiler_params=FEW_MIB,
        cost_estimate=SMALL,
        name="own_rows",
    )(*pieces)


def stack_kernel(scale, groups, codes_of, reach_ref, own, *refs):
    buffers, (out_hbm, partners, products, out, sems) = refs[:-5], refs[-5:]
    bins, lanes, _ = own.shape
    width = lanes // 2
    offsets = out_hbm.shape[0]
    pitch = products.shape[0] // bins
    slots = len(groups)
    first_offset = lax.axis_index("win") * offsets
    codes = codes_of()
    for slot, group in enumerate(groups):
        for which in range(2):
            candidates = [
                buffers[number] if index is None else buffers[number].at[index]
                for number, index in group
            ]

            def put(ref, slot=slot, which=which):
                partners[which, slot] = ref[...]

            copy_chosen(codes[which if slot < slots - 1 else 2 + which], candidates, put)

    first = first_offset % width
    lane = lax.broadcasted_iota(jnp.int32, (width, lanes), 1)
    in_first = lane % width >= lax.broadcasted_iota(jnp.int32, (width, lanes), 0) + first

    sign = jnp.where(lane < width, 1.0, -1.0)

    def products_of(f):
        right = jnp.concatenate(
            [
                jnp.concatenate([partners[which, slot, f] for slot in range(slots)], axis=0)
                for which in range(2)
            ],
            axis=1,
        )
        both = jnp.dot(own[f], right, preferred_element_type=jnp.float32)
        with_re = jnp.where(in_first, both[:width, :lanes], both[:width, lanes:])
        with_im = jnp.where(in_first, both[width:, :lanes], both[width:, lanes:])
        return with_re + sign * pltpu.roll(with_im, width, 1)

    def one_group(group, carry):
        results = [products_of(group * GROUP + n) for n in range(GROUP)]
        for n, result in enumerate(results):
            row = pl.multiple_of((group * GROUP + n) * pitch, 8)
            products[pl.ds(row, width), :] = result
        return carry

    lax.fori_loop(0, bins // GROUP, one_group, 0, unroll=2)

    lane = lax.broadcasted_iota(jnp.int32, (offsets, lanes), 1)
    shift = (lane + offsets * width - lax.broadcasted_iota(jnp.int32, (offsets, lanes), 0)) % width
    shift_re = jnp.where(lane < width, shift, width)
    shift_im = jnp.where(lane < width, width, shift)
    row_k = lax.broadcasted_iota(jnp.int32, (offsets, F), 0) + first_offset

    def copies(block):
        columns = pl.ds(pl.multiple_of(block * CHANNEL_BLOCK, CHANNEL_BLOCK), CHANNEL_BLOCK)
        return [
            pltpu.make_async_copy(
                out.at[part].reshape(offsets, pitch, F).at[:, columns, :],
                out_hbm.at[:, columns, pl.ds(part * F, F)],
                sems.at[block, part],
            )
            for part in range(2)
        ]

    def picked(i):
        at = (i + first) % width
        pick = jnp.concatenate(
            [jnp.where(shift_re == at, 1.0, 0.0), jnp.where(shift_im == at, -1.0, 0.0)], axis=0
        ).astype(jnp.bfloat16)
        x = products[pl.ds(i, F, stride=pitch), :].astype(jnp.bfloat16)
        y = lax.dot_general(
            pick, x, (((1,), (1,)), ((), ())), preferred_element_type=jnp.float32
        )
        inside = jnp.where(row_k < reach_ref[i], scale, 0.0)
        return [y[part * offsets : (part + 1) * offsets] * inside for part in range(2)]

    def one_block(block, carry):
        for begin in range(0, CHANNEL_BLOCK, GROUP):
            channels = [block * CHANNEL_BLOCK + begin + n for n in range(GROUP)]
            results = [picked(i) for i in channels]
            for i, result in zip(channels, results):
                for part in range(2):
                    out[part, pl.ds(i, offsets, stride=pitch), :] = result[part]
        for copy in copies(block):
            copy.start()
        return carry

    blocks = width // CHANNEL_BLOCK
    lax.fori_loop(0, blocks, one_block, 0)

    def finish(block, carry):
        for copy in copies(block):
            copy.wait()
        return carry

    lax.fori_loop(0, blocks, finish, 0)


def stacked(own, buffers, groups, codes_of, reach, offsets, windows):
    bins, lanes, _ = own.shape
    width = lanes // 2
    chunk_windows = buffers[0].shape[-2]
    pitch = width + PITCH_PAD
    return pl.pallas_call(
        functools.partial(stack_kernel, 1.0 / math.sqrt(windows), groups, codes_of),
        out_shape=jax.ShapeDtypeStruct((offsets, width, 2 * F), jnp.float32),
        in_specs=[SMEM] + [VMEM] * (1 + len(buffers)),
        out_specs=ANY,
        scratch_shapes=[
            pltpu.VMEM((2, len(groups), bins, chunk_windows, lanes), jnp.bfloat16),
            pltpu.VMEM((bins * pitch, lanes), jnp.float32),
            pltpu.VMEM((2, offsets * pitch, F), jnp.float32),
            pltpu.SemaphoreType.DMA((width // CHANNEL_BLOCK, 2)),
        ],
        compiler_params=pltpu.CompilerParams(vmem_limit_bytes=28 * MIB),
        cost_estimate=SMALL,
        name="stack",
    )(reach, own, *buffers)


def send(array, pairs):
    return lax.ppermute(array, AXES, pairs)


def pairs_of(n_win, n_chan, target):
    pairs = []
    for z in range(n_win):
        for c in range(n_chan):
            to = target(z, c)
            if to is not None:
                pairs.append((c * n_win + z, to * n_win + z))
    return pairs


def after(array, *others):
    return lax.optimization_barrier((array, *others))[0]


def direct_partners(pieces, hops, n_win, n_chan):
    buffers = []
    for piece in pieces:
        buffers.append(send(piece, pairs_of(n_win, n_chan, lambda z, c: (c - hops[z]) % n_chan)))
        buffers.append(
            send(piece, pairs_of(n_win, n_chan, lambda z, c: (c - hops[z] - 1) % n_chan))
        )
    groups = [[(2 * n, None), (2 * n + 1, None)] for n in range(len(pieces))]
    return own_rows(pieces), buffers, groups, lambda: (0, 1, 0, 1)


def square_codes():
    z, c = lax.axis_index("win"), lax.axis_index("chan")
    core, x = c & 1, (c >> 1) & 1
    onward = jnp.where((z == 0) | (x == 0) | ((z < 3) & (core == 1)), 1, 0)
    odd_next = jnp.where(x == 0, 1, 2)
    even_next = jnp.where(z == 0, odd_next, 2)
    next_code = jnp.where(core == 0, even_next, jnp.where(z == 3, 2, odd_next))
    outgoing = jnp.where(core == 0, jnp.where(z < 2, next_code, 1), jnp.where(z < 2, 0, next_code))
    first = jnp.where(z == 0, 0, jnp.where(z == 2, next_code, 3))
    second = jnp.where(z == 1, next_code, jnp.where(z == 3, 1, 3))
    is_late = (z == 3) & (core == 0)
    outgoing_late = jnp.where(is_late, 3, outgoing)
    second_last = jnp.where(is_late, 4, second)
    return onward, outgoing, outgoing_late, (first, second, first, second_last)


def square_partners(pieces, n_win, n_chan):
    def pairs(target):
        return pairs_of(n_win, n_chan, lambda z, c: target(z, c, c % 2, c // 2 % 2))

    def first_target(z, c, core, x):
        if z == 3:
            return c ^ 4
        if z == 0:
            return c ^ 2 if core == 0 else None
        if core == 1:
            return c ^ 2
        return c ^ 4 if z == 2 or x == 0 else None

    def second_target(z, c, core, x):
        if z == 3:
            return c ^ 2 if core == 1 else None
        if z == 0:
            return c ^ 4 if core == 0 and x == 1 else None
        if core == 0:
            return c ^ 2
        return c ^ 4 if x == 1 else None

    def swap(code_of, groups):
        return send(choose(code_of, groups), pairs(lambda z, c, core, x: c ^ 1))

    count = len(pieces)
    half = count // 2
    firsts, seconds = [], []

    def second_move(slot, arrived):
        relay = choose(lambda: square_codes()[0], [(pieces[slot], arrived)])[0]
        seconds.append(send(relay, pairs(second_target)))
        return relay

    for slot, piece in enumerate(pieces):
        last = slot == count - 1
        if slot >= 2:
            piece = after(piece, firsts[slot - 2])
        firsts.append(
            send(
                piece,
                pairs(
                    lambda z, c, core, x: (
                        None if last and z == 3 and core == 0 else first_target(z, c, core, x)
                    )
                ),
            )
        )
        if slot:
            arrived = firsts[slot - 1]
            arrived = after(arrived, *seconds[-1:])
            second_move(slot - 1, arrived)
    held = list(zip(pieces, firsts, seconds))
    own = own_rows(pieces)
    held[0] = (*held[0][:2], after(held[0][2], firsts[-1], own))
    swapped_early = swap(lambda: square_codes()[1], held[:half])
    relay = second_move(count - 1, firsts[-1])
    held.append((pieces[-1], firsts[-1], seconds[-1]))
    late = send(
        after(pieces[-1], relay),
        pairs(lambda z, c, core, x: c ^ 4 if z == 3 and core == 0 else None),
    )
    late_groups = [(*group, group[1]) for group in held[half:-1]] + [(*held[-1], late)]
    swapped_late = swap(lambda: square_codes()[2], late_groups)
    buffers = [buffer for group in held for buffer in group] + [swapped_early, swapped_late, late]
    groups = []
    for n in range(count):
        swapped = (3 * count, n) if n < half else (3 * count + 1, n - half)
        groups.append([(3 * n, None), (3 * n + 1, None), (3 * n + 2, None), swapped])
    groups[-1].append((3 * count + 2, None))
    return own, buffers, groups, lambda: square_codes()[3]


def on_device(traces, valid, reach):
    width = traces.shape[1]
    n_win, n_chan = lax.axis_size("win"), lax.axis_size("chan")
    offsets = BAND // n_win
    hops = [z * offsets // width for z in range(n_win)]
    pieces = [whitened_chunk(traces, valid)]
    while len(pieces) < n_win:
        ring = [(z, (z + 1) % n_win) for z in range(n_win)]
        pieces.append(lax.ppermute(pieces[-1], "win", ring))
    if n_chan == 8 and hops == list(range(4)):
        own, buffers, groups, codes_of = square_partners(pieces, n_win, n_chan)
    else:
        own, buffers, groups, codes_of = direct_partners(pieces, hops, n_win, n_chan)
    return stacked(own, buffers, groups, codes_of, reach, offsets, traces.shape[0] * n_win)


def solution(mesh):
    in_specs = (P("win", "chan", None), P("win", "chan"), P("chan"))
    out_specs = P("win", "chan", None)
    return jax.shard_map(
        on_device, mesh=mesh, in_specs=in_specs, out_specs=out_specs, check_vma=False
    )
```

```python
import functools
import math

import jax
import jax.numpy as jnp
import numpy as np
from jax import lax
from jax.experimental import pallas as pl
from jax.experimental.pallas import tpu as pltpu
from jax.sharding import PartitionSpec as P

F = 128
FIRST = 16
BAND = 256
AXES = ("chan", "win")
CHANNEL_BLOCK = 8
GROUP = 8
PITCH_PAD = 8
MIB = 1024 * 1024
VMEM = pl.BlockSpec(memory_space=pltpu.VMEM)
FEW_MIB = pltpu.CompilerParams(vmem_limit_bytes=4 * MIB)
SMEM = pl.BlockSpec(memory_space=pltpu.SMEM)
SMALL = pl.CostEstimate(flops=1, bytes_accessed=1, transcendentals=0)
ANY = pl.BlockSpec(memory_space=pl.ANY)


def make_table(samples):
    t_int = np.arange(samples, dtype=np.int64)
    j_int = np.arange(F, dtype=np.int64) + FIRST
    angle = 2.0 * np.pi / samples * (j_int[:, None] * t_int[None, :] % samples)
    hann = 0.5 - 0.5 * np.cos(2.0 * np.pi / samples * t_int)
    rows = np.concatenate([hann * np.cos(angle), -hann * np.sin(angle)], axis=0)
    return jnp.asarray(rows.astype(np.float32)).astype(jnp.bfloat16)


def whiten_kernel(table, traces, valid, out_ref, rows):
    windows, width, samples = traces.shape
    for w in range(0, windows, 2):
        spectra = lax.dot_general(
            table[...],
            traces[w : w + 2].reshape(2 * width, samples),
            (((1,), (1,)), ((), ())),
            preferred_element_type=jnp.float32,
        )
        re, im = spectra[:F], spectra[F:]
        power = re * re + im * im
        level = jnp.sqrt(jnp.mean(power, axis=0, keepdims=True) + 1e-06)
        usable = jnp.concatenate([valid[w : w + 1, :], valid[w + 1 : w + 2, :]], axis=1)
        factor = usable.astype(jnp.float32) / (jnp.sqrt(power) + 0.1 * level)
        re, im = re * factor, im * factor
        for k in range(2):
            half = slice(k * width, (k + 1) * width)
            rows[pl.ds(w + k, F, stride=windows), :] = jnp.concatenate(
                [re[:, half], im[:, half]], axis=1
            )
    out_ref[...] = rows[...].reshape(out_ref.shape).astype(jnp.bfloat16)


def whitened_chunk(traces, valid):
    windows, width, samples = traces.shape
    return pl.pallas_call(
        whiten_kernel,
        out_shape=jax.ShapeDtypeStruct((F, windows, 2 * width), jnp.bfloat16),
        in_specs=[VMEM] * 3,
        out_specs=VMEM,
        scratch_shapes=[pltpu.VMEM((F * windows, 2 * width), jnp.float32)],
        compiler_params=FEW_MIB,
        cost_estimate=SMALL,
        name="whiten",
    )(make_table(samples), traces, valid)


def copy_chosen(code, refs, put):
    for index, ref in enumerate(refs):

        @pl.when(code == index)
        def _(ref=ref):
            put(ref)


def choose_kernel(code_of, groups, *refs):
    out_ref = refs[-1]
    per_group = (len(refs) - 1) // groups
    code = code_of()
    for g in range(groups):

        def put(ref, g=g):
            out_ref[g] = ref[...]

        copy_chosen(code, refs[g * per_group : (g + 1) * per_group], put)


def choose(code_of, groups):
    operands = [buffer for group in groups for buffer in group]
    return pl.pallas_call(
        functools.partial(choose_kernel, code_of, len(groups)),
        out_shape=jax.ShapeDtypeStruct((len(groups), *groups[0][0].shape), jnp.bfloat16),
        in_specs=[VMEM] * len(operands),
        out_specs=VMEM,
        compiler_params=FEW_MIB,
        cost_estimate=SMALL,
        name="choose",
    )(*operands)


def own_kernel(*refs):
    out_ref = refs[-1]

    def one_bin(f, carry):
        out_ref[f] = jnp.concatenate([ref[f] for ref in refs[:-1]], axis=0).T
        return carry

    lax.fori_loop(0, out_ref.shape[0], one_bin, 0, unroll=8)


def own_rows(pieces):
    bins, windows, lanes = pieces[0].shape
    return pl.pallas_call(
        own_kernel,
        out_shape=jax.ShapeDtypeStruct(
            (bins, lanes, windows * len(pieces)), jnp.bfloat16
        ),
        in_specs=[VMEM] * len(pieces),
        out_specs=VMEM,
        compiler_params=FEW_MIB,
        cost_estimate=SMALL,
        name="own_rows",
    )(*pieces)


def stack_kernel(scale, groups, codes_of, reach_ref, own, *refs):
    buffers, (out_hbm, partners, products, out, sems) = refs[:-5], refs[-5:]
    bins, lanes, _ = own.shape
    width = lanes // 2
    offsets = out_hbm.shape[0]
    pitch = products.shape[0] // bins
    slots = len(groups)
    first_offset = lax.axis_index("win") * offsets
    codes = codes_of()
    for slot, group in enumerate(groups):
        for which in range(2):
            candidates = [
                buffers[number] if index is None else buffers[number].at[index]
                for number, index in group
            ]

            def put(ref, slot=slot, which=which):
                partners[which, slot] = ref[...]

            copy_chosen(codes[which if slot < slots - 1 else 2 + which], candidates, put)

    first = first_offset % width
    lane = lax.broadcasted_iota(jnp.int32, (width, lanes), 1)
    in_first = lane % width >= lax.broadcasted_iota(jnp.int32, (width, lanes), 0) + first

    sign = jnp.where(lane < width, 1.0, -1.0)

    def products_of(f):
        right = jnp.concatenate(
            [
                jnp.concatenate([partners[which, slot, f] for slot in range(slots)], axis=0)
                for which in range(2)
            ],
            axis=1,
        )
        both = jnp.dot(own[f], right, preferred_element_type=jnp.float32)
        with_re = jnp.where(in_first, both[:width, :lanes], both[:width, lanes:])
        with_im = jnp.where(in_first, both[width:, :lanes], both[width:, lanes:])
        return with_re + sign * pltpu.roll(with_im, width, 1)

    def one_group(group, carry):
        results = [products_of(group * GROUP + n) for n in range(GROUP)]
        for n, result in enumerate(results):
            row = pl.multiple_of((group * GROUP + n) * pitch, 8)
            products[pl.ds(row, width), :] = result
        return carry

    lax.fori_loop(0, bins // GROUP, one_group, 0, unroll=2)

    lane = lax.broadcasted_iota(jnp.int32, (offsets, lanes), 1)
    shift = (lane + offsets * width - lax.broadcasted_iota(jnp.int32, (offsets, lanes), 0)) % width
    shift_re = jnp.where(lane < width, shift, width)
    shift_im = jnp.where(lane < width, width, shift)
    row_k = lax.broadcasted_iota(jnp.int32, (offsets, F), 0) + first_offset

    def copies(block):
        columns = pl.ds(pl.multiple_of(block * CHANNEL_BLOCK, CHANNEL_BLOCK), CHANNEL_BLOCK)
        return [
            pltpu.make_async_copy(
                out.at[part].reshape(offsets, pitch, F).at[:, columns, :],
                out_hbm.at[:, columns, pl.ds(part * F, F)],
                sems.at[block, part],
            )
            for part in range(2)
        ]

    def picked(i):
        at = (i + first) % width
        pick = jnp.concatenate(
            [jnp.where(shift_re == at, 1.0, 0.0), jnp.where(shift_im == at, -1.0, 0.0)], axis=0
        ).astype(jnp.bfloat16)
        x = products[pl.ds(i, F, stride=pitch), :].astype(jnp.bfloat16)
        y = lax.dot_general(
            pick, x, (((1,), (1,)), ((), ())), preferred_element_type=jnp.float32
        )
        inside = jnp.where(row_k < reach_ref[i], scale, 0.0)
        return [y[part * offsets : (part + 1) * offsets] * inside for part in range(2)]

    def one_block(block, carry):
        for begin in range(0, CHANNEL_BLOCK, GROUP):
            channels = [block * CHANNEL_BLOCK + begin + n for n in range(GROUP)]
            results = [picked(i) for i in channels]
            for i, result in zip(channels, results):
                for part in range(2):
                    out[part, pl.ds(i, offsets, stride=pitch), :] = result[part]
        for copy in copies(block):
            copy.start()
        return carry

    blocks = width // CHANNEL_BLOCK
    lax.fori_loop(0, blocks, one_block, 0)

    def finish(block, carry):
        for copy in copies(block):
            copy.wait()
        return carry

    lax.fori_loop(0, blocks, finish, 0)


def stacked(own, buffers, groups, codes_of, reach, offsets, windows):
    bins, lanes, _ = own.shape
    width = lanes // 2
    chunk_windows = buffers[0].shape[-2]
    pitch = width + PITCH_PAD
    return pl.pallas_call(
        functools.partial(stack_kernel, 1.0 / math.sqrt(windows), groups, codes_of),
        out_shape=jax.ShapeDtypeStruct((offsets, width, 2 * F), jnp.float32),
        in_specs=[SMEM] + [VMEM] * (1 + len(buffers)),
        out_specs=ANY,
        scratch_shapes=[
            pltpu.VMEM((2, len(groups), bins, chunk_windows, lanes), jnp.bfloat16),
            pltpu.VMEM((bins * pitch, lanes), jnp.float32),
            pltpu.VMEM((2, offsets * pitch, F), jnp.float32),
            pltpu.SemaphoreType.DMA((width // CHANNEL_BLOCK, 2)),
        ],
        compiler_params=pltpu.CompilerParams(vmem_limit_bytes=28 * MIB),
        cost_estimate=SMALL,
        name="stack",
    )(reach, own, *buffers)


def send(array, pairs):
    return lax.ppermute(array, AXES, pairs)


def pairs_of(n_win, n_chan, target):
    pairs = []
    for z in range(n_win):
        for c in range(n_chan):
            to = target(z, c)
            if to is not None:
                pairs.append((c * n_win + z, to * n_win + z))
    return pairs


def after(array, *others):
    return lax.optimization_barrier((array, *others))[0]


def direct_partners(pieces, hops, n_win, n_chan):
    buffers = []
    for piece in pieces:
        buffers.append(send(piece, pairs_of(n_win, n_chan, lambda z, c: (c - hops[z]) % n_chan)))
        buffers.append(
            send(piece, pairs_of(n_win, n_chan, lambda z, c: (c - hops[z] - 1) % n_chan))
        )
    groups = [[(2 * n, None), (2 * n + 1, None)] for n in range(len(pieces))]
    return own_rows(pieces), buffers, groups, lambda: (0, 1, 0, 1)


def square_codes():
    z, c = lax.axis_index("win"), lax.axis_index("chan")
    core, x = c & 1, (c >> 1) & 1
    onward = jnp.where((z == 0) | (x == 0) | ((z < 3) & (core == 1)), 1, 0)
    odd_next = jnp.where(x == 0, 1, 2)
    even_next = jnp.where(z == 0, odd_next, 2)
    next_code = jnp.where(core == 0, even_next, jnp.where(z == 3, 2, odd_next))
    outgoing = jnp.where(core == 0, jnp.where(z < 2, next_code, 1), jnp.where(z < 2, 0, next_code))
    first = jnp.where(z == 0, 0, jnp.where(z == 2, next_code, 3))
    second = jnp.where(z == 1, next_code, jnp.where(z == 3, 1, 3))
    is_late = (z == 3) & (core == 0)
    outgoing_late = jnp.where(is_late, 3, outgoing)
    second_last = jnp.where(is_late, 4, second)
    return onward, outgoing, outgoing_late, (first, second, first, second_last)


def square_partners(pieces, n_win, n_chan):
    def pairs(target):
        return pairs_of(n_win, n_chan, lambda z, c: target(z, c, c % 2, c // 2 % 2))

    def first_target(z, c, core, x):
        if z == 3:
            return c ^ 4
        if z == 0:
            return c ^ 2 if core == 0 else None
        if core == 1:
            return c ^ 2
        return c ^ 4 if z == 2 or x == 0 else None

    def second_target(z, c, core, x):
        if z == 3:
            return c ^ 2 if core == 1 else None
        if z == 0:
            return c ^ 4 if core == 0 and x == 1 else None
        if core == 0:
            return c ^ 2
        return c ^ 4 if x == 1 else None

    def swap(code_of, groups):
        return send(choose(code_of, groups), pairs(lambda z, c, core, x: c ^ 1))

    count = len(pieces)
    half = count // 2
    firsts, seconds = [], []

    def second_move(slot, arrived):
        relay = choose(lambda: square_codes()[0], [(pieces[slot], arrived)])[0]
        seconds.append(send(relay, pairs(second_target)))
        return relay

    for slot, piece in enumerate(pieces):
        last = slot == count - 1
        if slot >= 2:
            piece = after(piece, firsts[slot - 2])
        firsts.append(
            send(
                piece,
                pairs(
                    lambda z, c, core, x: (
                        None if last and z == 3 and core == 0 else first_target(z, c, core, x)
                    )
                ),
            )
        )
        if slot:
            arrived = firsts[slot - 1]
            arrived = after(arrived, *seconds[-1:])
            second_move(slot - 1, arrived)
    held = list(zip(pieces, firsts, seconds))
    own = own_rows(pieces)
    held[0] = (*held[0][:2], after(held[0][2], firsts[-1], own))
    swapped_early = swap(lambda: square_codes()[1], held[:half])
    relay = second_move(count - 1, firsts[-1])
    held.append((pieces[-1], firsts[-1], seconds[-1]))
    late = send(
        after(pieces[-1], relay),
        pairs(lambda z, c, core, x: c ^ 4 if z == 3 and core == 0 else None),
    )
    late_groups = [(*group, group[1]) for group in held[half:-1]] + [(*held[-1], late)]
    swapped_late = swap(lambda: square_codes()[2], late_groups)
    buffers = [buffer for group in held for buffer in group] + [swapped_early, swapped_late, late]
    groups = []
    for n in range(count):
        swapped = (3 * count, n) if n < half else (3 * count + 1, n - half)
        groups.append([(3 * n, None), (3 * n + 1, None), (3 * n + 2, None), swapped])
    groups[-1].append((3 * count + 2, None))
    return own, buffers, groups, lambda: square_codes()[3]


def on_device(traces, valid, reach):
    width = traces.shape[1]
    n_win, n_chan = lax.axis_size("win"), lax.axis_size("chan")
    offsets = BAND // n_win
    hops = [z * offsets // width for z in range(n_win)]
    pieces = [whitened_chunk(traces, valid)]
    while len(pieces) < n_win:
        ring = [(z, (z + 1) % n_win) for z in range(n_win)]
        pieces.append(lax.ppermute(pieces[-1], "win", ring))
    if n_chan == 8 and hops == list(range(4)):
        own, buffers, groups, codes_of = square_partners(pieces, n_win, n_chan)
    else:
        own, buffers, groups, codes_of = direct_partners(pieces, hops, n_win, n_chan)
    return stacked(own, buffers, groups, codes_of, reach, offsets, traces.shape[0] * n_win)


def solution(mesh):
    in_specs = (P("win", "chan", None), P("win", "chan"), P("chan"))
    out_specs = P("win", "chan", None)
    return jax.shard_map(
        on_device, mesh=mesh, in_specs=in_specs, out_specs=out_specs, check_vma=False
    )
```
